32 devices in a mesh: ctx: 4 (over y, x), fsdp: 8 (over z, core).
Axes of the slice: x: 2, y: 2, z: 4, core: 2. Of those that a mesh axis runs over, the one named last changes fastest.
Arguments:
- hidden_in: bfloat16 [8, 1024, 1536], P('fsdp', 'ctx'), may hold values from -6 to 6
- span_order: int32 [8], replicated, may hold values from 0 to 7, as said below
- routes: int32 [8, 1024, 8], P('fsdp', 'ctx'), may hold values from 0 to 15, all different within a row; in each aligned block of 256 rows (0 to 255, 256 to 511, ..., all dimensions but the last counted through in order) at most 160 rows name the same one
- attn_gain: bfloat16 [1536], P('fsdp'), may hold values from 0.5 to 1.5
- query_weight: bfloat16 [1536, 1536], P('fsdp'), may hold values from -150 to 150
- key_weight: bfloat16 [1536, 512], P('fsdp'), may hold values from -1 to 1
- value_weight: bfloat16 [1536, 512], P('fsdp'), may hold values from -0.15625 to 0.15625
- out_weight: bfloat16 [1536, 1536], P('fsdp'), may hold values from -6 to 6
- ffn_gain: bfloat16 [1536], P('fsdp'), may hold values from 0.5 to 1.5
- router_weight: bfloat16 [1536, 16], P('fsdp'), may hold values from -4 to 4
- gate_weight: bfloat16 [16, 1536, 512], P('fsdp'), may hold values from -0.15625 to 0.15625
- up_weight: bfloat16 [16, 1536, 512], P('fsdp'), may hold values from -0.15625 to 0.15625
- down_weight: bfloat16 [16, 1536, 512], P('fsdp'), may hold values from -3 to 3
- cotangent: bfloat16 [8, 1024, 1536], P('fsdp', 'ctx'), may hold values from -6 to 6
Outputs:
- hidden_out: bfloat16 [8, 1024, 1536], P('fsdp', 'ctx')
- grad_in: float32 [8, 1024, 1536], P('fsdp', 'ctx')
- grad_attn_gain: float32 [1536], P(('ctx', 'fsdp'))
- grad_query: float32 [1536, 1536], P(('ctx', 'fsdp'))
- grad_key: float32 [1536, 512], P(('ctx', 'fsdp'))
- grad_value: float32 [1536, 512], P(('ctx', 'fsdp'))
- grad_out: float32 [1536, 1536], P(('ctx', 'fsdp'))
- grad_ffn_gain: float32 [1536], P(('ctx', 'fsdp'))
- grad_router: float32 [1536, 16], P(('ctx', 'fsdp'))
- grad_gate: float32 [16, 1536, 512], P('fsdp', 'ctx')
- grad_up: float32 [16, 1536, 512], P('fsdp', 'ctx')
- grad_down: float32 [16, 1536, 512], P('fsdp', 'ctx')
The draws below stay inside these ranges and needn't reach their ends.
Inputs may be any that keep to these rules, and one draw needn't show every extreme that they name: `span_order`: stored spans 2c and 2c + 1 hold spans p and 7 - p, in that order, for some p below 4; every span appears once. `routes`: the 8 experts of a token differ. Among the rows of one device no expert is named more than 160 times, and in every draw some expert is named exactly 160 times on some device.
All inputs are finite; a program needn't handle non-finite values.
Results may differ from the reference program's by a relative error of at most 0.018.
Values may be sent and summed in bfloat16 or wider, within the bound.
No kernel may reach another device: no remote copies, remote signals or barrier semaphores. Data moves between devices by JAX's collectives and lax.ppermute only.
A program may use at most 320 MiB of HBM per device.

```python
import math
import jax
import jax.numpy as jnp
import numpy as np
from jax import lax

D = 1536
HEADS = 24
KV_HEADS = 8
HEAD = 64
FF = 512
TOPK = 8
TOK_DEV = 256
EXPERTS = 16
CAP = 160
SPANS = 8
LENGTH = 1024
SEQS = 8
QW = 1536
KVW = 512


def key_matrix(key):
    return jnp.clip(jax.random.normal(jax.random.fold_in(key, 11), (D, KV_HEADS * HEAD), jnp.float32), -6.0, 6.0) * D ** (-0.5)


def draw_key_weight(key, part):
    return key_matrix(key).astype(jnp.bfloat16)


def draw_query_weight(key, part):
    query_matrix = jnp.clip(jax.random.normal(jax.random.fold_in(key, 12), (D, HEADS * HEAD), jnp.float32), -6.0, 6.0) * D ** (-0.5)
    return query_matrix.astype(jnp.bfloat16)


def draw_router_weight(key, part):
    router_matrix = jnp.clip(jax.random.normal(jax.random.fold_in(key, 13), (D, EXPERTS), jnp.float32), -6.0, 6.0) * (0.3 * D ** (-0.5))
    return router_matrix.astype(jnp.bfloat16)


def draw_span_order(key, part):
    pair_count = SPANS // 2
    first_span = jax.random.permutation(jax.random.fold_in(key, 21), pair_count).astype(jnp.int32)
    return jnp.stack([first_span, SPANS - 1 - first_span], axis=1).reshape(SPANS).astype(jnp.int32)


def level_of(stream_key, extent, pieces, low, top_value):
    loudness = 1.0
    for position, blocks in pieces:
        steps = jax.random.uniform(jax.random.fold_in(jax.random.fold_in(stream_key, 6), position), (blocks,), jnp.float32, low / len(pieces), top_value / len(pieces))
        loudness = loudness * jnp.repeat(jnp.exp(steps), extent[position] // blocks).reshape((-1,) + (1,) * (len(extent) - 1 - position))
    return loudness


def shared_out(key, own, number, rows, amount, top, limit, slope):
    sequence = jax.random.permutation(key, amount)
    packed, usual = portions_of(amount, rows * top, limit, slope, True), portions_of(amount, rows * top, limit, slope, False)
    places = jnp.arange(amount)

    def named(tallies, turn):
        used = int((tallies > 0).sum())
        fixed = max(1, used // 4)
        moved = fixed + (places - fixed + turn * (used - fixed)) % max(1, amount - fixed)
        return jnp.zeros((amount,), jnp.int32).at[sequence[jnp.where(places < fixed, places, moved)]].set(jnp.asarray(tallies, jnp.int32))

    tallies = jnp.where(number % 4 == 0, named(packed, number // 4), named(usual, number - number // 4 - 1))
    mixed = jax.random.permutation(jax.random.fold_in(own, 3), amount)
    source_of, taker = mixed[0:amount // 2 * 2:2], mixed[1:amount // 2 * 2:2]
    room = jnp.minimum(tallies[source_of] - 1, limit - tallies[taker]) // 2
    room = jnp.where((source_of == sequence[0]) | (taker == sequence[0]) | (tallies[taker] == 0), 0, jnp.maximum(room, 0))
    moved = jax.random.randint(jax.random.fold_in(own, 4), (amount // 2,), 0, 1 << 20) % (room + 1)
    tallies = tallies.at[source_of].add(-moved).at[taker].add(moved)
    labels = jnp.searchsorted(jnp.cumsum(tallies), jnp.arange(rows * top), side="right").astype(jnp.int32)
    listing = labels.reshape(top, rows).T
    listing = listing[jax.random.permutation(jax.random.fold_in(own, 1), rows)]
    turn = jax.random.randint(jax.random.fold_in(own, 2), (rows, 1), 0, top)
    return jnp.take_along_axis(listing, (jnp.arange(top)[None, :] + turn) % top, axis=1)


def portions_of(amount, total, limit, skew, full):
    loads = [(1 << 20) // math.isqrt(grade ** skew) + 1 for grade in range(1, amount + 1)]
    largest = limit if full else min(limit, max(-(-total // amount), total * loads[0] // sum(loads)))
    least = 1 if total - largest >= amount - 1 else 0
    holding, rest = [largest] + [least] * (amount - 1), total - largest - least * (amount - 1)
    while rest > 0:
        free = [i for i in range(1, amount) if holding[i] < largest] or [i for i in range(1, amount) if holding[i] < limit]
        whole, left = sum([loads[i] for i in free]), rest
        for i in free:
            more = min(limit - holding[i], max(1, left * loads[i] // whole), rest)
            holding[i] = holding[i] + more
            rest = rest - more
    return np.array(holding)


def scatter_about(rng, dims, scale, bound, cuts=(), held_as=jnp.bfloat16):
    result = scale * jax.random.normal(rng, dims, jnp.float32)
    if cuts:
        result = result * level_of(rng, dims, cuts, -0.22, 0.18)
    return jnp.clip(result, -bound, bound).astype(held_as)


def setup_inputs(seed: int = 0) -> dict:
    key_of = jax.random.split(jax.random.key(seed), 15)
    hidden_in = scatter_about(key_of[0], (SEQS, LENGTH, D), 1.0, 6.0, ((0, 8), (1, 4)))
    span_order = draw_span_order(jax.random.fold_in(key_of[14], 71), 0)
    routes_keys = jax.random.split(jax.random.fold_in(key_of[2], 1), SEQS * LENGTH // TOK_DEV)
    routes_turns = jax.random.permutation(jax.random.fold_in(key_of[2], 3), SEQS * LENGTH // TOK_DEV)
    routes = jax.vmap(lambda own, number: shared_out(jax.random.fold_in(key_of[2], 2), own, number, TOK_DEV, EXPERTS, TOPK, CAP, 1))(routes_keys, routes_turns).reshape((SEQS, LENGTH, TOPK))
    attn_gain = jnp.clip(1.0 + 0.1 * jax.random.normal(key_of[3], (D,), jnp.float32), 0.5, 1.5).astype(jnp.bfloat16)
    query_weight = draw_query_weight(jax.random.fold_in(key_of[14], 71), 0)
    key_weight = draw_key_weight(jax.random.fold_in(key_of[14], 71), 0)
    value_weight = scatter_about(key_of[6], (D, KVW), D ** -0.5, 0.15625, ((0, 8),))
    out_weight = scatter_about(key_of[7], (D, QW), 1.0, 6.0, ((0, 8),))
    ffn_gain = jnp.clip(1.0 + 0.1 * jax.random.normal(key_of[8], (D,), jnp.float32), 0.5, 1.5).astype(jnp.bfloat16)
    router_weight = draw_router_weight(jax.random.fold_in(key_of[14], 71), 0)
    gate_weight = scatter_about(key_of[10], (EXPERTS, D, FF), D ** -0.5, 0.15625, ((0, 8),))
    up_weight = scatter_about(key_of[11], (EXPERTS, D, FF), D ** -0.5, 0.15625, ((0, 8),))
    down_weight = scatter_about(key_of[12], (EXPERTS, D, FF), 0.5, 3.0, ((0, 8),))
    cotangent = scatter_about(key_of[13], (SEQS, LENGTH, D), 1.0, 6.0, ((0, 8), (1, 4)))
    return {"hidden_in": hidden_in, "span_order": span_order, "routes": routes, "attn_gain": attn_gain, "query_weight": query_weight, "key_weight": key_weight, "value_weight": value_weight, "out_weight": out_weight, "ffn_gain": ffn_gain, "router_weight": router_weight, "gate_weight": gate_weight, "up_weight": up_weight, "down_weight": down_weight, "cotangent": cotangent}


NORM_EPS = 1e-06
ATTN_SCALE = 0.015625
RESID_SCALE = 0.22
ROPE_THETA = 10000.0
MASKED_SCORE = -1e+30
HIGHEST = lax.Precision.HIGHEST

@jax.custom_vjp
def low(v):
    return lax.optimization_barrier(v.astype(jnp.bfloat16)).astype(jnp.float32)

@jax.custom_vjp
def low_back(v):
    return v

def low_keep(v):
    return (low(v), None)

def low_pass(kept, grad):
    return (grad,)

def back_keep(v):
    return (v, None)

def back_low(kept, grad):
    return (low(grad),)
low.defvjp(low_keep, low_pass)
low_back.defvjp(back_keep, back_low)

def rope_tables(positions, head_size):
    half_size = head_size // 2
    frequencies = ROPE_THETA ** (-2.0 * jnp.arange(half_size, dtype=jnp.float32) / head_size)
    angles = positions.astype(jnp.float32)[:, None] * frequencies[None, :]
    return (jnp.cos(angles)[:, None, :], jnp.sin(angles)[:, None, :])

def rotate(rope_field, cosine_table, sine_table):
    half_size = rope_field.shape[-1] // 2
    front_half = rope_field[..., :half_size]
    back_half = rope_field[..., half_size:]
    return jnp.concatenate([front_half * cosine_table - back_half * sine_table, back_half * cosine_table + front_half * sine_table], axis=-1)

def slot_maps(route_rows, expert_count, capacity):
    flat_routes = route_rows.reshape(-1)
    expert_hits = (flat_routes[:, None] == jnp.arange(expert_count, dtype=jnp.int32)[None, :]).astype(jnp.int32)
    slot_ranks = lax.optimization_barrier(jnp.sum((jnp.cumsum(expert_hits, axis=0) - 1) * expert_hits, axis=1))
    slot_of_pair = (flat_routes * capacity + slot_ranks).astype(jnp.int32)
    pair_token = (jnp.arange(flat_routes.shape[0], dtype=jnp.int32) // route_rows.shape[1]).astype(jnp.int32)
    slot_token = jnp.zeros((expert_count * capacity,), jnp.int32).at[slot_of_pair].set(pair_token)
    slot_used = jnp.zeros((expert_count * capacity,), jnp.int32).at[slot_of_pair].set(1)
    return (slot_of_pair, slot_token, slot_used)

def block_layer(params, inputs, positions, route_blocks, slot_of_pair, slot_token, slot_used):
    gain_one, w_query, w_key, w_value, w_out, gain_two, w_router, w_gate, w_up, w_down = params
    cosine_table, sine_table = rope_tables(positions, HEAD)
    causal = positions[:, None] >= positions[None, :]
    group_size = HEADS // KV_HEADS

    def attention(seq_rows):
        scale_one = lax.rsqrt(lax.optimization_barrier(jnp.mean(seq_rows * seq_rows, axis=-1, keepdims=True)) + NORM_EPS)
        attn_in = low(seq_rows * scale_one * gain_one)
        query_lin = low_back(jnp.dot(attn_in, w_query, precision=HIGHEST)).reshape(LENGTH, HEADS, HEAD)
        key_lin = low_back(jnp.dot(attn_in, w_key, precision=HIGHEST)).reshape(LENGTH, KV_HEADS, HEAD)
        value_rows = low(low_back(jnp.dot(attn_in, w_value, precision=HIGHEST))).reshape(LENGTH, KV_HEADS, HEAD)
        query_rot = low(rotate(query_lin, cosine_table, sine_table)).reshape(LENGTH, KV_HEADS, group_size, HEAD)
        key_rot = low(rotate(key_lin, cosine_table, sine_table))
        raw_scores = low_back(jnp.einsum('tkgd,skd->kgts', query_rot, key_rot, precision=HIGHEST))
        scores = jnp.where(causal, raw_scores * ATTN_SCALE, MASKED_SCORE)
        weights = low(jax.nn.softmax(scores, axis=-1))
        attn_mix = jnp.einsum('kgts,skd->tkgd', weights, value_rows, precision=HIGHEST).reshape(LENGTH, HEADS * HEAD)
        attn_mix = low(low_back(attn_mix))
        branch = low_back(lax.dot_general(attn_mix, w_out, (((1,), (1,)), ((), ())), precision=HIGHEST))
        return seq_rows + RESID_SCALE * branch
    after_attn = lax.map(jax.checkpoint(attention), inputs)
    scale_two = lax.rsqrt(lax.optimization_barrier(jnp.mean(after_attn * after_attn, axis=-1, keepdims=True)) + NORM_EPS)
    ffn_in = low(after_attn * scale_two * gain_two)
    router_probs = jax.nn.softmax(jnp.dot(ffn_in, w_router, precision=HIGHEST), axis=-1)
    ffn_blocks = ffn_in.reshape(-1, TOK_DEV, D)
    combine = jnp.take_along_axis(router_probs.reshape(-1, TOK_DEV, EXPERTS), route_blocks, axis=-1)

    def experts(block_args):
        block_rows, block_combine, block_slots, block_tokens, block_used = block_args
        dispatched = low_back(block_rows[block_tokens] * block_used[:, None].astype(jnp.float32)).reshape(EXPERTS, CAP, D)
        gate_act = low_back(jnp.einsum('ecd,edf->ecf', dispatched, w_gate, precision=HIGHEST))
        up_act = low_back(jnp.einsum('ecd,edf->ecf', dispatched, w_up, precision=HIGHEST))
        hidden = low(jax.nn.silu(gate_act) * up_act)
        expert_out = low(low_back(jnp.einsum('ecf,edf->ecd', hidden, w_down, precision=HIGHEST))).reshape(EXPERTS * CAP, D)
        picked = expert_out[block_slots].reshape(TOK_DEV, TOPK, D)
        return lax.optimization_barrier(jnp.sum(block_combine[:, :, None] * picked, axis=1))
    mixture = lax.map(jax.checkpoint(experts), (ffn_blocks, combine, slot_of_pair, slot_token, slot_used))
    return after_attn + RESID_SCALE * mixture.reshape(after_attn.shape)

def reference(hidden_in, span_order, routes, attn_gain, query_weight, key_weight, value_weight, out_weight, ffn_gain, router_weight, gate_weight, up_weight, down_weight, cotangent):
    half_block = TOK_DEV // 2
    row_index = jnp.arange(LENGTH, dtype=jnp.int32)
    positions = (span_order[row_index // half_block] * half_block + row_index % half_block).astype(jnp.int32)
    route_blocks = routes.reshape(-1, TOK_DEV, TOPK)
    slot_of_pair, slot_token, slot_used = jax.vmap(lambda route_rows: slot_maps(route_rows, EXPERTS, CAP))(route_blocks)
    params = tuple((weight_arg.astype(jnp.float32) for weight_arg in (attn_gain, query_weight, key_weight, value_weight, out_weight, ffn_gain, router_weight, gate_weight, up_weight, down_weight)))
    outputs, pullback = jax.vjp(lambda param_set, inputs_f: block_layer(param_set, inputs_f, positions, route_blocks, slot_of_pair, slot_token, slot_used), params, hidden_in.astype(jnp.float32))
    weight_grads, grad_in = pullback(cotangent.astype(jnp.float32))
    return (outputs.astype(jnp.bfloat16), grad_in, weight_grads[0], weight_grads[1], weight_grads[2], weight_grads[3], weight_grads[4], weight_grads[5], weight_grads[6], weight_grads[7], weight_grads[8], weight_grads[9])
```

```python
import functools
import math

import jax
import jax.numpy as jnp
from jax import lax
from jax.experimental import pallas as pl
from jax.experimental.pallas import tpu as pltpu
from jax.sharding import PartitionSpec as P

HEAD = 64
HALF = HEAD // 2
NORM_EPS = 1e-06
ATTN_SCALE = 0.015625
RESID_SCALE = 0.22
ROPE_THETA = 10000.0
MASKED_SCORE = -1e30
LANES = 128
LAST = (((1,), (1,)), ((), ()))
FIRST = (((0,), (0,)), ((), ()))
F32 = jnp.float32
BF16 = jnp.bfloat16
VMEM = pl.BlockSpec(memory_space=pltpu.VMEM)
SMEM = pl.BlockSpec(memory_space=pltpu.SMEM)


def params(mib=60, **kw):
    return pltpu.CompilerParams(vmem_limit_bytes=mib * 2**20, **kw)


def call(kernel, outs, ins, scratch=(), flops=0):
    size = lambda v: v.size * v.dtype.itemsize
    return pl.pallas_call(
        kernel,
        out_shape=outs,
        in_specs=[SMEM] + [VMEM] * (len(ins) - 1),
        out_specs=[VMEM] * len(outs),
        scratch_shapes=list(scratch),
        compiler_params=params(),
        cost_estimate=pl.CostEstimate(
            flops=flops, bytes_accessed=sum(map(size, list(ins) + list(outs))), transcendentals=0
        ),
    )(*ins)


def shape(dims, dtype):
    return jax.ShapeDtypeStruct(tuple(dims), dtype)


def dot(a, b, dims=(((1,), (0,)), ((), ()))):
    return lax.dot_general(a, b, dims, preferred_element_type=F32)


def scale_of(x):
    return lax.rsqrt(jnp.mean(x * x, axis=-1, keepdims=True) + NORM_EPS)


def gain_row(misc_ref, column):
    return misc_ref[...].astype(F32).T[column : column + 1, :]


def span_rows(spans, index, size):
    return pl.ds(pl.multiple_of(spans[index] * size, size), size)


def rope(front, back, cosine, sine):
    return jnp.concatenate([front * cosine - back * sine, back * cosine + front * sine], axis=-1)


def unrope(front, back, cosine, sine):
    return jnp.concatenate([front * cosine + back * sine, back * cosine - front * sine], axis=-1)


def project_kernel(count, heads, kv_heads, experts, spans, *refs):
    pieces = refs[:count]
    weight, misc, cosine, sine, attn_in, query, key, value = refs[count:]
    gain = gain_row(misc, experts)
    size = pieces[0].shape[0] // 2
    for j in range(count):
        x = pieces[j][...].astype(F32)
        rows_in = (x * scale_of(x) * gain).astype(BF16)
        lin = dot(rows_in, weight[...])
        for h in range(2):
            at = span_rows(spans, 2 * j + h, size)
            cut = slice(h * size, (h + 1) * size)
            attn_in[at, :] = rows_in[cut]
            cos, sin = cosine[at, :], sine[at, :]
            for i in range(heads + kv_heads):
                lo = i * HEAD
                turned = rope(lin[cut, lo : lo + HALF], lin[cut, lo + HALF : lo + HEAD], cos, sin)
                if i < heads:
                    query[i, at, :] = (turned * ATTN_SCALE).astype(BF16)
                else:
                    key[i - heads, at, :] = turned.astype(BF16)
            for i in range(kv_heads):
                lo = (heads + kv_heads + i) * HEAD
                value[i, at, :] = lin[cut, lo : lo + HEAD].astype(BF16)


def diagonal(size, group):
    keys = lax.broadcasted_iota(jnp.int32, (size, group * size), 0)
    queries = lax.broadcasted_iota(jnp.int32, (size, group * size), 1) % size
    return keys <= queries


def scores_of(key_rows, query_rows, keep, size):
    raw = dot(key_rows, query_rows, LAST)
    seen = raw.shape[0] - size
    last = jnp.where(keep, raw[seen:], MASKED_SCORE)
    return last if seen == 0 else jnp.concatenate([raw[:seen], last], axis=0)


def attend_kernel(count, spans, query, key, value, w_out, mix, lse, *parts):
    kv_heads, length, _ = key.shape
    group = query.shape[0] // kv_heads
    blocks = 2 * count
    size = length // blocks
    keep = diagonal(size, group)
    for g in range(kv_heads):
        for i in range(blocks):
            rows = slice(i * size, (i + 1) * size)
            seen = (i + 1) * size
            q = query[g * group : (g + 1) * group, rows, :].reshape(group * size, HEAD)
            scores = scores_of(key[g, :seen, :], q, keep, size)
            top = jnp.max(scores, axis=0, keepdims=True)
            grown = jnp.exp(scores - top)
            total = jnp.sum(grown, axis=0, keepdims=True)
            mixed = dot(value[g, :seen, :], grown.astype(BF16), FIRST) / total
            lse[g, i, :, :] = top + jnp.log(total)
            for r in range(group):
                lo = (g * group + r) * HEAD
                mix[rows, lo : lo + HEAD] = mixed[:, r * size : (r + 1) * size].T.astype(BF16)
    for j in range(count):
        own = jnp.concatenate([mix[span_rows(spans, 2 * j + h, size), :] for h in range(2)], axis=0)
        parts[j][...] = dot(own, w_out[...], LAST).astype(parts[j].dtype)


def norm_two_kernel(experts, _, x, misc, *refs):
    parts, (after, ffn_in) = refs[:-2], refs[-2:]
    branch = sum(p[...].astype(F32) for p in parts)
    rows = x[...].astype(F32) + RESID_SCALE * branch
    after[...] = rows
    ffn_in[...] = (rows * scale_of(rows) * gain_row(misc, experts + 1)).astype(BF16)


def router_probs(rows, router, experts):
    logits = dot(rows, router)
    lane = lax.broadcasted_iota(jnp.int32, logits.shape, 1)
    logits = jnp.where(lane < experts, logits, MASKED_SCORE)
    grown = jnp.exp(logits - jnp.max(logits, axis=-1, keepdims=True))
    return grown / jnp.sum(grown, axis=-1, keepdims=True), lane


def experts_kernel(
    experts, cap, me, rows_ref, grad_ref, w_gate, w_up, w_down, misc,
    mix_ref, back_ref, disp, slots, grad_gate, grad_up, hidden_ref, keys
):
    local = w_gate.shape[0]
    width = w_gate.shape[1]
    rows = rows_ref[...]
    count = rows.shape[0] // 2
    probs, lane = router_probs(rows, misc[...], experts)
    keys[...] = grad_ref[:, width:].astype(F32).T
    grad = grad_ref[:, :width].astype(F32) * RESID_SCALE
    slot = lax.broadcasted_iota(jnp.int32, (cap, count), 0).astype(F32)
    mixed = [jnp.zeros((count, width), F32)] * 2
    back = [jnp.zeros((count, width), F32)] * 2
    notes = [jnp.zeros((count, LANES), F32)] * 2
    for e in range(local):
        name = me[0] * local + e
        key = keys[pl.ds(name, 1), :]
        share = jnp.sum(jnp.where(lane == name, probs, 0.0), axis=-1, keepdims=True)
        scaled = (grad * share).astype(BF16)
        picks = [(slot == key[:, b * count : (b + 1) * count]).astype(BF16) for b in range(2)]
        cuts = [slice(b * count, (b + 1) * count) for b in range(2)]
        mine = jnp.concatenate([dot(picks[b], rows[cuts[b]]) for b in range(2)], 0).astype(BF16)
        grads = jnp.concatenate([dot(picks[b], scaled[cuts[b]]) for b in range(2)], 0).astype(BF16)
        disp[e, 0] = mine
        slots[e, 0] = grads
        gate, up = dot(mine, w_gate[e]), dot(mine, w_up[e])
        sigmoid = 1.0 / (1.0 + jnp.exp(-gate))
        silu = gate * sigmoid
        hidden = (silu * up).astype(BF16)
        hidden_ref[e, 0] = hidden
        out = dot(hidden, w_down[e], LAST).astype(BF16)
        grad_hidden = dot(grads, w_down[e])
        d_gate = (grad_hidden * up * sigmoid * (1.0 + gate * (1.0 - sigmoid))).astype(BF16)
        d_up = (grad_hidden * silu).astype(BF16)
        grad_gate[e, 0] = d_gate
        grad_up[e, 0] = d_up
        d_in = (dot(d_gate, w_gate[e], LAST) + dot(d_up, w_up[e], LAST)).astype(BF16)
        for b in range(2):
            at = slice(b * cap, (b + 1) * cap)
            picked = dot(picks[b], out[at], FIRST)
            mixed[b] = mixed[b] + share[cuts[b]] * picked
            note = jnp.sum(grad[cuts[b]] * picked, axis=-1, keepdims=True)
            high = note.astype(BF16).astype(F32)
            notes[b] = (
                notes[b]
                + jnp.where(lane[cuts[b]] == name, high, 0.0)
                + jnp.where(lane[cuts[b]] == name + LANES // 2, note - high, 0.0)
            )
            back[b] = back[b] + dot(picks[b], d_in[at], FIRST)
    for b in range(2):
        at = slice(b * count, (b + 1) * count)
        mix_ref[at, :] = mixed[b].astype(BF16)
        back_ref[at, :width] = back[b].astype(BF16)
        back_ref[at, width:] = notes[b].astype(BF16)


def expert_terms_kernel(disp, slots, grad_gate, grad_up, hidden, out):
    count, _, _, depth, _ = out.shape
    pairs = ((disp, grad_gate), (disp, grad_up), (slots, hidden))
    for i, (left, right) in enumerate(pairs):
        full = dot(left[0], right[0], FIRST).astype(BF16)
        for c in range(count):
            out[c, i, 0] = full[c * depth : (c + 1) * depth]


def norm_two_back_kernel(experts, _, back, cotangent, after, misc, grad_after, grad_branch, terms):
    width = after.shape[1]
    rows = after[...]
    scale = scale_of(rows)
    normed = rows * scale
    gain = gain_row(misc, experts + 1)
    ffn_in = (normed * gain).astype(BF16)
    probs, lane = router_probs(ffn_in, misc[...], experts)
    notes = back[:, width:].astype(F32)
    notes = notes + pltpu.roll(notes, LANES // 2, 1)
    notes = jnp.where(lane < experts, notes, 0.0)
    logits = probs * (notes - jnp.sum(probs * notes, axis=-1, keepdims=True))
    high = logits.astype(BF16)
    low = (logits - high.astype(F32)).astype(BF16)
    grad_in = back[:, :width].astype(F32) + dot(high, misc[...], LAST) + dot(low, misc[...], LAST)
    grad_gain = jnp.sum(grad_in * normed, axis=0, keepdims=True)
    line = lax.broadcasted_iota(jnp.int32, (LANES, width), 0)
    terms[...] = (
        dot(ffn_in, high, FIRST)
        + dot(ffn_in, low, FIRST)
        + jnp.where(line == experts + 1, grad_gain, 0.0).T
    )
    scaled = grad_in * gain
    grad = cotangent[...].astype(F32) + scale * (
        scaled - normed * jnp.mean(scaled * normed, axis=-1, keepdims=True)
    )
    grad_after[...] = grad
    grad_branch[...] = (RESID_SCALE * grad).astype(BF16)


def attend_back_kernel(count, spans, *refs):
    pieces = refs[:count]
    w_out, query, key, value, lse, cosine, sine, lin, grads, key_sum, value_sum = refs[count:]
    kv_heads, length, _ = key.shape
    heads = query.shape[0]
    group = heads // kv_heads
    blocks = 2 * count
    size = length // blocks
    keep = diagonal(size, group)
    for j in range(count):
        rows = dot(pieces[j][...], w_out[...]).astype(BF16)
        for h in range(2):
            at = span_rows(spans, 2 * j + h, size)
            for i in range(heads):
                grads[i, at, :] = rows[h * size : (h + 1) * size, i * HEAD : (i + 1) * HEAD]
    for g in range(kv_heads):
        key_sum[...] = jnp.zeros_like(key_sum)
        value_sum[...] = jnp.zeros_like(value_sum)
        for i in range(blocks):
            rows = slice(i * size, (i + 1) * size)
            seen = (i + 1) * size
            q = query[g * group : (g + 1) * group, rows, :].reshape(group * size, HEAD)
            grad = grads[g * group : (g + 1) * group, rows, :].reshape(group * size, HEAD)
            probs = jnp.exp(scores_of(key[g, :seen, :], q, keep, size) - lse[g, i])
            grad_probs = dot(value[g, :seen, :], grad, LAST)
            delta = jnp.sum(probs * grad_probs, axis=0, keepdims=True)
            raw = (probs * (grad_probs - delta)).astype(BF16)
            value_sum[:seen, :] += dot(probs.astype(BF16), grad)
            key_sum[:seen, :] += dot(raw, q)
            grad_query = dot(key[g, :seen, :], raw, FIRST) * ATTN_SCALE
            for r in range(group):
                turned = grad_query[:, r * size : (r + 1) * size].T
                lo = (g * group + r) * HEAD
                lin[rows, lo : lo + HEAD] = unrope(
                    turned[:, :HALF], turned[:, HALF:], cosine[rows, :], sine[rows, :]
                ).astype(BF16)
        lo = (heads + g) * HEAD
        lin[:, lo : lo + HEAD] = unrope(
            key_sum[:, :HALF], key_sum[:, HALF:], cosine[...], sine[...]
        ).astype(BF16)
        lo = (heads + kv_heads + g) * HEAD
        lin[:, lo : lo + HEAD] = value_sum[...].astype(BF16)


def input_terms_kernel(count, spans, lin, weight, *parts):
    size = lin.shape[0] // (2 * count)
    for j in range(count):
        own = jnp.concatenate([lin[span_rows(spans, 2 * j + h, size), :] for h in range(2)], axis=0)
        parts[j][...] = dot(own, weight[...], LAST).astype(parts[j].dtype)


def weight_terms_kernel(count, experts, spans, *refs):
    pieces = refs[:count]
    attn_in, lin, mix, weight, misc, more, out, branch = refs[count:]
    length, width = attn_in.shape
    size = length // (2 * count)
    for j in range(count):
        for h in range(2):
            branch[span_rows(spans, 2 * j + h, size), :] = pieces[j][h * size : (h + 1) * size, :]
    step = width // count
    lane = lax.broadcasted_iota(jnp.int32, (step, LANES), 1)
    for c in range(count):
        cut = slice(c * step, (c + 1) * step)
        attn = dot(attn_in[:, cut], lin[...], FIRST)
        outs = dot(branch[:, cut], mix[...], FIRST)
        gain = misc[cut, :].astype(F32)[:, experts : experts + 1]
        grad_gain = jnp.sum(weight[cut, :].astype(F32) * attn, axis=-1, keepdims=True) / gain
        notes = more[cut, :] + jnp.where(lane == experts, grad_gain, 0.0)
        high = notes.astype(BF16).astype(F32)
        notes = high + pltpu.roll(jnp.where(lane < LANES // 2, notes - high, 0.0), LANES // 2, 1)
        full = jnp.concatenate([attn, outs, notes], axis=1).astype(BF16)
        if len(out.shape) == 2:
            out[cut, :] = full
        else:
            each = out.shape[2]
            for f in range(out.shape[0]):
                out[f, c] = full[f * each : (f + 1) * each]


def norm_one_back_kernel(experts, _, x, misc, grad_after, *refs):
    parts, grad_in = refs[:-1], refs[-1]
    grad = sum(p[...].astype(F32) for p in parts) * gain_row(misc, experts)
    rows = x[...].astype(F32)
    scale = scale_of(rows)
    normed = rows * scale
    grad_in[...] = grad_after[...] + scale * (
        grad - normed * jnp.mean(grad * normed, axis=-1, keepdims=True)
    )


def split_kernel(experts, widths, _, terms, query, key, value, out, notes):
    count = terms.shape[0]
    for s in range(count):
        lo = 0
        for ref, wide in zip((query, key, value, out), widths):
            ref[:, s * wide : (s + 1) * wide] = terms[s, :, lo : lo + wide].astype(F32)
            lo += wide
    total = sum(terms[s, :, lo:].astype(F32) for s in range(count))
    notes[...] = total + pltpu.roll(total, LANES // 2, 1)


def exchange(value, axis, offset):
    n = lax.axis_size(axis)
    return lax.ppermute(value, axis, [(i, i ^ offset) for i in range(n)])


def slot_keys(route_rows, experts):
    hits = (route_rows[:, :, None] == jnp.arange(experts, dtype=jnp.int32)).any(axis=1)
    rows = jnp.arange(route_rows.shape[0], dtype=jnp.int32)
    earlier = (rows[None, :] < rows[:, None]).astype(BF16)
    ranks = jnp.dot(earlier, hits.astype(BF16), preferred_element_type=F32)
    keys = jnp.where(hits, ranks, -1.0).astype(BF16)
    return jnp.pad(keys, ((0, 0), (0, LANES - experts)), constant_values=-1)


def body(
    hidden_in, span_order, routes, attn_gain, query_weight, key_weight, value_weight, out_weight,
    ffn_gain, router_weight, gate_weight, up_weight, down_weight, cotangent
):
    ctx, fsdp = lax.axis_size("ctx"), lax.axis_size("fsdp")
    me_ctx, me_fsdp = lax.axis_index("ctx"), lax.axis_index("fsdp")
    x = hidden_in[0]
    count, width = x.shape
    length = ctx * count
    heads = query_weight.shape[1] // HEAD // ctx
    kv_heads = key_weight.shape[1] // HEAD // ctx
    experts = router_weight.shape[1]
    local, _, units = gate_weight.shape
    cap = count * routes.shape[2] * 5 // (4 * experts)
    q_wide, kv_wide = heads * HEAD, kv_heads * HEAD
    lin_wide = q_wide + 2 * kv_wide
    chips = fsdp // 2
    no_scalars = jnp.zeros((1,), jnp.int32)

    own = lambda w, wide: lax.dynamic_slice_in_dim(w, me_ctx * wide, wide, 1)
    pack = jnp.concatenate(
        [
            own(query_weight, q_wide),
            own(key_weight, kv_wide),
            own(value_weight, kv_wide),
            own(out_weight, q_wide),
            router_weight,
            attn_gain[:, None],
            ffn_gain[:, None],
            jnp.zeros((attn_gain.shape[0], LANES - experts - 2), BF16),
        ],
        axis=1,
    )
    pack = lax.all_gather(pack, "fsdp", axis=0, tiled=True)
    w_lin, w_out, misc = (
        pack[:, :lin_wide],
        pack[:, lin_wide : lin_wide + q_wide],
        pack[:, lin_wide + q_wide :],
    )
    pieces = [x] + [exchange(x, "ctx", j) for j in range(1, ctx)]
    owners = jnp.stack([me_ctx ^ j for j in range(ctx)])
    spans = span_order.reshape(ctx, 2)[owners].reshape(-1)
    keys = slot_keys(routes[0], experts)
    grad_pack = lax.all_gather(
        jnp.concatenate([cotangent[0], keys], axis=1), "fsdp", axis=0, tiled=True
    )
    frequencies = ROPE_THETA ** (-2.0 * jnp.arange(HALF, dtype=F32) / HEAD)
    angles = jnp.arange(length, dtype=F32)[:, None] * frequencies[None, :]
    cosine, sine = jnp.cos(angles), jnp.sin(angles)

    attn_in, query, key, value = call(
        functools.partial(project_kernel, ctx, heads, kv_heads, experts),
        [
            shape((length, width), BF16),
            shape((heads, length, HEAD), BF16),
            shape((kv_heads, length, HEAD), BF16),
            shape((kv_heads, length, HEAD), BF16),
        ],
        [spans, *pieces, w_lin, misc, cosine, sine],
        flops=2 * length * width * lin_wide,
    )
    part_types = [shape((count, width), F32 if j == 0 else BF16) for j in range(ctx)]
    mix, lse, *parts = call(
        functools.partial(attend_kernel, ctx),
        [
            shape((length, q_wide), BF16),
            shape((kv_heads, 2 * ctx, 1, heads // kv_heads * length // (2 * ctx)), F32),
            *part_types,
        ],
        [spans, query, key, value, w_out],
        flops=8 * length * length * q_wide,
    )
    parts = [parts[0]] + [exchange(parts[j], "ctx", j) for j in range(1, ctx)]
    after, ffn_in = call(
        functools.partial(norm_two_kernel, experts),
        [shape((count, width), F32), shape((count, width), BF16)],
        [no_scalars, x, misc, *parts],
    )
    rows_all = lax.all_gather(ffn_in, "fsdp", axis=0, tiled=True)

    whole = lambda *dims: pl.BlockSpec(
        dims, lambda i, me: (0,) * len(dims), pipeline_mode=pl.Buffered(1)
    )
    lines = lambda wide: pl.BlockSpec((2 * count, wide), lambda i, me: (i, 0))
    stored = lambda wide: pl.BlockSpec((local, 1, 2 * cap, wide), lambda i, me: (0, i, 0, 0))
    mix_part, back_part, *saved = pl.pallas_call(
        functools.partial(experts_kernel, experts, cap),
        out_shape=[
            shape((fsdp * count, width), BF16),
            shape((fsdp * count, width + LANES), BF16),
            *[shape((local, chips, 2 * cap, w), BF16) for w in (width, width, units, units, units)],
        ],
        grid_spec=pltpu.PrefetchScalarGridSpec(
            num_scalar_prefetch=1,
            grid=(chips,),
            in_specs=[
                lines(width),
                lines(width + LANES),
                *[whole(local, width, units)] * 3,
                whole(width, LANES),
            ],
            out_specs=[
                lines(width),
                lines(width + LANES),
                *[stored(w) for w in (width, width, units, units, units)],
            ],
            scratch_shapes=[pltpu.VMEM((LANES, 2 * count), F32)],
        ),
        compiler_params=params(),
        cost_estimate=pl.CostEstimate(
            flops=16 * local * fsdp * cap * width * units,
            bytes_accessed=60 * 2**20,
            transcendentals=0,
        ),
    )(me_fsdp[None], rows_all, grad_pack, gate_weight, up_weight, down_weight, misc)

    back = lax.psum_scatter(back_part, "fsdp", scatter_dimension=0, tiled=True)
    mixture = lax.psum_scatter(mix_part, "fsdp", scatter_dimension=0, tiled=True)
    hidden_out = (after + RESID_SCALE * mixture.astype(F32)).astype(BF16)[None]

    depth = width // ctx
    slots = fsdp * cap
    saved = [s.reshape(local, slots, s.shape[-1]) for s in saved]
    step = math.lcm(depth, LANES)
    tall = pl.BlockSpec((1, slots, step), lambda e, c: (e, 0, c))
    thin = pl.BlockSpec((1, slots, units), lambda e, c: (e, 0, 0))
    expert_terms = pl.pallas_call(
        expert_terms_kernel,
        out_shape=shape((ctx, 3, local, depth, units), BF16),
        grid=(local, width // step),
        in_specs=[tall, tall, thin, thin, thin],
        out_specs=pl.BlockSpec((step // depth, 3, 1, depth, units), lambda e, c: (c, 0, e, 0, 0)),
        compiler_params=params(),
        cost_estimate=pl.CostEstimate(
            flops=6 * local * slots * width * units, bytes_accessed=40 * 2**20, transcendentals=0
        ),
    )(*saved)
    expert_sums = lax.psum_scatter(
        expert_terms.reshape(-1, units), "ctx", scatter_dimension=0, tiled=True
    ).reshape(3, local, depth, units)
    grad_gate, grad_up, grad_down = (expert_sums[i].astype(F32) for i in range(3))

    grad_after, grad_branch, more = call(
        functools.partial(norm_two_back_kernel, experts),
        [shape((count, width), F32), shape((count, width), BF16), shape((width, LANES), F32)],
        [no_scalars, back, cotangent[0], after, misc],
    )
    branches = [grad_branch] + [exchange(grad_branch, "ctx", j) for j in range(1, ctx)]
    [lin] = call(
        functools.partial(attend_back_kernel, ctx),
        [shape((length, lin_wide), BF16)],
        [spans, *branches, w_out, query, key, value, lse, cosine, sine],
        scratch=[
            pltpu.VMEM((heads, length, HEAD), BF16),
            pltpu.VMEM((length, HEAD), F32),
            pltpu.VMEM((length, HEAD), F32),
        ],
        flops=20 * length * length * q_wide,
    )
    in_parts = call(
        functools.partial(input_terms_kernel, ctx),
        part_types,
        [spans, lin, w_lin],
        flops=2 * length * width * lin_wide,
    )
    in_parts = [in_parts[0]] + [exchange(in_parts[j], "ctx", j) for j in range(1, ctx)]
    total_wide = lin_wide + q_wide + LANES
    each = width // (ctx * fsdp)
    direct = each % 16 == 0
    [terms] = call(
        functools.partial(weight_terms_kernel, ctx, experts),
        [shape((fsdp, ctx, each, total_wide) if direct else (width, total_wide), BF16)],
        [spans, *branches, attn_in, lin, mix, w_lin, misc, more],
        scratch=[pltpu.VMEM((length, width), BF16)],
        flops=2 * length * width * (lin_wide + q_wide),
    )
    if not direct:
        terms = terms.reshape(ctx, fsdp, each, total_wide).swapaxes(0, 1)
    terms = lax.psum_scatter(terms, "fsdp", scatter_dimension=0, tiled=True)[0]
    terms = lax.all_to_all(terms, "ctx", split_axis=0, concat_axis=0, tiled=True)
    grad_query, grad_key, grad_value, grad_out, notes = call(
        functools.partial(split_kernel, experts, (q_wide, kv_wide, kv_wide, q_wide)),
        [
            *[shape((each, ctx * w), F32) for w in (q_wide, kv_wide, kv_wide, q_wide)],
            shape((each, LANES), F32),
        ],
        [no_scalars, terms],
    )
    [grad_in] = call(
        functools.partial(norm_one_back_kernel, experts),
        [shape((count, width), F32)],
        [no_scalars, x, misc, grad_after, *in_parts],
    )
    return (
        hidden_out,
        grad_in[None],
        notes[:, experts],
        grad_query,
        grad_key,
        grad_value,
        grad_out,
        notes[:, experts + 1],
        notes[:, :experts],
        grad_gate,
        grad_up,
        grad_down,
    )


def solution(mesh):
    rows, both = P("fsdp", "ctx", None), ("ctx", "fsdp")
    split = P("fsdp", None)
    return jax.shard_map(
        body,
        mesh=mesh,
        in_specs=(
            rows, P(), rows, P("fsdp"), split, split, split, split, P("fsdp"), split,
            P("fsdp", None, None), P("fsdp", None, None), P("fsdp", None, None), rows,
        ),
        out_specs=(
            rows, rows, P(both), P(both, None), P(both, None), P(both, None), P(both, None),
            P(both), P(both, None), rows, rows, rows,
        ),
        check_vma=False,
    )
```

```python
import functools
import math

import jax
import jax.numpy as jnp
from jax import lax
from jax.experimental import pallas as pl
from jax.experimental.pallas import tpu as pltpu
from jax.sharding import PartitionSpec as P

HEAD = 64
HALF = HEAD // 2
NORM_EPS = 1e-06
ATTN_SCALE = 0.015625
RESID_SCALE = 0.22
ROPE_THETA = 10000.0
MASKED_SCORE = -1e30
LANES = 128
LAST = (((1,), (1,)), ((), ()))
FIRST = (((0,), (0,)), ((), ()))
F32 = jnp.float32
BF16 = jnp.bfloat16
VMEM = pl.BlockSpec(memory_space=pltpu.VMEM)
SMEM = pl.BlockSpec(memory_space=pltpu.SMEM)


def params(mib=60, **kw):
    return pltpu.CompilerParams(vmem_limit_bytes=mib * 2**20, **kw)


def call(kernel, outs, ins, scratch=(), flops=0):
    size = lambda v: v.size * v.dtype.itemsize
    return pl.pallas_call(
        kernel,
        out_shape=outs,
        in_specs=[SMEM] + [VMEM] * (len(ins) - 1),
        out_specs=[VMEM] * len(outs),
        scratch_shapes=list(scratch),
        compiler_params=params(),
        cost_estimate=pl.CostEstimate(
            flops=flops, bytes_accessed=sum(map(size, list(ins) + list(outs))), transcendentals=0
        ),
    )(*ins)


def shape(dims, dtype):
    return jax.ShapeDtypeStruct(tuple(dims), dtype)


def dot(a, b, dims=(((1,), (0,)), ((), ()))):
    return lax.dot_general(a, b, dims, preferred_element_type=F32)


def scale_of(x):
    return lax.rsqrt(jnp.mean(x * x, axis=-1, keepdims=True) + NORM_EPS)


def span_rows(spans, index, size):
    return pl.ds(pl.multiple_of(spans[index] * size, size), size)


def rope(front, back, cosine, sine):
    return jnp.concatenate([front * cosine - back * sine, back * cosine + front * sine], axis=-1)


def unrope(front, back, cosine, sine):
    return jnp.concatenate([front * cosine + back * sine, back * cosine - front * sine], axis=-1)


def project_kernel(count, heads, kv_heads, experts, spans, *refs):
    pieces = refs[:count]
    pack, cosine, sine, attn_in, query, key, value, router, gains = refs[count:]
    lin_wide = (heads + 2 * kv_heads) * HEAD
    router[...] = pack[:, lin_wide + heads * HEAD :]
    turned = router[...].astype(F32).T
    gains[...] = turned[experts : experts + 2, :]
    gain = turned[experts : experts + 1, :]
    size = pieces[0].shape[0] // 2
    for j in range(count):
        x = pieces[j][...].astype(F32)
        rows_in = (x * scale_of(x) * gain).astype(BF16)
        lin = dot(rows_in, pack[:, :lin_wide])
        for h in range(2):
            at = span_rows(spans, 2 * j + h, size)
            cut = slice(h * size, (h + 1) * size)
            attn_in[at, :] = rows_in[cut]
            cos, sin = cosine[at, :], sine[at, :]
            for i in range(heads + kv_heads):
                lo = i * HEAD
                turned = rope(lin[cut, lo : lo + HALF], lin[cut, lo + HALF : lo + HEAD], cos, sin)
                if i < heads:
                    query[i, at, :] = (turned * ATTN_SCALE).astype(BF16)
                else:
                    key[i - heads, at, :] = turned.astype(BF16)
            for i in range(kv_heads):
                lo = (heads + kv_heads + i) * HEAD
                value[i, at, :] = lin[cut, lo : lo + HEAD].astype(BF16)


def diagonal(size, group):
    keys = lax.broadcasted_iota(jnp.int32, (size, group * size), 0)
    queries = lax.broadcasted_iota(jnp.int32, (size, group * size), 1) % size
    return keys <= queries


def scores_of(key_rows, query_rows, keep, size):
    raw = dot(key_rows, query_rows, LAST)
    seen = raw.shape[0] - size
    last = jnp.where(keep, raw[seen:], MASKED_SCORE)
    return last if seen == 0 else jnp.concatenate([raw[:seen], last], axis=0)


def attend_kernel(count, spans, query, key, value, pack, mix, lse, *parts):
    kv_heads, length, _ = key.shape
    lo = (query.shape[0] + 2 * kv_heads) * HEAD
    w_out = pack[:, lo : lo + mix.shape[1]]
    group = query.shape[0] // kv_heads
    blocks = 2 * count
    size = length // blocks
    keep = diagonal(size, group)
    for g in range(kv_heads):
        for i in range(blocks):
            rows = slice(i * size, (i + 1) * size)
            seen = (i + 1) * size
            q = query[g * group : (g + 1) * group, rows, :].reshape(group * size, HEAD)
            scores = scores_of(key[g, :seen, :], q, keep, size)
            top = jnp.max(scores, axis=0, keepdims=True)
            grown = jnp.exp(scores - top)
            total = jnp.sum(grown, axis=0, keepdims=True)
            mixed = dot(value[g, :seen, :], grown.astype(BF16), FIRST) / total
            lse[g, i, :, :] = top + jnp.log(total)
            for r in range(group):
                lo = (g * group + r) * HEAD
                mix[rows, lo : lo + HEAD] = mixed[:, r * size : (r + 1) * size].T.astype(BF16)
    for j in range(count):
        own = jnp.concatenate([mix[span_rows(spans, 2 * j + h, size), :] for h in range(2)], axis=0)
        parts[j][...] = dot(own, w_out, LAST).astype(parts[j].dtype)


def norm_two_kernel(_, x, gains, *refs):
    parts, (after, ffn_in) = refs[:-2], refs[-2:]
    branch = sum(p[...].astype(F32) for p in parts)
    rows = x[...].astype(F32) + RESID_SCALE * branch
    after[...] = rows
    ffn_in[...] = (rows * scale_of(rows) * gains[1:2, :]).astype(BF16)


def router_probs(rows, router, experts):
    logits = dot(rows, router)
    lane = lax.broadcasted_iota(jnp.int32, logits.shape, 1)
    logits = jnp.where(lane < experts, logits, MASKED_SCORE)
    grown = jnp.exp(logits - jnp.max(logits, axis=-1, keepdims=True))
    return grown / jnp.sum(grown, axis=-1, keepdims=True), lane


def experts_kernel(experts, cap, splits, where, *refs):
    row_refs = refs[: 2 * splits]
    grad_all, *weights, misc = refs[2 * splits : 2 * splits + 5]
    mix_refs, back_refs, saved = refs[2 * splits + 5 :][:2], refs[2 * splits + 7 :][:2], refs[2 * splits + 9 :][:5]
    keys, grad_in, *held = refs[2 * splits + 14 :]
    kept, held, sems = held[3:8], held[:3], held[8]
    local, width, _ = weights[0].shape
    count = grad_in.shape[1]
    loads = [
        pltpu.make_async_copy(
            grad_all.at[pl.ds(pl.multiple_of(where[1 + b] * count, count), count), :],
            grad_in.at[b],
            sems.at[b],
        )
        for b in range(2)
    ]
    pulls = [
        [
            pltpu.make_async_copy(weights[i].at[e], held[i].at[e], sems.at[2 + 3 * e + i])
            for i in range(3)
        ]
        for e in range(local)
    ]
    stores = [
        [
            pltpu.make_async_copy(
                kept[i].at[e], saved[i].at[e], sems.at[2 + 3 * local + 5 * e + i]
            )
            for i in range(5)
        ]
        for e in range(local)
    ]
    for copy in loads + sum(pulls, []):
        copy.start()
    rows = [
        jnp.concatenate([r[...] for r in row_refs[b * splits : (b + 1) * splits]], axis=0)
        for b in range(2)
    ]
    shares = [router_probs(rows[b], misc[...], experts) for b in range(2)]
    for copy in loads:
        copy.wait()
    grad = []
    for b in range(2):
        keys[b] = grad_in[b, :, width:].astype(F32).T
        grad.append(grad_in[b, :, :width].astype(F32) * RESID_SCALE)
    slot = lax.broadcasted_iota(jnp.int32, (cap, count), 0).astype(F32)
    mixed = [jnp.zeros((count, width), F32)] * 2
    back = [jnp.zeros((count, width), F32)] * 2
    notes = [jnp.zeros((count, LANES), F32)] * 2
    w_gate, w_up, w_down = held
    for e in range(local):
        name = where[0] * local + e
        mine, grads, picks, share = [], [], [], []
        for b in range(2):
            probs, lane = shares[b]
            share.append(jnp.sum(jnp.where(lane == name, probs, 0.0), axis=-1, keepdims=True))
            picks.append((slot == keys[b, pl.ds(name, 1), :]).astype(BF16))
            mine.append(dot(picks[b], rows[b]).astype(BF16))
            grads.append(dot(picks[b], (grad[b] * share[b]).astype(BF16)).astype(BF16))
        mine, grads = jnp.concatenate(mine, axis=0), jnp.concatenate(grads, axis=0)
        for copy in pulls[e]:
            copy.wait()
        gate, up = dot(mine, w_gate[e]), dot(mine, w_up[e])
        sigmoid = 1.0 / (1.0 + jnp.exp(-gate))
        silu = gate * sigmoid
        hidden = (silu * up).astype(BF16)
        out = dot(hidden, w_down[e], LAST).astype(BF16)
        grad_hidden = dot(grads, w_down[e])
        d_gate = (grad_hidden * up * sigmoid * (1.0 + gate * (1.0 - sigmoid))).astype(BF16)
        d_up = (grad_hidden * silu).astype(BF16)
        for i, term in enumerate((mine, grads, d_gate, d_up, hidden)):
            kept[i][e] = term
            stores[e][i].start()
        d_in = (dot(d_gate, w_gate[e], LAST) + dot(d_up, w_up[e], LAST)).astype(BF16)
        for b in range(2):
            at = slice(b * cap, (b + 1) * cap)
            picked = dot(picks[b], out[at], FIRST)
            mixed[b] = mixed[b] + share[b] * picked
            note = jnp.sum(grad[b] * picked, axis=-1, keepdims=True)
            high = note.astype(BF16).astype(F32)
            lane = shares[b][1]
            notes[b] = (
                notes[b]
                + jnp.where(lane == name, high, 0.0)
                + jnp.where(lane == name + LANES // 2, note - high, 0.0)
            )
            back[b] = back[b] + dot(picks[b], d_in[at], FIRST)
    for b in range(2):
        mix_refs[b][...] = mixed[b].astype(BF16)
        back_refs[b][:, :width] = back[b].astype(BF16)
        back_refs[b][:, width:] = notes[b].astype(BF16)
    for copy in sum(stores, []):
        copy.wait()


def expert_terms_kernel(chips, *refs):
    out = refs[-1]
    count, _, _, depth, _ = out.shape
    disp, slots, grad_gate, grad_up, hidden = (
        jnp.concatenate([r[0] for r in refs[i : 5 * chips : 5]], axis=0) for i in range(5)
    )
    pairs = ((disp, grad_gate), (disp, grad_up), (slots, hidden))
    for i, (left, right) in enumerate(pairs):
        full = dot(left, right, FIRST).astype(BF16)
        for c in range(count):
            out[c, i, 0] = full[c * depth : (c + 1) * depth]


def norm_two_back_kernel(
    experts, _, back, cotangent, after, misc, gains, grad_after, grad_branch, terms
):
    width = after.shape[1]
    rows = after[...]
    scale = scale_of(rows)
    normed = rows * scale
    gain = gains[1:2, :]
    ffn_in = (normed * gain).astype(BF16)
    probs, lane = router_probs(ffn_in, misc[...], experts)
    notes = back[:, width:].astype(F32)
    notes = notes + pltpu.roll(notes, LANES // 2, 1)
    notes = jnp.where(lane < experts, notes, 0.0)
    logits = probs * (notes - jnp.sum(probs * notes, axis=-1, keepdims=True))
    high = logits.astype(BF16)
    low = (logits - high.astype(F32)).astype(BF16)
    grad_in = back[:, :width].astype(F32) + dot(high, misc[...], LAST) + dot(low, misc[...], LAST)
    grad_gain = jnp.sum(grad_in * normed, axis=0, keepdims=True)
    line = lax.broadcasted_iota(jnp.int32, (LANES, width), 0)
    terms[...] = (
        dot(ffn_in, high, FIRST)
        + dot(ffn_in, low, FIRST)
        + jnp.where(line == experts + 1, grad_gain, 0.0).T
    )
    scaled = grad_in * gain
    grad = cotangent[...].astype(F32) + scale * (
        scaled - normed * jnp.mean(scaled * normed, axis=-1, keepdims=True)
    )
    grad_after[...] = grad
    grad_branch[...] = (RESID_SCALE * grad).astype(BF16)


def attend_back_kernel(count, spans, *refs):
    pieces = refs[:count]
    pack, query, key, value, lse, cosine, sine, lin, grads, key_sum, value_sum = refs[count:]
    kv_heads, length, _ = key.shape
    heads = query.shape[0]
    w_out = pack[:, lin.shape[1] : lin.shape[1] + heads * HEAD]
    group = heads // kv_heads
    blocks = 2 * count
    size = length // blocks
    keep = diagonal(size, group)
    for j in range(count):
        rows = dot(pieces[j][...], w_out).astype(BF16)
        for h in range(2):
            at = span_rows(spans, 2 * j + h, size)
            for i in range(heads):
                grads[i, at, :] = rows[h * size : (h + 1) * size, i * HEAD : (i + 1) * HEAD]
    for g in range(kv_heads):
        key_sum[...] = jnp.zeros_like(key_sum)
        value_sum[...] = jnp.zeros_like(value_sum)
        for i in range(blocks):
            rows = slice(i * size, (i + 1) * size)
            seen = (i + 1) * size
            q = query[g * group : (g + 1) * group, rows, :].reshape(group * size, HEAD)
            grad = grads[g * group : (g + 1) * group, rows, :].reshape(group * size, HEAD)
            probs = jnp.exp(scores_of(key[g, :seen, :], q, keep, size) - lse[g, i])
            grad_probs = dot(value[g, :seen, :], grad, LAST)
            delta = jnp.sum(probs * grad_probs, axis=0, keepdims=True)
            raw = (probs * (grad_probs - delta)).astype(BF16)
            value_sum[:seen, :] += dot(probs.astype(BF16), grad)
            key_sum[:seen, :] += dot(raw, q)
            grad_query = dot(key[g, :seen, :], raw, FIRST) * ATTN_SCALE
            for r in range(group):
                turned = grad_query[:, r * size : (r + 1) * size].T
                lo = (g * group + r) * HEAD
                lin[rows, lo : lo + HEAD] = unrope(
                    turned[:, :HALF], turned[:, HALF:], cosine[rows, :], sine[rows, :]
                ).astype(BF16)
        lo = (heads + g) * HEAD
        lin[:, lo : lo + HEAD] = unrope(
            key_sum[:, :HALF], key_sum[:, HALF:], cosine[...], sine[...]
        ).astype(BF16)
        lo = (heads + kv_heads + g) * HEAD
        lin[:, lo : lo + HEAD] = value_sum[...].astype(BF16)


def input_terms_kernel(count, spans, lin, pack, *parts):
    weight = pack[:, : lin.shape[1]]
    size = lin.shape[0] // (2 * count)
    for j in range(count):
        own = jnp.concatenate([lin[span_rows(spans, 2 * j + h, size), :] for h in range(2)], axis=0)
        parts[j][...] = dot(own, weight, LAST).astype(parts[j].dtype)


def weight_terms_kernel(count, experts, spans, *refs):
    pieces = refs[:count]
    attn_in, lin, mix, pack, more, out, branch = refs[count:]
    lin_wide = lin.shape[1]
    misc_at = lin_wide + mix.shape[1]
    length, width = attn_in.shape
    size = length // (2 * count)
    for j in range(count):
        for h in range(2):
            branch[span_rows(spans, 2 * j + h, size), :] = pieces[j][h * size : (h + 1) * size, :]
    step = width // count
    lane = lax.broadcasted_iota(jnp.int32, (step, LANES), 1)
    for c in range(count):
        cut = slice(c * step, (c + 1) * step)
        attn = dot(attn_in[:, cut], lin[...], FIRST)
        outs = dot(branch[:, cut], mix[...], FIRST)
        gain = pack[cut, misc_at:].astype(F32)[:, experts : experts + 1]
        weight = pack[cut, :lin_wide].astype(F32)
        grad_gain = jnp.sum(weight * attn, axis=-1, keepdims=True) / gain
        notes = more[cut, :] + jnp.where(lane == experts, grad_gain, 0.0)
        high = notes.astype(BF16).astype(F32)
        notes = high + pltpu.roll(jnp.where(lane < LANES // 2, notes - high, 0.0), LANES // 2, 1)
        full = jnp.concatenate([attn, outs, notes], axis=1).astype(BF16)
        if len(out.shape) == 2:
            out[cut, :] = full
        else:
            each = out.shape[2]
            for f in range(out.shape[0]):
                out[f, c] = full[f * each : (f + 1) * each]


def norm_one_back_kernel(_, x, gains, grad_after, *refs):
    parts, grad_in = refs[:-1], refs[-1]
    grad = sum(p[...].astype(F32) for p in parts) * gains[0:1, :]
    rows = x[...].astype(F32)
    scale = scale_of(rows)
    normed = rows * scale
    grad_in[...] = grad_after[...] + scale * (
        grad - normed * jnp.mean(grad * normed, axis=-1, keepdims=True)
    )


def split_kernel(experts, widths, _, terms, query, key, value, out, notes):
    count = terms.shape[0]
    for s in range(count):
        lo = 0
        for ref, wide in zip((query, key, value, out), widths):
            ref[:, s * wide : (s + 1) * wide] = terms[s, :, lo : lo + wide].astype(F32)
            lo += wide
    total = sum(terms[s, :, lo:].astype(F32) for s in range(count))
    notes[...] = total + pltpu.roll(total, LANES // 2, 1)


def exchange(value, axis, offset):
    n = lax.axis_size(axis)
    return lax.ppermute(value, axis, [(i, i ^ offset) for i in range(n)])


def ring_pairs(n, hop):
    chips = n // 2
    return [(z * 2 + c, ((z + hop) % chips) * 2 + c) for z in range(chips) for c in range(2)]


def swap_pairs(n):
    return [(i, i ^ 1) for i in range(n)]


def ring_scatter(total, axis):
    n = lax.axis_size(axis)
    chips = n // 2
    move = lambda v, hop: lax.ppermute(v, axis, ring_pairs(n, hop))
    half = total[0].shape[0] // 2
    right = left = None
    if chips % 2 == 0:
        far = total[chips // 2]
        first, second = yield move(far[:half], 1), move(far[half:], -1)
    for s in range((chips - 1) // 2, 0, -1):
        up, down = total[s], total[chips - s]
        if right is not None:
            up, down = add(up, right), add(down, left)
        elif chips % 2 == 0:
            up = jnp.concatenate([add(up[:half], first), up[half:]], 0)
            down = jnp.concatenate([down[:half], add(down[half:], second)], 0)
        right, left = yield move(up, 1), move(down, -1)
    yield total[0], right, left


def add(*values):
    return sum(v.astype(F32) for v in values).astype(BF16)


def total_of(values):
    return sum(v.astype(F32) for v in values)


def slot_keys(route_rows, experts):
    hits = (route_rows[:, :, None] == jnp.arange(experts, dtype=jnp.int32)).any(axis=1)
    rows = jnp.arange(route_rows.shape[0], dtype=jnp.int32)
    earlier = (rows[None, :] < rows[:, None]).astype(BF16)
    ranks = jnp.dot(earlier, hits.astype(BF16), preferred_element_type=F32)
    keys = jnp.where(hits, ranks, -1.0).astype(BF16)
    return jnp.pad(keys, ((0, 0), (0, LANES - experts)), constant_values=-1)


def body(
    hidden_in, span_order, routes, attn_gain, query_weight, key_weight, value_weight, out_weight,
    ffn_gain, router_weight, gate_weight, up_weight, down_weight, cotangent
):
    ctx, fsdp = lax.axis_size("ctx"), lax.axis_size("fsdp")
    me_ctx, me_fsdp = lax.axis_index("ctx"), lax.axis_index("fsdp")
    x = hidden_in[0]
    count, width = x.shape
    length = ctx * count
    heads = query_weight.shape[1] // HEAD // ctx
    kv_heads = key_weight.shape[1] // HEAD // ctx
    experts = router_weight.shape[1]
    local, _, units = gate_weight.shape
    cap = count * routes.shape[2] * 5 // (4 * experts)
    q_wide, kv_wide = heads * HEAD, kv_heads * HEAD
    lin_wide = q_wide + 2 * kv_wide
    chips = fsdp // 2
    no_scalars = jnp.zeros((1,), jnp.int32)

    own = lambda w, wide: lax.dynamic_slice_in_dim(w, me_ctx * wide, wide, 1)
    pack = jnp.concatenate(
        [
            own(query_weight, q_wide),
            own(key_weight, kv_wide),
            own(value_weight, kv_wide),
            own(out_weight, q_wide),
            router_weight,
            attn_gain[:, None],
            ffn_gain[:, None],
            jnp.zeros((attn_gain.shape[0], LANES - experts - 2), BF16),
        ],
        axis=1,
    )
    pack = lax.all_gather(pack, "fsdp", axis=0, tiled=True)
    pieces = [x] + [exchange(x, "ctx", j) for j in range(1, ctx)]
    owners = jnp.stack([me_ctx ^ j for j in range(ctx)])
    spans = span_order.reshape(ctx, 2)[owners].reshape(-1)
    keys = slot_keys(routes[0], experts)
    grad_pack = lax.all_gather(
        jnp.concatenate([cotangent[0], keys], axis=1), "fsdp", axis=0, tiled=True
    )
    frequencies = ROPE_THETA ** (-2.0 * jnp.arange(HALF, dtype=F32) / HEAD)
    angles = jnp.arange(length, dtype=F32)[:, None] * frequencies[None, :]
    cosine, sine = jnp.cos(angles), jnp.sin(angles)

    attn_in, query, key, value, misc, gains = call(
        functools.partial(project_kernel, ctx, heads, kv_heads, experts),
        [
            shape((length, width), BF16),
            shape((heads, length, HEAD), BF16),
            shape((kv_heads, length, HEAD), BF16),
            shape((kv_heads, length, HEAD), BF16),
            shape((width, LANES), BF16),
            shape((2, width), F32),
        ],
        [spans, *pieces, pack, cosine, sine],
        flops=2 * length * width * lin_wide,
    )
    part_types = [shape((count, width), F32 if j == 0 else BF16) for j in range(ctx)]
    mix, lse, *parts = call(
        functools.partial(attend_kernel, ctx),
        [
            shape((length, q_wide), BF16),
            shape((kv_heads, 2 * ctx, 1, heads // kv_heads * length // (2 * ctx)), F32),
            *part_types,
        ],
        [spans, query, key, value, pack],
        flops=8 * length * length * q_wide,
    )
    parts = [parts[0]] + [exchange(parts[j], "ctx", j) for j in range(1, ctx)]
    after, ffn_in = call(
        norm_two_kernel,
        [shape((count, width), F32), shape((count, width), BF16)],
        [no_scalars, x, gains, *parts],
    )
    place = me_fsdp % 2
    wides = (width, width, units, units, units)
    anywhere = pl.BlockSpec(memory_space=pl.ANY)

    move = lambda v, hop: lax.ppermute(v, "fsdp", ring_pairs(fsdp, hop))
    swap = lambda v: lax.ppermute(v, "fsdp", swap_pairs(fsdp))

    def run_experts(offset, *same):
        rows = [*same, *map(swap, same)]
        chip = (me_fsdp // 2 + offset) % chips * 2
        outs = pl.pallas_call(
            functools.partial(experts_kernel, experts, cap, len(rows) // 2),
            out_shape=[
                *[shape((count, width), BF16)] * 2,
                *[shape((count, width + LANES), BF16)] * 2,
                *[shape((local, 2 * cap, w), BF16) for w in wides],
            ],
            in_specs=[SMEM, *[VMEM] * len(rows), *[anywhere] * 4, VMEM],
            out_specs=[VMEM] * 4 + [anywhere] * 5,
            scratch_shapes=[
                pltpu.VMEM((2, LANES, count), F32),
                pltpu.VMEM((2, count, width + LANES), BF16),
                *[pltpu.VMEM((local, width, units), BF16)] * 3,
                *[pltpu.VMEM((local, 2 * cap, w), BF16) for w in wides],
                pltpu.SemaphoreType.DMA((2 + 8 * local,)),
            ],
            compiler_params=params(),
            cost_estimate=pl.CostEstimate(
                flops=32 * local * cap * width * units,
                bytes_accessed=20 * 2**20,
                transcendentals=0,
            ),
        )(
            jnp.stack([me_fsdp, chip + place, chip + 1 - place]),
            *rows, grad_pack, gate_weight, up_weight, down_weight, misc,
        )
        return outs[0:2], outs[2:4], outs[4:]

    ran, ready = {}, [(0, ffn_in)]
    right = left = ffn_in
    for s in range(1, (chips + 1) // 2):
        right, left = move(right, 1), move(left, -1)
        for offset, rows in ready:
            ran[offset] = run_experts(offset, rows)
        right, left, ran = lax.optimization_barrier((right, left, ran))
        ready = [(chips - s, right), (s, left)]
    if chips % 2 == 0:
        first, second = move(right[: count // 2], 1), move(left[count // 2 :], -1)
        for offset, rows in ready[:-1]:
            ran[offset] = run_experts(offset, rows)
        first, second, ran = lax.optimization_barrier((first, second, ran))
        ran[chips // 2] = run_experts(chips // 2, first, second)
        far = add(ran[chips // 2][1][0], swap(ran[chips // 2][1][1]))
        first, second = move(far[: count // 2], 1), move(far[count // 2 :], -1)
        ready = ready[-1:]
    for offset, rows in ready:
        ran[offset] = run_experts(offset, rows)
    first, second, ran = lax.optimization_barrier((first, second, ran))
    turns = range(chips)

    depth = width // ctx
    slots = fsdp * cap
    saved = [v for r in turns for v in ran[r][2]]
    step = math.lcm(depth, LANES)
    tall = pl.BlockSpec((1, 2 * cap, step), lambda e, c: (e, 0, c))
    thin = pl.BlockSpec((1, 2 * cap, units), lambda e, c: (e, 0, 0))
    expert_terms = pl.pallas_call(
        functools.partial(expert_terms_kernel, chips),
        out_shape=shape((ctx, 3, local, depth, units), BF16),
        grid=(local, width // step),
        in_specs=[tall, tall, thin, thin, thin] * chips,
        out_specs=pl.BlockSpec((step // depth, 3, 1, depth, units), lambda e, c: (c, 0, e, 0, 0)),
        compiler_params=params(),
        cost_estimate=pl.CostEstimate(
            flops=6 * local * slots * width * units, bytes_accessed=40 * 2**20, transcendentals=0
        ),
    )(*saved)
    backs = {r: add(ran[r][1][0], swap(ran[r][1][1])) for r in turns if 2 * r != chips}
    right = left = None
    half = count // 2
    for s in range((chips - 1) // 2, 0, -1):
        up, down = backs[s], backs[chips - s]
        if right is not None:
            up, down = add(up, right), add(down, left)
        elif chips % 2 == 0:
            up = jnp.concatenate([add(up[:half], first), up[half:]], 0)
            down = jnp.concatenate([down[:half], add(down[half:], second)], 0)
        right, left = move(up, 1), move(down, -1)
    right, left, expert_terms = lax.optimization_barrier((right, left, expert_terms))
    back = total_of((backs[0], right, left))
    mixes = {r: add(ran[r][0][0], swap(ran[r][0][1])) for r in turns}
    mixes, back = lax.optimization_barrier((mixes, back))
    mix_steps = ring_scatter(mixes, "fsdp")
    moving = next(mix_steps)
    expert_sums = lax.psum_scatter(
        expert_terms.reshape(-1, units), "ctx", scatter_dimension=0, tiled=True
    ).reshape(3, local, depth, units)

    grad_after, grad_branch, more = call(
        functools.partial(norm_two_back_kernel, experts),
        [shape((count, width), F32), shape((count, width), BF16), shape((width, LANES), F32)],
        [no_scalars, back, cotangent[0], after, misc, gains],
    )
    branches = [grad_branch] + [exchange(grad_branch, "ctx", j) for j in range(1, ctx)]
    branches, moving = lax.optimization_barrier((branches, moving))
    moving = mix_steps.send(moving)
    [lin] = call(
        functools.partial(attend_back_kernel, ctx),
        [shape((length, lin_wide), BF16)],
        [spans, *branches, pack, query, key, value, lse, cosine, sine],
        scratch=[
            pltpu.VMEM((heads, length, HEAD), BF16),
            pltpu.VMEM((length, HEAD), F32),
            pltpu.VMEM((length, HEAD), F32),
        ],
        flops=20 * length * length * q_wide,
    )
    for _ in range((chips - 1) // 2):
        lin, moving = lax.optimization_barrier((lin, moving))
        moving = mix_steps.send(moving)
    hidden_out = (after + RESID_SCALE * total_of(moving)).astype(BF16)[None]
    in_parts = call(
        functools.partial(input_terms_kernel, ctx),
        part_types,
        [spans, lin, pack],
        flops=2 * length * width * lin_wide,
    )
    in_parts = [in_parts[0]] + [exchange(in_parts[j], "ctx", j) for j in range(1, ctx)]
    total_wide = lin_wide + q_wide + LANES
    each = width // (ctx * fsdp)
    direct = each % 16 == 0
    [terms] = call(
        functools.partial(weight_terms_kernel, ctx, experts),
        [shape((fsdp, ctx, each, total_wide) if direct else (width, total_wide), BF16)],
        [spans, *branches, attn_in, lin, mix, pack, more],
        scratch=[pltpu.VMEM((length, width), BF16)],
        flops=2 * length * width * (lin_wide + q_wide),
    )
    if not direct:
        terms = terms.reshape(ctx, fsdp, each, total_wide).swapaxes(0, 1)
    terms, expert_sums = lax.optimization_barrier((terms, expert_sums))
    grad_gate, grad_up, grad_down = (expert_sums[i].astype(F32) for i in range(3))
    terms = lax.psum_scatter(terms, "fsdp", scatter_dimension=0, tiled=True)[0]
    terms = lax.all_to_all(terms, "ctx", split_axis=0, concat_axis=0, tiled=True)
    grad_query, grad_key, grad_value, grad_out, notes = call(
        functools.partial(split_kernel, experts, (q_wide, kv_wide, kv_wide, q_wide)),
        [
            *[shape((each, ctx * w), F32) for w in (q_wide, kv_wide, kv_wide, q_wide)],
            shape((each, LANES), F32),
        ],
        [no_scalars, terms],
    )
    [grad_in] = call(
        norm_one_back_kernel,
        [shape((count, width), F32)],
        [no_scalars, x, gains, grad_after, *in_parts],
    )
    return (
        hidden_out,
        grad_in[None],
        notes[:, experts],
        grad_query,
        grad_key,
        grad_value,
        grad_out,
        notes[:, experts + 1],
        notes[:, :experts],
        grad_gate,
        grad_up,
        grad_down,
    )


def solution(mesh):
    rows, both = P("fsdp", "ctx", None), ("ctx", "fsdp")
    split = P("fsdp", None)
    return jax.shard_map(
        body,
        mesh=mesh,
        in_specs=(
            rows, P(), rows, P("fsdp"), split, split, split, split, P("fsdp"), split,
            P("fsdp", None, None), P("fsdp", None, None), P("fsdp", None, None), rows,
        ),
        out_specs=(
            rows, rows, P(both), P(both, None), P(both, None), P(both, None), P(both, None),
            P(both), P(both, None), rows, rows, rows,
        ),
        check_vma=False,
    )
```

```python
import functools
import math

import jax
import jax.numpy as jnp
from jax import lax
from jax.experimental import pallas as pl
from jax.experimental.pallas import tpu as pltpu
from jax.sharding import PartitionSpec as P

HEAD = 64
HALF = HEAD // 2
NORM_EPS = 1e-06
ATTN_SCALE = 0.015625
RESID_SCALE = 0.22
ROPE_THETA = 10000.0
MASKED_SCORE = -1e30
LANES = 128
LAST = (((1,), (1,)), ((), ()))
FIRST = (((0,), (0,)), ((), ()))
F32 = jnp.float32
BF16 = jnp.bfloat16
VMEM = pl.BlockSpec(memory_space=pltpu.VMEM)
SMEM = pl.BlockSpec(memory_space=pltpu.SMEM)


def params(mib=60, **kw):
    return pltpu.CompilerParams(vmem_limit_bytes=mib * 2**20, **kw)


def call(kernel, outs, ins, scratch=(), flops=0, mib=24):
    size = lambda v: v.size * v.dtype.itemsize
    return pl.pallas_call(
        kernel,
        out_shape=outs,
        in_specs=[SMEM] + [VMEM] * (len(ins) - 1),
        out_specs=[VMEM] * len(outs),
        scratch_shapes=list(scratch),
        compiler_params=params(mib),
        cost_estimate=pl.CostEstimate(
            flops=flops, bytes_accessed=sum(map(size, list(ins) + list(outs))), transcendentals=0
        ),
    )(*ins)


def shape(dims, dtype):
    return jax.ShapeDtypeStruct(tuple(dims), dtype)


def dot(a, b, dims=(((1,), (0,)), ((), ()))):
    return lax.dot_general(a, b, dims, preferred_element_type=F32)


def scale_of(x):
    return lax.rsqrt(jnp.mean(x * x, axis=-1, keepdims=True) + NORM_EPS)


def span_rows(spans, index, size):
    return pl.ds(pl.multiple_of(spans[index] * size, size), size)


def rope(front, back, cosine, sine):
    return jnp.concatenate([front * cosine - back * sine, back * cosine + front * sine], axis=-1)


def unrope(front, back, cosine, sine):
    return jnp.concatenate([front * cosine + back * sine, back * cosine - front * sine], axis=-1)


def project_kernel(count, heads, kv_heads, experts, spans, *refs):
    pieces = refs[:count]
    pack, cosine, sine, attn_in, query, key, value, router, gains = refs[count:]
    lin_wide = (heads + 2 * kv_heads) * HEAD
    router[...] = pack[:, lin_wide + heads * HEAD :]
    turned = router[...].astype(F32).T
    gains[...] = turned[experts : experts + 2, :]
    gain = turned[experts : experts + 1, :]
    size = pieces[0].shape[0] // 2
    for j in range(count):
        x = pieces[j][...].astype(F32)
        rows_in = (x * scale_of(x) * gain).astype(BF16)
        lin = dot(rows_in, pack[:, :lin_wide])
        for h in range(2):
            at = span_rows(spans, 2 * j + h, size)
            cut = slice(h * size, (h + 1) * size)
            attn_in[at, :] = rows_in[cut]
            cos, sin = cosine[at, :], sine[at, :]
            for i in range(heads + kv_heads):
                lo = i * HEAD
                turned = rope(lin[cut, lo : lo + HALF], lin[cut, lo + HALF : lo + HEAD], cos, sin)
                if i < heads:
                    query[i, at, :] = (turned * ATTN_SCALE).astype(BF16)
                else:
                    key[i - heads, at, :] = turned.astype(BF16)
            for i in range(kv_heads):
                lo = (heads + kv_heads + i) * HEAD
                value[i, at, :] = lin[cut, lo : lo + HEAD].astype(BF16)


def diagonal(size, group):
    keys = lax.broadcasted_iota(jnp.int32, (size, group * size), 0)
    queries = lax.broadcasted_iota(jnp.int32, (size, group * size), 1) % size
    return keys <= queries


def scores_of(key_rows, query_rows, keep, size):
    raw = dot(key_rows, query_rows, LAST)
    seen = raw.shape[0] - size
    last = jnp.where(keep, raw[seen:], MASKED_SCORE)
    return last if seen == 0 else jnp.concatenate([raw[:seen], last], axis=0)


def attend_kernel(count, spans, query, key, value, pack, mix, lse, *refs):
    parts, rows_of = refs[:-1], refs[-1]
    kv_heads, length, _ = key.shape
    heads = query.shape[0]
    lo = (heads + 2 * kv_heads) * HEAD
    w_out = pack[:, lo : lo + mix.shape[1]]
    group = heads // kv_heads
    blocks = 2 * count
    size = length // blocks
    keep = diagonal(size, group)

    def one_group(g, _):
        for i in range(blocks):
            rows = slice(i * size, (i + 1) * size)
            seen = (i + 1) * size
            q = query[pl.ds(g * group, group), rows, :].reshape(group * size, HEAD)
            scores = scores_of(key[g, :seen, :], q, keep, size)
            top = jnp.max(scores, axis=0, keepdims=True)
            grown = jnp.exp(scores - top)
            total = jnp.sum(grown, axis=0, keepdims=True)
            mixed = dot(value[g, :seen, :], grown.astype(BF16), FIRST) / total
            lse[g, i, :, :] = top + jnp.log(total)
            for r in range(group):
                turned = mixed[:, r * size : (r + 1) * size].T
                rows_of[g * group + r, rows, :] = turned.astype(BF16)
        return 0

    lax.fori_loop(0, kv_heads, one_group, 0)
    for i in range(heads):
        mix[:, i * HEAD : (i + 1) * HEAD] = rows_of[i]
    for j in range(count):
        own = jnp.concatenate([mix[span_rows(spans, 2 * j + h, size), :] for h in range(2)], axis=0)
        parts[j][...] = dot(own, w_out, LAST).astype(parts[j].dtype)


def norm_two_kernel(_, x, gains, *refs):
    parts, (after, upper, lower) = refs[:-3], refs[-3:]
    branch = sum(p[...].astype(F32) for p in parts)
    rows = x[...].astype(F32) + RESID_SCALE * branch
    after[...] = rows
    ffn_in = (rows * scale_of(rows) * gains[1:2, :]).astype(BF16)
    half = upper.shape[0]
    upper[...], lower[...] = ffn_in[:half], ffn_in[half:]


def router_probs(rows, router, experts):
    logits = dot(rows, router)
    lane = lax.broadcasted_iota(jnp.int32, logits.shape, 1)
    logits = jnp.where(lane < experts, logits, MASKED_SCORE)
    grown = jnp.exp(logits - jnp.max(logits, axis=-1, keepdims=True))
    return grown / jnp.sum(grown, axis=-1, keepdims=True), lane


def experts_kernel(experts, cap, splits, where, *refs):
    row_refs = refs[: 2 * splits]
    grad_all, *weights, misc = refs[2 * splits : 2 * splits + 5]
    mix_refs, back_refs, saved = refs[2 * splits + 5 :][:2], refs[2 * splits + 7 :][:2], refs[2 * splits + 9 :][:5]
    keys, chances, grad_in, *held = refs[2 * splits + 14 :]
    kept, held, sems = held[3:8], held[:3], held[8]
    local, width, _ = weights[0].shape
    count = grad_in.shape[1]
    loads = [
        pltpu.make_async_copy(
            grad_all.at[pl.ds(pl.multiple_of(where[1 + b] * count, count), count), :],
            grad_in.at[b],
            sems.at[b],
        )
        for b in range(2)
    ]
    pulls = [
        [
            pltpu.make_async_copy(weights[i].at[e], held[i].at[e], sems.at[2 + 3 * e + i])
            for i in range(3)
        ]
        for e in range(local)
    ]
    stores = [
        [
            pltpu.make_async_copy(
                kept[i].at[e], saved[i].at[e], sems.at[2 + 3 * local + 5 * e + i]
            )
            for i in range(5)
        ]
        for e in range(local)
    ]
    for copy in loads + sum(pulls, []):
        copy.start()
    rows = [
        jnp.concatenate([r[...] for r in row_refs[b * splits : (b + 1) * splits]], axis=0)
        for b in range(2)
    ]
    for b in range(2):
        chances[b] = router_probs(rows[b], misc[...], experts)[0].T
    for copy in loads:
        copy.wait()
    slot = lax.broadcasted_iota(jnp.int32, (cap, count), 0).astype(F32)
    lane = lax.broadcasted_iota(jnp.int32, (2 * cap, LANES), 1)
    names = [where[0] * local + e for e in range(local)]
    picks, share, mine, raw = [], [], [], []
    for b in range(2):
        keys[b] = grad_in[b, :, width:].astype(F32).T
        hits = [slot == keys[b, pl.ds(name, 1), :] for name in names]
        share.append(
            [
                jnp.sum(
                    jnp.where(hit, chances[b, pl.ds(name, 1), :], 0.0), axis=-1, keepdims=True
                )
                for hit, name in zip(hits, names)
            ]
        )
        picks.append(jnp.concatenate([hit.astype(BF16) for hit in hits], axis=0))
        mine.append(dot(picks[b], rows[b]).astype(BF16))
        raw.append(dot(picks[b], grad_in[b, :, :width]))
    both = lambda parts, e: jnp.concatenate([p[e * cap : (e + 1) * cap] for p in parts], axis=0)
    w_gate, w_up, w_down = held
    outs, backs, notes = [], [], []
    for e in range(local):
        weight = jnp.concatenate([share[b][e] for b in range(2)], axis=0)
        taken = both(mine, e)
        grad = both(raw, e) * RESID_SCALE
        grads = (grad * weight).astype(BF16)
        for copy in pulls[e]:
            copy.wait()
        gate, up = dot(taken, w_gate[e]), dot(taken, w_up[e])
        sigmoid = 1.0 / (1.0 + jnp.exp(-gate))
        silu = gate * sigmoid
        hidden = (silu * up).astype(BF16)
        out = dot(hidden, w_down[e], LAST).astype(BF16).astype(F32)
        grad_hidden = dot(grads, w_down[e])
        d_gate = (grad_hidden * up * sigmoid * (1.0 + gate * (1.0 - sigmoid))).astype(BF16)
        d_up = (grad_hidden * silu).astype(BF16)
        for i, term in enumerate((taken, grads, d_gate, d_up, hidden)):
            kept[i][e] = term
            stores[e][i].start()
        outs.append((out * weight).astype(BF16))
        backs.append((dot(d_gate, w_gate[e], LAST) + dot(d_up, w_up[e], LAST)).astype(BF16))
        note = jnp.sum(grad * out, axis=-1, keepdims=True)
        high = note.astype(BF16).astype(F32)
        notes.append(
            jnp.where(
                lane == names[e], high, jnp.where(lane == names[e] + LANES // 2, note - high, 0.0)
            ).astype(BF16)
        )
    for b in range(2):
        home = lambda parts: dot(
            picks[b],
            jnp.concatenate([p[b * cap : (b + 1) * cap] for p in parts], axis=0),
            FIRST,
        ).astype(BF16)
        mix_refs[b][...] = home(outs)
        back_refs[b][:, :width] = home(backs)
        back_refs[b][:, width:] = home(notes)
    for copy in sum(stores, []):
        copy.wait()


def expert_terms_kernel(chips, *refs):
    out = refs[-1]
    count, _, _, depth, _ = out.shape
    disp, slots, grad_gate, grad_up, hidden = (
        jnp.concatenate([r[0] for r in refs[i : 5 * chips : 5]], axis=0) for i in range(5)
    )
    pairs = ((disp, grad_gate), (disp, grad_up), (slots, hidden))
    for i, (left, right) in enumerate(pairs):
        full = dot(left, right, FIRST).astype(BF16)
        for c in range(count):
            out[c, i, 0] = full[c * depth : (c + 1) * depth]


def norm_two_back_kernel(
    experts, full, tops, _, cotangent, after, misc, gains, *refs
):
    *parts, grad_after, grad_branch, terms = refs
    width = after.shape[1]
    back = total_of([p[...] for p in parts[:full]])
    if tops:
        halves = parts[full : full + tops], parts[full + tops :]
        back = back + jnp.concatenate([total_of([p[...] for p in h]) for h in halves], axis=0)
    rows = after[...]
    scale = scale_of(rows)
    normed = rows * scale
    gain = gains[1:2, :]
    ffn_in = (normed * gain).astype(BF16)
    probs, lane = router_probs(ffn_in, misc[...], experts)
    notes = back[:, width:]
    notes = notes + pltpu.roll(notes, LANES // 2, 1)
    notes = jnp.where(lane < experts, notes, 0.0)
    logits = probs * (notes - jnp.sum(probs * notes, axis=-1, keepdims=True))
    high = logits.astype(BF16)
    low = (logits - high.astype(F32)).astype(BF16)
    grad_in = back[:, :width] + dot(high, misc[...], LAST) + dot(low, misc[...], LAST)
    grad_gain = jnp.sum(grad_in * normed, axis=0, keepdims=True)
    line = lax.broadcasted_iota(jnp.int32, (LANES, width), 0)
    terms[...] = (
        dot(ffn_in, high, FIRST)
        + dot(ffn_in, low, FIRST)
        + jnp.where(line == experts + 1, grad_gain, 0.0).T
    )
    scaled = grad_in * gain
    grad = cotangent[...].astype(F32) + scale * (
        scaled - normed * jnp.mean(scaled * normed, axis=-1, keepdims=True)
    )
    grad_after[...] = grad
    grad_branch[...] = (RESID_SCALE * grad).astype(BF16)


def pieces_of(splits, refs):
    pieces = []
    for n in splits:
        pieces.append(jnp.concatenate([r[...] for r in refs[:n]], axis=0))
        refs = refs[n:]
    return pieces, refs


def attend_back_kernel(splits, spans, *refs):
    count = len(splits)
    pieces, refs = pieces_of(splits, refs)
    pack, query, key, value, lse, cosine, sine, lin, grads, turned_of, key_sum, value_sum = refs
    kv_heads, length, _ = key.shape
    heads = query.shape[0]
    w_out = pack[:, lin.shape[1] : lin.shape[1] + heads * HEAD]
    group = heads // kv_heads
    blocks = 2 * count
    size = length // blocks
    keep = diagonal(size, group)
    for j in range(count):
        rows = dot(pieces[j], w_out).astype(BF16)
        for h in range(2):
            at = span_rows(spans, 2 * j + h, size)
            for i in range(heads):
                grads[i, at, :] = rows[h * size : (h + 1) * size, i * HEAD : (i + 1) * HEAD]

    def one_group(g, _):
        key_sum[...] = jnp.zeros_like(key_sum)
        value_sum[...] = jnp.zeros_like(value_sum)
        for i in range(blocks):
            rows = slice(i * size, (i + 1) * size)
            seen = (i + 1) * size
            q = query[pl.ds(g * group, group), rows, :].reshape(group * size, HEAD)
            grad = grads[pl.ds(g * group, group), rows, :].reshape(group * size, HEAD)
            probs = jnp.exp(scores_of(key[g, :seen, :], q, keep, size) - lse[g, i])
            grad_probs = dot(value[g, :seen, :], grad, LAST)
            delta = jnp.sum(probs * grad_probs, axis=0, keepdims=True)
            raw = (probs * (grad_probs - delta)).astype(BF16)
            value_sum[:seen, :] += dot(probs.astype(BF16), grad)
            key_sum[:seen, :] += dot(raw, q)
            grad_query = dot(key[g, :seen, :], raw, FIRST) * ATTN_SCALE
            for r in range(group):
                turned = grad_query[:, r * size : (r + 1) * size].T
                turned_of[g * group + r, rows, :] = unrope(
                    turned[:, :HALF], turned[:, HALF:], cosine[rows, :], sine[rows, :]
                ).astype(BF16)
        turned_of[heads + g] = unrope(
            key_sum[:, :HALF], key_sum[:, HALF:], cosine[...], sine[...]
        ).astype(BF16)
        turned_of[heads + kv_heads + g] = value_sum[...].astype(BF16)
        return 0

    lax.fori_loop(0, kv_heads, one_group, 0)
    for i in range(heads + 2 * kv_heads):
        lin[:, i * HEAD : (i + 1) * HEAD] = turned_of[i]


def input_terms_kernel(count, spans, lin, pack, *parts):
    weight = pack[:, : lin.shape[1]]
    size = lin.shape[0] // (2 * count)
    for j in range(count):
        own = jnp.concatenate([lin[span_rows(spans, 2 * j + h, size), :] for h in range(2)], axis=0)
        parts[j][...] = dot(own, weight, LAST).astype(parts[j].dtype)


def noted(notes):
    lane = lax.broadcasted_iota(jnp.int32, notes.shape, 1)
    high = notes.astype(BF16).astype(F32)
    return high + pltpu.roll(jnp.where(lane < LANES // 2, notes - high, 0.0), LANES // 2, 1)


def store_terms(where, out, c, full):
    if len(out.shape) == 2:
        out[c * full.shape[0] : (c + 1) * full.shape[0], :] = full
    else:
        chips, each = out.shape[1], out.shape[3]
        for f in range(2 * chips):
            offset = (f // 2 - where[1] + chips) % chips
            out[(f + where[2]) % 2, offset, c] = full[f * each : (f + 1) * each]


def weight_terms_kernel(splits, experts, spans, *refs):
    count = len(splits)
    where = [spans[2 * count + i] for i in range(3)]
    pieces, refs = pieces_of(splits, refs)
    attn_in, lin, mix, pack, more, out, branch = refs
    length, width = attn_in.shape
    lin_wide = lin.shape[1]
    size = length // (2 * count)
    for j in range(count):
        for h in range(2):
            branch[span_rows(spans, 2 * j + h, size), :] = pieces[j][h * size : (h + 1) * size, :]
    step = width // count
    lane = lax.broadcasted_iota(jnp.int32, (step, LANES), 1)
    for c in range(count):
        cut = slice(c * step, (c + 1) * step)
        attn = dot(attn_in[:, cut], lin[...], FIRST)
        outs = dot(branch[:, cut], mix[...], FIRST)
        gain = pack[cut, pack.shape[1] - LANES :].astype(F32)[:, experts : experts + 1]
        weight = pack[cut, :lin_wide].astype(F32)
        grad_gain = jnp.sum(weight * attn, axis=-1, keepdims=True) / gain
        notes = noted(more[cut, :] + jnp.where(lane == experts, grad_gain, 0.0))
        store_terms(where, out, c, jnp.concatenate([attn, outs, notes], axis=1).astype(BF16))


def norm_one_back_kernel(_, x, gains, grad_after, *refs):
    parts, grad_in = refs[:-1], refs[-1]
    grad = sum(p[...].astype(F32) for p in parts) * gains[0:1, :]
    rows = x[...].astype(F32)
    scale = scale_of(rows)
    normed = rows * scale
    grad_in[...] = grad_after[...] + scale * (
        grad - normed * jnp.mean(grad * normed, axis=-1, keepdims=True)
    )


def split_kernel(widths, _, terms, *refs):
    count = terms.shape[0]
    total = 0.0
    for s in range(count):
        lo, at = 0, 0
        for wide in widths:
            part = terms[s, :, lo : lo + (wide or LANES)].astype(F32)
            lo += wide or LANES
            if wide:
                refs[at][:, s * wide : (s + 1) * wide] = part
                at += 1
            else:
                total = total + part
    refs[-1][...] = total + pltpu.roll(total, LANES // 2, 1)


def exchange(value, axis, offset):
    n = lax.axis_size(axis)
    return lax.ppermute(value, axis, [(i, i ^ offset) for i in range(n)])


def ring_pairs(n, hop):
    chips = n // 2
    return [(z * 2 + c, ((z + hop) % chips) * 2 + c) for z in range(chips) for c in range(2)]


def swap_pairs(n):
    return [(i, i ^ 1) for i in range(n)]


def ring_scatter(total, axis):
    n = lax.axis_size(axis)
    chips = n // 2
    move = lambda v, hop: lax.ppermute(v, axis, ring_pairs(n, hop))
    half = total[0].shape[0] // 2
    right = left = None
    if chips % 2 == 0:
        far = total[chips // 2]
        first, second = yield move(far[:half], 1), move(far[half:], -1)
    for s in range((chips - 1) // 2, 0, -1):
        up, down = total[s], total[chips - s]
        if right is not None:
            up, down = add(up, right), add(down, left)
        elif chips % 2 == 0:
            up = jnp.concatenate([add(up[:half], first), up[half:]], 0)
            down = jnp.concatenate([down[:half], add(down[half:], second)], 0)
        right, left = yield move(up, 1), move(down, -1)
    yield total[0], right, left


def add(*values):
    return sum(v.astype(F32) for v in values).astype(BF16)


def total_of(values):
    return sum(v.astype(F32) for v in values)


def slot_keys(route_rows, experts):
    hits = (route_rows[:, :, None] == jnp.arange(experts, dtype=jnp.int32)).any(axis=1)
    rows = jnp.arange(route_rows.shape[0], dtype=jnp.int32)
    earlier = (rows[None, :] < rows[:, None]).astype(BF16)
    ranks = jnp.dot(earlier, hits.astype(BF16), preferred_element_type=F32)
    keys = jnp.where(hits, ranks, -1.0).astype(BF16)
    return jnp.pad(keys, ((0, 0), (0, LANES - experts)), constant_values=-1)


def body(
    hidden_in, span_order, routes, attn_gain, query_weight, key_weight, value_weight, out_weight,
    ffn_gain, router_weight, gate_weight, up_weight, down_weight, cotangent
):
    ctx, fsdp = lax.axis_size("ctx"), lax.axis_size("fsdp")
    me_ctx, me_fsdp = lax.axis_index("ctx"), lax.axis_index("fsdp")
    x = hidden_in[0]
    count, width = x.shape
    length = ctx * count
    heads = query_weight.shape[1] // HEAD // ctx
    kv_heads = key_weight.shape[1] // HEAD // ctx
    experts = router_weight.shape[1]
    local, _, units = gate_weight.shape
    cap = count * routes.shape[2] * 5 // (4 * experts)
    q_wide, kv_wide = heads * HEAD, kv_heads * HEAD
    lin_wide = q_wide + 2 * kv_wide
    chips = fsdp // 2
    no_scalars = jnp.zeros((1,), jnp.int32)

    own = lambda w, wide: lax.dynamic_slice_in_dim(w, me_ctx * wide, wide, 1)
    pack = jnp.concatenate(
        [
            own(query_weight, q_wide),
            own(key_weight, kv_wide),
            own(value_weight, kv_wide),
            own(out_weight, q_wide),
            router_weight,
            attn_gain[:, None],
            ffn_gain[:, None],
            jnp.zeros((attn_gain.shape[0], LANES - experts - 2), BF16),
        ],
        axis=1,
    )
    pack = lax.all_gather(pack, "fsdp", axis=0, tiled=True)
    pieces = [x] + [exchange(x, "ctx", j) for j in range(1, ctx)]
    owners = jnp.stack([me_ctx ^ j for j in range(ctx)])
    spans = span_order.reshape(ctx, 2)[owners].reshape(-1)
    keys = slot_keys(routes[0], experts)
    grad_pack = lax.all_gather(
        jnp.concatenate([cotangent[0], keys], axis=1), "fsdp", axis=0, tiled=True
    )
    frequencies = ROPE_THETA ** (-2.0 * jnp.arange(HALF, dtype=F32) / HEAD)
    angles = jnp.arange(length, dtype=F32)[:, None] * frequencies[None, :]
    cosine, sine = jnp.cos(angles), jnp.sin(angles)

    attn_in, query, key, value, misc, gains = call(
        functools.partial(project_kernel, ctx, heads, kv_heads, experts),
        [
            shape((length, width), BF16),
            shape((heads, length, HEAD), BF16),
            shape((kv_heads, length, HEAD), BF16),
            shape((kv_heads, length, HEAD), BF16),
            shape((width, LANES), BF16),
            shape((2, width), F32),
        ],
        [spans, *pieces, pack, cosine, sine],
        flops=2 * length * width * lin_wide,
        mib=60,
    )
    part_types = [shape((count, width), F32 if j == 0 else BF16) for j in range(ctx)]
    mix, lse, *parts = call(
        functools.partial(attend_kernel, ctx),
        [
            shape((length, q_wide), BF16),
            shape((kv_heads, 2 * ctx, 1, heads // kv_heads * length // (2 * ctx)), F32),
            *part_types,
        ],
        [spans, query, key, value, pack],
        scratch=[pltpu.VMEM((heads, length, HEAD), BF16)],
        flops=8 * length * length * q_wide,
        mib=60,
    )
    parts = [parts[0]] + [exchange(parts[j], "ctx", j) for j in range(1, ctx)]
    half = count // 2
    after, upper, lower = call(
        norm_two_kernel,
        [shape((count, width), F32), *[shape((half, width), BF16)] * 2],
        [no_scalars, x, gains, *parts],
    )
    place = me_fsdp % 2
    wides = (width, width, units, units, units)
    anywhere = pl.BlockSpec(memory_space=pl.ANY)

    move = lambda v, hop: lax.ppermute(v, "fsdp", ring_pairs(fsdp, hop))
    swap = lambda v: lax.ppermute(v, "fsdp", swap_pairs(fsdp))

    def run_experts(offset, same, other):
        rows = [*same, *other]
        chip = (me_fsdp // 2 + offset) % chips * 2
        outs = pl.pallas_call(
            functools.partial(experts_kernel, experts, cap, len(rows) // 2),
            out_shape=[
                *[shape((count, width), BF16)] * 2,
                *[shape((count, width + LANES), BF16)] * 2,
                *[shape((local, 2 * cap, w), BF16) for w in wides],
            ],
            in_specs=[SMEM, *[VMEM] * len(rows), *[anywhere] * 4, VMEM],
            out_specs=[VMEM] * 4 + [anywhere] * 5,
            scratch_shapes=[
                pltpu.VMEM((2, LANES, count), F32),
                pltpu.VMEM((2, LANES, count), F32),
                pltpu.VMEM((2, count, width + LANES), BF16),
                *[pltpu.VMEM((local, width, units), BF16)] * 3,
                *[pltpu.VMEM((local, 2 * cap, w), BF16) for w in wides],
                pltpu.SemaphoreType.DMA((2 + 8 * local,)),
            ],
            compiler_params=params(60),
            cost_estimate=pl.CostEstimate(
                flops=32 * local * cap * width * units,
                bytes_accessed=20 * 2**20,
                transcendentals=0,
            ),
        )(
            jnp.stack([me_fsdp, chip + place, chip + 1 - place]),
            *rows, grad_pack, gate_weight, up_weight, down_weight, misc,
        )
        return outs[0:2], outs[2:4], outs[4:]

    swaps = lambda *values: [swap(v) for v in values]
    cut_add = lambda cut, *values: add(*[v[cut] for v in values])
    top, bottom = slice(0, half), slice(half, count)
    ran = {}
    if chips == 4:
        far_top, far_bottom = move(upper, 1), move(lower, -1)
        ran[0] = run_experts(0, [upper, lower], swaps(upper, lower))
        from_left, from_right, ran = lax.optimization_barrier((far_top, far_bottom, ran))
        far_top, far_bottom = move(from_left, 1), move(from_right, -1)
        far_top, far_bottom, upper, lower = lax.optimization_barrier(
            (far_top, far_bottom, upper, lower)
        )
        left_rows = [from_left, move(lower, 1)]
        right_rows = [move(upper, -1), from_right]
        ran[2] = run_experts(2, [far_top, far_bottom], swaps(far_top, far_bottom))
        left_rows, right_rows, ran = lax.optimization_barrier((left_rows, right_rows, ran))
        same, other = ran[2][1]
        other = swap(other)
        sums = cut_add(top, same, other), cut_add(bottom, same, other)
        left_rows, right_rows, sums = lax.optimization_barrier((left_rows, right_rows, sums))
        far_top, far_bottom = move(sums[0], 1), move(sums[1], -1)
        ran[3] = run_experts(3, left_rows, swaps(*left_rows))
        far_top, far_bottom, ran = lax.optimization_barrier((far_top, far_bottom, ran))
        same, other = ran[3][1]
        other = swap(other)
        sums = cut_add(top, same, other), add(same[bottom], other[bottom], far_bottom)
        right_rows, sums = lax.optimization_barrier((right_rows, sums))
        down_top, down_bottom = move(sums[0], -1), move(sums[1], -1)
        ran[1] = run_experts(1, right_rows, swaps(*right_rows))
        down_top, down_bottom, ran = lax.optimization_barrier((down_top, down_bottom, ran))
        same, other = ran[1][1]
        other = swap(other)
        sums = add(same[top], other[top], far_top), cut_add(bottom, same, other)
        saved = [v for r in range(chips) for v in ran[r][2]]
        sums, saved = lax.optimization_barrier((sums, saved))
        backs = [
            [ran[0][1][0], swap(ran[0][1][1])],
            [move(sums[0], 1), down_top],
            [move(sums[1], 1), down_bottom],
        ]
    else:
        rows_all = lax.all_gather(jnp.concatenate([upper, lower], axis=0), "fsdp", axis=0, tiled=True)
        back = jnp.zeros((fsdp * count, width + LANES), BF16)
        mix_all = jnp.zeros((fsdp * count, width), BF16)
        for r in range(chips):
            chip = (me_fsdp // 2 + r) % chips * 2
            at = [(chip + place) * count, (chip + 1 - place) * count]
            same, other = (lax.dynamic_slice_in_dim(rows_all, v, count, 0) for v in at)
            ran[r] = run_experts(r, [same], [other])
            for b in range(2):
                mix_all = lax.dynamic_update_slice_in_dim(mix_all, ran[r][0][b], at[b], 0)
                back = lax.dynamic_update_slice_in_dim(back, ran[r][1][b], at[b], 0)
        backs = [[lax.psum_scatter(back, "fsdp", scatter_dimension=0, tiled=True)], [], []]
        saved = [v for r in range(chips) for v in ran[r][2]]

    depth = width // ctx
    slots = fsdp * cap
    step = math.lcm(depth, LANES)
    tall = pl.BlockSpec((1, 2 * cap, step), lambda e, c: (e, 0, c))
    thin = pl.BlockSpec((1, 2 * cap, units), lambda e, c: (e, 0, 0))
    expert_terms = pl.pallas_call(
        functools.partial(expert_terms_kernel, chips),
        out_shape=shape((ctx, 3, local, depth, units), BF16),
        grid=(local, width // step),
        in_specs=[tall, tall, thin, thin, thin] * chips,
        out_specs=pl.BlockSpec((step // depth, 3, 1, depth, units), lambda e, c: (c, 0, e, 0, 0)),
        compiler_params=params(60),
        cost_estimate=pl.CostEstimate(
            flops=6 * local * slots * width * units, bytes_accessed=40 * 2**20, transcendentals=0
        ),
    )(*saved)
    backs, expert_terms = lax.optimization_barrier((backs, expert_terms))
    expert_sums = lax.psum_scatter(
        expert_terms.reshape(-1, units), "ctx", scatter_dimension=0, tiled=True
    ).reshape(3, local, depth, units)
    if chips == 4:
        mixes = {r: add(ran[r][0][0], swap(ran[r][0][1])) for r in range(chips)}
        mixes, backs = lax.optimization_barrier((mixes, backs))
        mix_steps = ring_scatter(mixes, "fsdp")
        moving = mix_steps.send(next(mix_steps))
    else:
        moving = [lax.psum_scatter(mix_all, "fsdp", scatter_dimension=0, tiled=True)]
    grad_after, grad_branch, more = call(
        functools.partial(norm_two_back_kernel, experts, len(backs[0]), len(backs[1])),
        [shape((count, width), F32), shape((count, width), BF16), shape((width, LANES), F32)],
        [no_scalars, cotangent[0], after, misc, gains, *backs[0], *backs[1], *backs[2]],
    )
    if ctx == 4:
        beside = [exchange(grad_branch, "ctx", j) for j in (1, 2)]
        branches = [[grad_branch], [beside[0]], [beside[1]]]
        branches.append(
            [exchange(beside[0][:half], "ctx", 2), exchange(beside[1][half:], "ctx", 1)]
        )
    else:
        branches = [[grad_branch]] + [[exchange(grad_branch, "ctx", j)] for j in range(1, ctx)]
    splits = [len(b) for b in branches]
    branches = sum(branches, [])
    branches, moving = lax.optimization_barrier((branches, moving))
    each = width // (ctx * fsdp)
    direct = each % 16 == 0 and chips == 4
    term_shape = lambda wide: shape(
        (2, chips, ctx, each, wide) if direct else (width, wide), BF16
    )

    def sum_terms(terms):
        if not direct:
            terms = terms.reshape(ctx, fsdp, each, -1).swapaxes(0, 1)
            return lax.psum_scatter(terms, "fsdp", scatter_dimension=0, tiled=True)[0]
        other = swap(terms[1])
        steps = ring_scatter({r: add(terms[0, r], other[r]) for r in range(chips)}, "fsdp")
        return total_of(steps.send(steps.send(next(steps)))).astype(BF16)

    [lin] = call(
        functools.partial(attend_back_kernel, splits),
        [shape((length, lin_wide), BF16)],
        [spans, *branches, pack, query, key, value, lse, cosine, sine],
        mib=60,
        scratch=[
            pltpu.VMEM((heads, length, HEAD), BF16),
            pltpu.VMEM((heads + 2 * kv_heads, length, HEAD), BF16),
            pltpu.VMEM((length, HEAD), F32),
            pltpu.VMEM((length, HEAD), F32),
        ],
        flops=20 * length * length * q_wide,
    )
    [terms] = call(
        functools.partial(weight_terms_kernel, splits, experts),
        [term_shape(lin_wide + q_wide + LANES)],
        [
            jnp.concatenate([spans, jnp.stack([me_fsdp, me_fsdp // 2, place])]),
            *branches, attn_in, lin, mix, pack, more,
        ],
        scratch=[pltpu.VMEM((length, width), BF16)],
        flops=2 * length * width * (lin_wide + q_wide),
        mib=60,
    )
    terms = sum_terms(terms)
    terms, expert_sums = lax.optimization_barrier((terms, expert_sums))
    if chips == 4:
        moving = mix_steps.send(moving)
    hidden_out = (after + RESID_SCALE * total_of(moving)).astype(BF16)[None]
    in_parts = call(
        functools.partial(input_terms_kernel, ctx),
        part_types,
        [spans, lin, pack],
        flops=2 * length * width * lin_wide,
    )
    in_parts = [in_parts[0]] + [exchange(in_parts[j], "ctx", j) for j in range(1, ctx)]
    [grad_in] = call(
        norm_one_back_kernel,
        [shape((count, width), F32)],
        [no_scalars, x, gains, grad_after, *in_parts],
    )
    grad_gate, grad_up, grad_down = (expert_sums[i].astype(F32) for i in range(3))
    terms = lax.all_to_all(terms, "ctx", split_axis=0, concat_axis=0, tiled=True)
    widths = (q_wide, kv_wide, kv_wide, q_wide, None)
    grad_query, grad_key, grad_value, grad_out, notes = call(
        functools.partial(split_kernel, widths),
        [*[shape((each, ctx * w), F32) for w in widths if w], shape((each, LANES), F32)],
        [no_scalars, terms],
    )
    return (
        hidden_out,
        grad_in[None],
        notes[:, experts],
        grad_query,
        grad_key,
        grad_value,
        grad_out,
        notes[:, experts + 1],
        notes[:, :experts],
        grad_gate,
        grad_up,
        grad_down,
    )


def solution(mesh):
    rows, both = P("fsdp", "ctx", None), ("ctx", "fsdp")
    split = P("fsdp", None)
    return jax.shard_map(
        body,
        mesh=mesh,
        in_specs=(
            rows, P(), rows, P("fsdp"), split, split, split, split, P("fsdp"), split,
            P("fsdp", None, None), P("fsdp", None, None), P("fsdp", None, None), rows,
        ),
        out_specs=(
            rows, rows, P(both), P(both, None), P(both, None), P(both, None), P(both, None),
            P(both), P(both, None), rows, rows, rows,
        ),
        check_vma=False,
    )
```

```python
import functools
import math

import jax
import jax.numpy as jnp
from jax import lax
from jax.experimental import pallas as pl
from jax.experimental.pallas import tpu as pltpu
from jax.sharding import PartitionSpec as P

HEAD = 64
HALF = HEAD // 2
NORM_EPS = 1e-06
ATTN_SCALE = 0.015625
RESID_SCALE = 0.22
ROPE_THETA = 10000.0
MASKED_SCORE = -1e30
LANES = 128
LAST = (((1,), (1,)), ((), ()))
FIRST = (((0,), (0,)), ((), ()))
F32 = jnp.float32
BF16 = jnp.bfloat16
VMEM = pl.BlockSpec(memory_space=pltpu.VMEM)
SMEM = pl.BlockSpec(memory_space=pltpu.SMEM)


def params(mib=60, **kw):
    return pltpu.CompilerParams(vmem_limit_bytes=mib * 2**20, **kw)


def call(kernel, outs, ins, scratch=(), flops=0, mib=24):
    size = lambda v: v.size * v.dtype.itemsize
    return pl.pallas_call(
        kernel,
        out_shape=outs,
        in_specs=[SMEM] + [VMEM] * (len(ins) - 1),
        out_specs=[VMEM] * len(outs),
        scratch_shapes=list(scratch),
        compiler_params=params(mib),
        cost_estimate=pl.CostEstimate(
            flops=flops, bytes_accessed=sum(map(size, list(ins) + list(outs))), transcendentals=0
        ),
    )(*ins)


def shape(dims, dtype):
    return jax.ShapeDtypeStruct(tuple(dims), dtype)


def dot(a, b, dims=(((1,), (0,)), ((), ()))):
    return lax.dot_general(a, b, dims, preferred_element_type=F32)


def scale_of(x):
    return lax.rsqrt(jnp.mean(x * x, axis=-1, keepdims=True) + NORM_EPS)


def span_rows(spans, index, size):
    return pl.ds(pl.multiple_of(spans[index] * size, size), size)


def rope(front, back, cosine, sine):
    return jnp.concatenate([front * cosine - back * sine, back * cosine + front * sine], axis=-1)


def unrope(front, back, cosine, sine):
    return jnp.concatenate([front * cosine + back * sine, back * cosine - front * sine], axis=-1)


def project_kernel(count, heads, kv_heads, experts, spans, *refs):
    pieces = refs[:count]
    pack, cosine, sine, attn_in, query, key, value, router, gains = refs[count:]
    lin_wide = (heads + 2 * kv_heads) * HEAD
    router[...] = pack[:, lin_wide + heads * HEAD :]
    turned = router[...].astype(F32).T
    gains[...] = turned[experts : experts + 2, :]
    gain = turned[experts : experts + 1, :]
    size = pieces[0].shape[0] // 2
    for j in range(count):
        x = pieces[j][...].astype(F32)
        rows_in = (x * scale_of(x) * gain).astype(BF16)
        lin = dot(rows_in, pack[:, :lin_wide])
        for h in range(2):
            at = span_rows(spans, 2 * j + h, size)
            cut = slice(h * size, (h + 1) * size)
            attn_in[at, :] = rows_in[cut]
            cos, sin = cosine[at, :], sine[at, :]
            for i in range(heads + kv_heads):
                lo = i * HEAD
                turned = rope(lin[cut, lo : lo + HALF], lin[cut, lo + HALF : lo + HEAD], cos, sin)
                if i < heads:
                    query[i, at, :] = (turned * ATTN_SCALE).astype(BF16)
                else:
                    key[i - heads, at, :] = turned.astype(BF16)
            for i in range(kv_heads):
                lo = (heads + kv_heads + i) * HEAD
                value[i, at, :] = lin[cut, lo : lo + HEAD].astype(BF16)


def diagonal(size, group):
    keys = lax.broadcasted_iota(jnp.int32, (size, group * size), 0)
    queries = lax.broadcasted_iota(jnp.int32, (size, group * size), 1) % size
    return keys <= queries


def scores_of(key_rows, query_rows, keep, size):
    raw = dot(key_rows, query_rows, LAST)
    seen = raw.shape[0] - size
    last = jnp.where(keep, raw[seen:], MASKED_SCORE)
    return last if seen == 0 else jnp.concatenate([raw[:seen], last], axis=0)


def attend_kernel(count, spans, query, key, value, pack, mix, lse, *refs):
    parts, rows_of = refs[:-1], refs[-1]
    kv_heads, length, _ = key.shape
    heads = query.shape[0]
    lo = (heads + 2 * kv_heads) * HEAD
    w_out = pack[:, lo : lo + mix.shape[1]]
    group = heads // kv_heads
    blocks = 2 * count
    size = length // blocks
    keep = diagonal(size, group)

    def one_group(g, _):
        for i in range(blocks):
            rows = slice(i * size, (i + 1) * size)
            seen = (i + 1) * size
            q = query[pl.ds(g * group, group), rows, :].reshape(group * size, HEAD)
            scores = scores_of(key[g, :seen, :], q, keep, size)
            top = jnp.max(scores, axis=0, keepdims=True)
            grown = jnp.exp(scores - top)
            total = jnp.sum(grown, axis=0, keepdims=True)
            mixed = dot(value[g, :seen, :], grown.astype(BF16), FIRST) / total
            lse[g, i, :, :] = top + jnp.log(total)
            for r in range(group):
                turned = mixed[:, r * size : (r + 1) * size].T
                rows_of[g * group + r, rows, :] = turned.astype(BF16)
        return 0

    lax.fori_loop(0, kv_heads, one_group, 0)
    for i in range(heads):
        mix[:, i * HEAD : (i + 1) * HEAD] = rows_of[i]
    for j in range(count):
        own = jnp.concatenate([mix[span_rows(spans, 2 * j + h, size), :] for h in range(2)], axis=0)
        parts[j][...] = dot(own, w_out, LAST).astype(parts[j].dtype)


def norm_two_kernel(_, x, gains, *refs):
    parts, (after, upper, lower) = refs[:-3], refs[-3:]
    branch = sum(p[...].astype(F32) for p in parts)
    rows = x[...].astype(F32) + RESID_SCALE * branch
    after[...] = rows
    ffn_in = (rows * scale_of(rows) * gains[1:2, :]).astype(BF16)
    half = upper.shape[0]
    upper[...], lower[...] = ffn_in[:half], ffn_in[half:]


def router_probs(rows, router, experts):
    logits = dot(rows, router)
    lane = lax.broadcasted_iota(jnp.int32, logits.shape, 1)
    logits = jnp.where(lane < experts, logits, MASKED_SCORE)
    grown = jnp.exp(logits - jnp.max(logits, axis=-1, keepdims=True))
    return grown / jnp.sum(grown, axis=-1, keepdims=True), lane


def experts_kernel(experts, cap, splits, chips, offset, where, *refs):
    row_refs = refs[: 2 * splits]
    grad_all, *weights, misc = refs[2 * splits : 2 * splits + 5]
    mix_refs, back_refs, saved = refs[2 * splits + 5 :][:2], refs[2 * splits + 7 :][:2], refs[2 * splits + 9 :][:5]
    keys, chances, grad_in, *held = refs[2 * splits + 14 :]
    kept, held, sems = held[3:8], held[:3], held[8]
    local, width, _ = weights[0].shape
    count = grad_in.shape[1]
    loads = [
        pltpu.make_async_copy(
            grad_all.at[
                pl.ds(pl.multiple_of(where[1 + b * chips + offset] * count, count), count), :
            ],
            grad_in.at[b],
            sems.at[b],
        )
        for b in range(2)
    ]
    pulls = [
        [
            pltpu.make_async_copy(weights[i].at[e], held[i].at[e], sems.at[2 + 3 * e + i])
            for i in range(3)
        ]
        for e in range(local)
    ]
    stores = [
        [
            pltpu.make_async_copy(
                kept[i].at[e], saved[i].at[e], sems.at[2 + 3 * local + 5 * e + i]
            )
            for i in range(5)
        ]
        for e in range(local)
    ]
    for copy in loads + sum(pulls, []):
        copy.start()
    rows = [
        jnp.concatenate([r[...] for r in row_refs[b * splits : (b + 1) * splits]], axis=0)
        for b in range(2)
    ]
    for b in range(2):
        chances[b] = router_probs(rows[b], misc[...], experts)[0].T
    for copy in loads:
        copy.wait()
    slot = lax.broadcasted_iota(jnp.int32, (cap, count), 0).astype(F32)
    lane = lax.broadcasted_iota(jnp.int32, (2 * cap, LANES), 1)
    names = [where[0] * local + e for e in range(local)]
    picks, share, mine, raw = [], [], [], []
    for b in range(2):
        keys[b] = grad_in[b, :, width:].astype(F32).T
        hits = [slot == keys[b, pl.ds(name, 1), :] for name in names]
        share.append(
            [
                jnp.sum(
                    jnp.where(hit, chances[b, pl.ds(name, 1), :], 0.0), axis=-1, keepdims=True
                )
                for hit, name in zip(hits, names)
            ]
        )
        picks.append(jnp.concatenate([hit.astype(BF16) for hit in hits], axis=0))
        mine.append(dot(picks[b], rows[b]).astype(BF16))
        raw.append(dot(picks[b], grad_in[b, :, :width]))
    both = lambda parts, e: jnp.concatenate([p[e * cap : (e + 1) * cap] for p in parts], axis=0)
    w_gate, w_up, w_down = held
    outs, backs, notes = [], [], []
    for e in range(local):
        weight = jnp.concatenate([share[b][e] for b in range(2)], axis=0)
        taken = both(mine, e)
        grad = both(raw, e) * RESID_SCALE
        grads = (grad * weight).astype(BF16)
        for copy in pulls[e]:
            copy.wait()
        gate, up = dot(taken, w_gate[e]), dot(taken, w_up[e])
        sigmoid = 1.0 / (1.0 + jnp.exp(-gate))
        silu = gate * sigmoid
        hidden = (silu * up).astype(BF16)
        out = dot(hidden, w_down[e], LAST).astype(BF16).astype(F32)
        grad_hidden = dot(grads, w_down[e])
        d_gate = (grad_hidden * up * sigmoid * (1.0 + gate * (1.0 - sigmoid))).astype(BF16)
        d_up = (grad_hidden * silu).astype(BF16)
        for i, term in enumerate((taken, grads, d_gate, d_up, hidden)):
            kept[i][e] = term
            stores[e][i].start()
        outs.append((out * weight).astype(BF16))
        backs.append((dot(d_gate, w_gate[e], LAST) + dot(d_up, w_up[e], LAST)).astype(BF16))
        note = jnp.sum(grad * out, axis=-1, keepdims=True)
        high = note.astype(BF16).astype(F32)
        notes.append(
            jnp.where(
                lane == names[e], high, jnp.where(lane == names[e] + LANES // 2, note - high, 0.0)
            ).astype(BF16)
        )
    for b in range(2):
        home = lambda parts: dot(
            picks[b],
            jnp.concatenate([p[b * cap : (b + 1) * cap] for p in parts], axis=0),
            FIRST,
        ).astype(BF16)
        mix_refs[b][...] = home(outs)
        back_refs[b][:, :width] = home(backs)
        back_refs[b][:, width:] = home(notes)
    for copy in sum(stores, []):
        copy.wait()


def expert_terms_kernel(chips, *refs):
    out = refs[-1]
    count, _, _, depth, _ = out.shape
    disp, slots, grad_gate, grad_up, hidden = (
        jnp.concatenate([r[0] for r in refs[i : 5 * chips : 5]], axis=0) for i in range(5)
    )
    pairs = ((disp, grad_gate), (disp, grad_up), (slots, hidden))
    for i, (left, right) in enumerate(pairs):
        full = dot(left, right, FIRST).astype(BF16)
        for c in range(count):
            out[c, i, 0] = full[c * depth : (c + 1) * depth]


def norm_two_back_kernel(
    experts, full, tops, _, cotangent, after, misc, gains, *refs
):
    *parts, grad_after, grad_branch, terms = refs
    width = after.shape[1]
    back = total_of([p[...] for p in parts[:full]])
    if tops:
        halves = parts[full : full + tops], parts[full + tops :]
        back = back + jnp.concatenate([total_of([p[...] for p in h]) for h in halves], axis=0)
    rows = after[...]
    scale = scale_of(rows)
    normed = rows * scale
    gain = gains[1:2, :]
    ffn_in = (normed * gain).astype(BF16)
    probs, lane = router_probs(ffn_in, misc[...], experts)
    notes = back[:, width:]
    notes = notes + pltpu.roll(notes, LANES // 2, 1)
    notes = jnp.where(lane < experts, notes, 0.0)
    logits = probs * (notes - jnp.sum(probs * notes, axis=-1, keepdims=True))
    high = logits.astype(BF16)
    low = (logits - high.astype(F32)).astype(BF16)
    grad_in = back[:, :width] + dot(high, misc[...], LAST) + dot(low, misc[...], LAST)
    grad_gain = jnp.sum(grad_in * normed, axis=0, keepdims=True)
    line = lax.broadcasted_iota(jnp.int32, (LANES, width), 0)
    terms[...] = (
        dot(ffn_in, high, FIRST)
        + dot(ffn_in, low, FIRST)
        + jnp.where(line == experts + 1, grad_gain, 0.0).T
    )
    scaled = grad_in * gain
    grad = cotangent[...].astype(F32) + scale * (
        scaled - normed * jnp.mean(scaled * normed, axis=-1, keepdims=True)
    )
    grad_after[...] = grad
    grad_branch[...] = (RESID_SCALE * grad).astype(BF16)


def pieces_of(splits, refs):
    pieces = []
    for n in splits:
        pieces.append(jnp.concatenate([r[...] for r in refs[:n]], axis=0))
        refs = refs[n:]
    return pieces, refs


def attend_back_kernel(splits, spans, *refs):
    count = len(splits)
    pieces, refs = pieces_of(splits, refs)
    pack, query, key, value, lse, cosine, sine, lin, grads, turned_of, key_sum, value_sum = refs
    kv_heads, length, _ = key.shape
    heads = query.shape[0]
    w_out = pack[:, lin.shape[1] : lin.shape[1] + heads * HEAD]
    group = heads // kv_heads
    blocks = 2 * count
    size = length // blocks
    keep = diagonal(size, group)
    for j in range(count):
        rows = dot(pieces[j], w_out).astype(BF16)
        for h in range(2):
            at = span_rows(spans, 2 * j + h, size)
            for i in range(heads):
                grads[i, at, :] = rows[h * size : (h + 1) * size, i * HEAD : (i + 1) * HEAD]

    def one_group(g, _):
        key_sum[...] = jnp.zeros_like(key_sum)
        value_sum[...] = jnp.zeros_like(value_sum)
        for i in range(blocks):
            rows = slice(i * size, (i + 1) * size)
            seen = (i + 1) * size
            q = query[pl.ds(g * group, group), rows, :].reshape(group * size, HEAD)
            grad = grads[pl.ds(g * group, group), rows, :].reshape(group * size, HEAD)
            probs = jnp.exp(scores_of(key[g, :seen, :], q, keep, size) - lse[g, i])
            grad_probs = dot(value[g, :seen, :], grad, LAST)
            delta = jnp.sum(probs * grad_probs, axis=0, keepdims=True)
            raw = (probs * (grad_probs - delta)).astype(BF16)
            value_sum[:seen, :] += dot(probs.astype(BF16), grad)
            key_sum[:seen, :] += dot(raw, q)
            grad_query = dot(key[g, :seen, :], raw, FIRST) * ATTN_SCALE
            for r in range(group):
                turned = grad_query[:, r * size : (r + 1) * size].T
                turned_of[g * group + r, rows, :] = unrope(
                    turned[:, :HALF], turned[:, HALF:], cosine[rows, :], sine[rows, :]
                ).astype(BF16)
        turned_of[heads + g] = unrope(
            key_sum[:, :HALF], key_sum[:, HALF:], cosine[...], sine[...]
        ).astype(BF16)
        turned_of[heads + kv_heads + g] = value_sum[...].astype(BF16)
        return 0

    lax.fori_loop(0, kv_heads, one_group, 0)
    for i in range(heads + 2 * kv_heads):
        lin[:, i * HEAD : (i + 1) * HEAD] = turned_of[i]


def input_terms_kernel(count, spans, lin, pack, *parts):
    weight = pack[:, : lin.shape[1]]
    size = lin.shape[0] // (2 * count)
    for j in range(count):
        own = jnp.concatenate([lin[span_rows(spans, 2 * j + h, size), :] for h in range(2)], axis=0)
        parts[j][...] = dot(own, weight, LAST).astype(parts[j].dtype)


def noted(notes):
    lane = lax.broadcasted_iota(jnp.int32, notes.shape, 1)
    high = notes.astype(BF16).astype(F32)
    return high + pltpu.roll(jnp.where(lane < LANES // 2, notes - high, 0.0), LANES // 2, 1)


def store_terms(where, out, c, full):
    if len(out.shape) == 2:
        out[c * full.shape[0] : (c + 1) * full.shape[0], :] = full
    else:
        chips, each = out.shape[1], out.shape[3]
        for f in range(2 * chips):
            offset = (f // 2 - where[1] + chips) % chips
            out[(f + where[2]) % 2, offset, c ^ where[0]] = full[f * each : (f + 1) * each]


def weight_terms_kernel(splits, experts, spans, *refs):
    count = len(splits)
    where = [spans[2 * count + i] for i in range(3)]
    pieces, refs = pieces_of(splits, refs)
    attn_in, lin, mix, pack, more, out, branch = refs
    length, width = attn_in.shape
    lin_wide = lin.shape[1]
    size = length // (2 * count)
    for j in range(count):
        for h in range(2):
            branch[span_rows(spans, 2 * j + h, size), :] = pieces[j][h * size : (h + 1) * size, :]
    step = width // count
    lane = lax.broadcasted_iota(jnp.int32, (step, LANES), 1)
    for c in range(count):
        cut = slice(c * step, (c + 1) * step)
        attn = dot(attn_in[:, cut], lin[...], FIRST)
        outs = dot(branch[:, cut], mix[...], FIRST)
        gain = pack[cut, pack.shape[1] - LANES :].astype(F32)[:, experts : experts + 1]
        weight = pack[cut, :lin_wide].astype(F32)
        grad_gain = jnp.sum(weight * attn, axis=-1, keepdims=True) / gain
        notes = noted(more[cut, :] + jnp.where(lane == experts, grad_gain, 0.0))
        store_terms(where, out, c, jnp.concatenate([attn, outs, notes], axis=1).astype(BF16))


def norm_one_back_kernel(_, x, gains, grad_after, *refs):
    parts, grad_in = refs[:-1], refs[-1]
    grad = sum(p[...].astype(F32) for p in parts) * gains[0:1, :]
    rows = x[...].astype(F32)
    scale = scale_of(rows)
    normed = rows * scale
    grad_in[...] = grad_after[...] + scale * (
        grad - normed * jnp.mean(grad * normed, axis=-1, keepdims=True)
    )


def split_kernel(count, widths, me, *refs):
    terms, outs = refs[:count], refs[count:]

    def place(own):
        for j in range(count):
            lo = 0
            for wide, out in zip(widths, outs):
                s = own ^ j
                out[:, s * wide : (s + 1) * wide] = terms[j][:, lo : lo + wide].astype(F32)
                lo += wide

    for own in range(count):
        pl.when(me[0] == own)(functools.partial(place, own))
    lo = sum(widths)
    total = total_of([t[:, lo:] for t in terms])
    outs[-1][...] = total + pltpu.roll(total, LANES // 2, 1)


def exchange(value, axis, offset):
    n = lax.axis_size(axis)
    return lax.ppermute(value, axis, [(i, i ^ offset) for i in range(n)])


def ring_pairs(n, hop):
    chips = n // 2
    return [(z * 2 + c, ((z + hop) % chips) * 2 + c) for z in range(chips) for c in range(2)]


def swap_pairs(n):
    return [(i, i ^ 1) for i in range(n)]


def ring_scatter(total, axis):
    n = lax.axis_size(axis)
    chips = n // 2
    move = lambda v, hop: lax.ppermute(v, axis, ring_pairs(n, hop))
    half = total[0].shape[0] // 2
    right = left = None
    if chips % 2 == 0:
        far = total[chips // 2]
        first, second = yield move(far[:half], 1), move(far[half:], -1)
    for s in range((chips - 1) // 2, 0, -1):
        up, down = total[s], total[chips - s]
        if right is not None:
            up, down = add(up, right), add(down, left)
        elif chips % 2 == 0:
            up = jnp.concatenate([add(up[:half], first), up[half:]], 0)
            down = jnp.concatenate([down[:half], add(down[half:], second)], 0)
        right, left = yield move(up, 1), move(down, -1)
    yield total[0], right, left


def add(*values):
    return sum(v.astype(F32) for v in values).astype(BF16)


def total_of(values):
    return sum(v.astype(F32) for v in values)


def slot_keys(route_rows, experts):
    hits = (route_rows[:, :, None] == jnp.arange(experts, dtype=jnp.int32)).any(axis=1)
    rows = jnp.arange(route_rows.shape[0], dtype=jnp.int32)
    earlier = (rows[None, :] < rows[:, None]).astype(BF16)
    ranks = jnp.dot(earlier, hits.astype(BF16), preferred_element_type=F32)
    keys = jnp.where(hits, ranks, -1.0).astype(BF16)
    return jnp.pad(keys, ((0, 0), (0, LANES - experts)), constant_values=-1)


def body(
    hidden_in, span_order, routes, attn_gain, query_weight, key_weight, value_weight, out_weight,
    ffn_gain, router_weight, gate_weight, up_weight, down_weight, cotangent
):
    ctx, fsdp = lax.axis_size("ctx"), lax.axis_size("fsdp")
    me_ctx, me_fsdp = lax.axis_index("ctx"), lax.axis_index("fsdp")
    x = hidden_in[0]
    count, width = x.shape
    length = ctx * count
    heads = query_weight.shape[1] // HEAD // ctx
    kv_heads = key_weight.shape[1] // HEAD // ctx
    experts = router_weight.shape[1]
    local, _, units = gate_weight.shape
    cap = count * routes.shape[2] * 5 // (4 * experts)
    q_wide, kv_wide = heads * HEAD, kv_heads * HEAD
    lin_wide = q_wide + 2 * kv_wide
    chips = fsdp // 2
    no_scalars = jnp.zeros((1,), jnp.int32)

    own = lambda w, wide: lax.dynamic_slice_in_dim(w, me_ctx * wide, wide, 1)
    pack = jnp.concatenate(
        [
            own(query_weight, q_wide),
            own(key_weight, kv_wide),
            own(value_weight, kv_wide),
            own(out_weight, q_wide),
            router_weight,
            attn_gain[:, None],
            ffn_gain[:, None],
            jnp.zeros((attn_gain.shape[0], LANES - experts - 2), BF16),
        ],
        axis=1,
    )
    pack = lax.all_gather(pack, "fsdp", axis=0, tiled=True)
    pieces = [x] + [exchange(x, "ctx", j) for j in range(1, ctx)]
    owners = jnp.stack([me_ctx ^ j for j in range(ctx)])
    spans = span_order.reshape(ctx, 2)[owners].reshape(-1)
    keys = slot_keys(routes[0], experts)
    grad_pack = lax.all_gather(
        jnp.concatenate([cotangent[0], keys], axis=1), "fsdp", axis=0, tiled=True
    )
    frequencies = ROPE_THETA ** (-2.0 * jnp.arange(HALF, dtype=F32) / HEAD)
    angles = jnp.arange(length, dtype=F32)[:, None] * frequencies[None, :]
    cosine, sine = jnp.cos(angles), jnp.sin(angles)

    attn_in, query, key, value, misc, gains = call(
        functools.partial(project_kernel, ctx, heads, kv_heads, experts),
        [
            shape((length, width), BF16),
            shape((heads, length, HEAD), BF16),
            shape((kv_heads, length, HEAD), BF16),
            shape((kv_heads, length, HEAD), BF16),
            shape((width, LANES), BF16),
            shape((2, width), F32),
        ],
        [spans, *pieces, pack, cosine, sine],
        flops=2 * length * width * lin_wide,
        mib=60,
    )
    part_types = [shape((count, width), F32 if j == 0 else BF16) for j in range(ctx)]
    mix, lse, *parts = call(
        functools.partial(attend_kernel, ctx),
        [
            shape((length, q_wide), BF16),
            shape((kv_heads, 2 * ctx, 1, heads // kv_heads * length // (2 * ctx)), F32),
            *part_types,
        ],
        [spans, query, key, value, pack],
        scratch=[pltpu.VMEM((heads, length, HEAD), BF16)],
        flops=8 * length * length * q_wide,
        mib=60,
    )
    parts = [parts[0]] + [exchange(parts[j], "ctx", j) for j in range(1, ctx)]
    half = count // 2
    after, upper, lower = call(
        norm_two_kernel,
        [shape((count, width), F32), *[shape((half, width), BF16)] * 2],
        [no_scalars, x, gains, *parts],
    )
    place = me_fsdp % 2
    wides = (width, width, units, units, units)
    anywhere = pl.BlockSpec(memory_space=pltpu.HBM)
    offsets = (me_fsdp // 2 + jnp.arange(chips, dtype=jnp.int32)) % chips * 2
    places = jnp.concatenate([me_fsdp[None], offsets + place, offsets + 1 - place])

    move = lambda v, hop: lax.ppermute(v, "fsdp", ring_pairs(fsdp, hop))
    swap = lambda v: lax.ppermute(v, "fsdp", swap_pairs(fsdp))

    def run_experts(offset, same, other):
        rows = [*same, *other]
        outs = pl.pallas_call(
            functools.partial(experts_kernel, experts, cap, len(rows) // 2, chips, offset),
            out_shape=[
                *[pltpu.HBM((count, width), BF16)] * 2,
                *[shape((count, width + LANES), BF16)] * 2,
                *[pltpu.HBM((local, 2 * cap, w), BF16) for w in wides],
            ],
            in_specs=[SMEM, *[VMEM] * len(rows), *[anywhere] * 4, VMEM],
            out_specs=[VMEM] * 4 + [anywhere] * 5,
            scratch_shapes=[
                pltpu.VMEM((2, LANES, count), F32),
                pltpu.VMEM((2, LANES, count), F32),
                pltpu.VMEM((2, count, width + LANES), BF16),
                *[pltpu.VMEM((local, width, units), BF16)] * 3,
                *[pltpu.VMEM((local, 2 * cap, w), BF16) for w in wides],
                pltpu.SemaphoreType.DMA((2 + 8 * local,)),
            ],
            compiler_params=params(44),
            cost_estimate=pl.CostEstimate(
                flops=32 * local * cap * width * units,
                bytes_accessed=20 * 2**20,
                transcendentals=0,
            ),
        )(
            places,
            *rows, grad_pack, gate_weight, up_weight, down_weight, misc,
        )
        return outs[0:2], outs[2:4], outs[4:]

    swaps = lambda *values: [swap(v) for v in values]
    cut_add = lambda cut, *values: add(*[v[cut] for v in values])
    top, bottom = slice(0, half), slice(half, count)
    ran = {}
    if chips == 4:
        far_top, far_bottom = move(upper, 1), move(lower, -1)
        from_left, from_right, upper, lower = lax.optimization_barrier(
            (far_top, far_bottom, upper, lower)
        )
        far_top, far_bottom = move(from_left, 1), move(from_right, -1)
        ran[0] = run_experts(0, [upper, lower], swaps(upper, lower))
        far_top, far_bottom, ran, upper, lower = lax.optimization_barrier(
            (far_top, far_bottom, ran, upper, lower)
        )
        left_rows = [from_left, move(lower, 1)]
        right_rows = [move(upper, -1), from_right]
        ran[2] = run_experts(2, [far_top, far_bottom], swaps(far_top, far_bottom))
        left_rows, right_rows, ran = lax.optimization_barrier((left_rows, right_rows, ran))
        same, other = ran[2][1]
        other = swap(other)
        sums = cut_add(top, same, other), cut_add(bottom, same, other)
        left_rows, right_rows, sums = lax.optimization_barrier((left_rows, right_rows, sums))
        far_top, far_bottom = move(sums[0], 1), move(sums[1], -1)
        ran[3] = run_experts(3, left_rows, swaps(*left_rows))
        far_top, far_bottom, ran = lax.optimization_barrier((far_top, far_bottom, ran))
        same, other = ran[3][1]
        other = swap(other)
        sums = cut_add(top, same, other), add(same[bottom], other[bottom], far_bottom)
        right_rows, sums = lax.optimization_barrier((right_rows, sums))
        down_top, down_bottom = move(sums[0], -1), move(sums[1], -1)
        ran[1] = run_experts(1, right_rows, swaps(*right_rows))
        down_top, down_bottom, ran = lax.optimization_barrier((down_top, down_bottom, ran))
        same, other = ran[1][1]
        other = swap(other)
        sums = add(same[top], other[top], far_top), cut_add(bottom, same, other)
        saved = [v for r in range(chips) for v in ran[r][2]]
        sums, saved = lax.optimization_barrier((sums, saved))
        backs = [
            [ran[0][1][0], swap(ran[0][1][1])],
            [move(sums[0], 1), down_top],
            [move(sums[1], 1), down_bottom],
        ]
    else:
        rows_all = lax.all_gather(jnp.concatenate([upper, lower], axis=0), "fsdp", axis=0, tiled=True)
        back = jnp.zeros((fsdp * count, width + LANES), BF16)
        mix_all = jnp.zeros((fsdp * count, width), BF16)
        for r in range(chips):
            chip = (me_fsdp // 2 + r) % chips * 2
            at = [(chip + place) * count, (chip + 1 - place) * count]
            same, other = (lax.dynamic_slice_in_dim(rows_all, v, count, 0) for v in at)
            ran[r] = run_experts(r, [same], [other])
            for b in range(2):
                mix_all = lax.dynamic_update_slice_in_dim(mix_all, ran[r][0][b], at[b], 0)
                back = lax.dynamic_update_slice_in_dim(back, ran[r][1][b], at[b], 0)
        backs = [[lax.psum_scatter(back, "fsdp", scatter_dimension=0, tiled=True)], [], []]
        saved = [v for r in range(chips) for v in ran[r][2]]

    depth = width // ctx
    slots = fsdp * cap
    step = math.lcm(depth, LANES)
    tall = pl.BlockSpec((1, 2 * cap, step), lambda e, c: (e, 0, c))
    thin = pl.BlockSpec((1, 2 * cap, units), lambda e, c: (e, 0, 0))
    expert_terms = pl.pallas_call(
        functools.partial(expert_terms_kernel, chips),
        out_shape=shape((ctx, 3, local, depth, units), BF16),
        grid=(local, width // step),
        in_specs=[tall, tall, thin, thin, thin] * chips,
        out_specs=pl.BlockSpec((step // depth, 3, 1, depth, units), lambda e, c: (c, 0, e, 0, 0)),
        compiler_params=params(60),
        cost_estimate=pl.CostEstimate(
            flops=6 * local * slots * width * units, bytes_accessed=40 * 2**20, transcendentals=0
        ),
    )(*saved)
    backs, expert_terms = lax.optimization_barrier((backs, expert_terms))
    expert_sums = lax.psum_scatter(
        expert_terms.reshape(-1, units), "ctx", scatter_dimension=0, tiled=True
    ).reshape(3, local, depth, units)
    if chips == 4:
        mixes = {r: add(ran[r][0][0], swap(ran[r][0][1])) for r in range(chips)}
        mixes, backs = lax.optimization_barrier((mixes, backs))
        mix_steps = ring_scatter(mixes, "fsdp")
        moving = mix_steps.send(next(mix_steps))
    else:
        moving = [lax.psum_scatter(mix_all, "fsdp", scatter_dimension=0, tiled=True)]
    grad_after, grad_branch, more = call(
        functools.partial(norm_two_back_kernel, experts, len(backs[0]), len(backs[1])),
        [shape((count, width), F32), shape((count, width), BF16), shape((width, LANES), F32)],
        [no_scalars, cotangent[0], after, misc, gains, *backs[0], *backs[1], *backs[2]],
    )
    if ctx == 4:
        beside = [exchange(grad_branch, "ctx", j) for j in (1, 2)]
        branches = [[grad_branch], [beside[0]], [beside[1]]]
        branches.append(
            [exchange(beside[0][:half], "ctx", 2), exchange(beside[1][half:], "ctx", 1)]
        )
    else:
        branches = [[grad_branch]] + [[exchange(grad_branch, "ctx", j)] for j in range(1, ctx)]
    splits = [len(b) for b in branches]
    branches = sum(branches, [])
    branches, moving = lax.optimization_barrier((branches, moving))
    each = width // (ctx * fsdp)
    direct = each % 16 == 0 and chips == 4
    term_shape = lambda wide: shape(
        (2, chips, ctx, each, wide) if direct else (width, wide), BF16
    )

    [lin] = call(
        functools.partial(attend_back_kernel, splits),
        [shape((length, lin_wide), BF16)],
        [spans, *branches, pack, query, key, value, lse, cosine, sine],
        scratch=[
            pltpu.VMEM((heads, length, HEAD), BF16),
            pltpu.VMEM((heads + 2 * kv_heads, length, HEAD), BF16),
            pltpu.VMEM((length, HEAD), F32),
            pltpu.VMEM((length, HEAD), F32),
        ],
        flops=20 * length * length * q_wide,
    )
    [terms] = call(
        functools.partial(weight_terms_kernel, splits, experts),
        [term_shape(lin_wide + q_wide + LANES)],
        [
            jnp.concatenate([spans, jnp.stack([me_ctx, me_fsdp // 2, place])]),
            *branches, attn_in, lin, mix, pack, more,
        ],
        scratch=[pltpu.VMEM((length, width), BF16)],
        flops=2 * length * width * (lin_wide + q_wide),
    )
    in_parts = call(
        functools.partial(input_terms_kernel, ctx),
        part_types,
        [spans, lin, pack],
        flops=2 * length * width * lin_wide,
    )
    if direct:
        other = swap(terms[1])
        other, in_parts = lax.optimization_barrier((other, in_parts))
        totals = {r: add(terms[0, r], other[r]) for r in range(chips)}
        totals, in_parts = lax.optimization_barrier((totals, in_parts))
        steps = ring_scatter(totals, "fsdp")
        arriving = steps.send(steps.send(next(steps)))
    else:
        terms = terms.reshape(ctx, fsdp, each, -1).swapaxes(0, 1)
        terms = lax.psum_scatter(terms, "fsdp", scatter_dimension=0, tiled=True)[0]
        terms = [
            lax.dynamic_index_in_dim(terms, me_ctx ^ j, 0, keepdims=False) for j in range(ctx)
        ]
    in_parts = [in_parts[0]] + [exchange(in_parts[j], "ctx", j) for j in range(1, ctx)]
    if chips == 4:
        moving = mix_steps.send(moving)
    hidden_out = (after + RESID_SCALE * total_of(moving)).astype(BF16)[None]
    grad_gate, grad_up, grad_down = (expert_sums[i].astype(F32) for i in range(3))
    grad_gate, grad_up, grad_down, in_parts = lax.optimization_barrier(
        (grad_gate, grad_up, grad_down, in_parts)
    )
    [grad_in] = call(
        norm_one_back_kernel,
        [shape((count, width), F32)],
        [no_scalars, x, gains, grad_after, *in_parts],
    )
    if direct:
        arriving, grad_in = lax.optimization_barrier((arriving, grad_in))
        terms = [add(*[v[j] for v in arriving]) for j in range(ctx)]
    terms = [terms[0]] + [exchange(terms[j], "ctx", j) for j in range(1, ctx)]
    widths = (q_wide, kv_wide, kv_wide, q_wide)
    grad_query, grad_key, grad_value, grad_out, notes = call(
        functools.partial(split_kernel, ctx, widths),
        [*[shape((each, ctx * w), F32) for w in widths], shape((each, LANES), F32)],
        [me_ctx[None], *terms],
    )
    return (
        hidden_out,
        grad_in[None],
        notes[:, experts],
        grad_query,
        grad_key,
        grad_value,
        grad_out,
        notes[:, experts + 1],
        notes[:, :experts],
        grad_gate,
        grad_up,
        grad_down,
    )


def solution(mesh):
    rows, both = P("fsdp", "ctx", None), ("ctx", "fsdp")
    split = P("fsdp", None)
    return jax.shard_map(
        body,
        mesh=mesh,
        in_specs=(
            rows, P(), rows, P("fsdp"), split, split, split, split, P("fsdp"), split,
            P("fsdp", None, None), P("fsdp", None, None), P("fsdp", None, None), rows,
        ),
        out_specs=(
            rows, rows, P(both), P(both, None), P(both, None), P(both, None), P(both, None),
            P(both), P(both, None), rows, rows, rows,
        ),
        check_vma=False,
    )
```

```python
import functools
import math

import jax
import jax.numpy as jnp
from jax import lax
from jax.experimental import pallas as pl
from jax.experimental.pallas import tpu as pltpu
from jax.sharding import PartitionSpec as P

HEAD = 64
HALF = HEAD // 2
NORM_EPS = 1e-06
ATTN_SCALE = 0.015625
RESID_SCALE = 0.22
ROPE_THETA = 10000.0
MASKED_SCORE = -1e30
LANES = 128
LAST = (((1,), (1,)), ((), ()))
FIRST = (((0,), (0,)), ((), ()))
F32 = jnp.float32
BF16 = jnp.bfloat16
VMEM = pl.BlockSpec(memory_space=pltpu.VMEM)
SMEM = pl.BlockSpec(memory_space=pltpu.SMEM)


def params(mib=60, **kw):
    return pltpu.CompilerParams(vmem_limit_bytes=mib * 2**20, **kw)


def call(kernel, outs, ins, scratch=(), flops=0, mib=24):
    size = lambda v: v.size * v.dtype.itemsize
    return pl.pallas_call(
        kernel,
        out_shape=outs,
        in_specs=[SMEM] + [VMEM] * (len(ins) - 1),
        out_specs=[VMEM] * len(outs),
        scratch_shapes=list(scratch),
        compiler_params=params(mib),
        cost_estimate=pl.CostEstimate(
            flops=flops, bytes_accessed=sum(map(size, list(ins) + list(outs))), transcendentals=0
        ),
    )(*ins)


def shape(dims, dtype):
    return jax.ShapeDtypeStruct(tuple(dims), dtype)


def dot(a, b, dims=(((1,), (0,)), ((), ()))):
    return lax.dot_general(a, b, dims, preferred_element_type=F32)


def scale_of(x):
    return lax.rsqrt(jnp.mean(x * x, axis=-1, keepdims=True) + NORM_EPS)


def span_rows(spans, index, size):
    return pl.ds(pl.multiple_of(spans[index] * size, size), size)


def rope(front, back, cosine, sine):
    return jnp.concatenate([front * cosine - back * sine, back * cosine + front * sine], axis=-1)


def unrope(front, back, cosine, sine):
    return jnp.concatenate([front * cosine + back * sine, back * cosine - front * sine], axis=-1)


def project_kernel(count, heads, kv_heads, experts, spans, *refs):
    pieces = refs[:count]
    pack, cosine, sine, attn_in, query, key, value, router, gains = refs[count:]
    lin_wide = (heads + 2 * kv_heads) * HEAD
    router[...] = pack[:, lin_wide + heads * HEAD :]
    turned = router[...].astype(F32).T
    gains[...] = turned[experts : experts + 2, :]
    gain = turned[experts : experts + 1, :]
    size = pieces[0].shape[0] // 2
    for j in range(count):
        x = pieces[j][...].astype(F32)
        rows_in = (x * scale_of(x) * gain).astype(BF16)
        lin = dot(rows_in, pack[:, :lin_wide])
        for h in range(2):
            at = span_rows(spans, 2 * j + h, size)
            cut = slice(h * size, (h + 1) * size)
            attn_in[at, :] = rows_in[cut]
            cos, sin = cosine[at, :], sine[at, :]
            for i in range(heads + kv_heads):
                lo = i * HEAD
                turned = rope(lin[cut, lo : lo + HALF], lin[cut, lo + HALF : lo + HEAD], cos, sin)
                if i < heads:
                    query[i, at, :] = (turned * ATTN_SCALE).astype(BF16)
                else:
                    key[i - heads, at, :] = turned.astype(BF16)
            for i in range(kv_heads):
                lo = (heads + kv_heads + i) * HEAD
                value[i, at, :] = lin[cut, lo : lo + HEAD].astype(BF16)


def diagonal(size, group):
    keys = lax.broadcasted_iota(jnp.int32, (size, group * size), 0)
    queries = lax.broadcasted_iota(jnp.int32, (size, group * size), 1) % size
    return keys <= queries


def scores_of(key_rows, query_rows, keep, size):
    raw = dot(key_rows, query_rows, LAST)
    seen = raw.shape[0] - size
    last = jnp.where(keep, raw[seen:], MASKED_SCORE)
    return last if seen == 0 else jnp.concatenate([raw[:seen], last], axis=0)


def attend_kernel(count, spans, query, key, value, pack, mix, lse, *refs):
    parts, rows_of = refs[:-1], refs[-1]
    kv_heads, length, _ = key.shape
    heads = query.shape[0]
    lo = (heads + 2 * kv_heads) * HEAD
    w_out = pack[:, lo : lo + mix.shape[1]]
    group = heads // kv_heads
    blocks = 2 * count
    size = length // blocks
    keep = diagonal(size, group)

    def one_group(g, _):
        for i in range(blocks):
            rows = slice(i * size, (i + 1) * size)
            seen = (i + 1) * size
            q = query[pl.ds(g * group, group), rows, :].reshape(group * size, HEAD)
            scores = scores_of(key[g, :seen, :], q, keep, size)
            top = jnp.max(scores, axis=0, keepdims=True)
            grown = jnp.exp(scores - top)
            total = jnp.sum(grown, axis=0, keepdims=True)
            mixed = dot(value[g, :seen, :], grown.astype(BF16), FIRST) / total
            lse[g, i, :, :] = top + jnp.log(total)
            for r in range(group):
                turned = mixed[:, r * size : (r + 1) * size].T
                rows_of[g * group + r, rows, :] = turned.astype(BF16)
        return 0

    lax.fori_loop(0, kv_heads, one_group, 0)
    for i in range(heads):
        mix[:, i * HEAD : (i + 1) * HEAD] = rows_of[i]
    for j in range(count):
        own = jnp.concatenate([mix[span_rows(spans, 2 * j + h, size), :] for h in range(2)], axis=0)
        parts[j][...] = dot(own, w_out, LAST).astype(parts[j].dtype)


def norm_two_kernel(_, x, gains, *refs):
    parts, (after, upper, lower) = refs[:-3], refs[-3:]
    branch = sum(p[...].astype(F32) for p in parts)
    rows = x[...].astype(F32) + RESID_SCALE * branch
    after[...] = rows
    ffn_in = (rows * scale_of(rows) * gains[1:2, :]).astype(BF16)
    half = upper.shape[0]
    upper[...], lower[...] = ffn_in[:half], ffn_in[half:]


def router_probs(rows, router, experts):
    logits = dot(rows, router)
    lane = lax.broadcasted_iota(jnp.int32, logits.shape, 1)
    logits = jnp.where(lane < experts, logits, MASKED_SCORE)
    grown = jnp.exp(logits - jnp.max(logits, axis=-1, keepdims=True))
    return grown / jnp.sum(grown, axis=-1, keepdims=True), lane


def experts_kernel(experts, cap, splits, chips, offset, where, *refs):
    row_refs = refs[: 2 * splits]
    grad_all, *weights, misc = refs[2 * splits : 2 * splits + 5]
    mix_refs, back_refs, saved = refs[2 * splits + 5 :][:2], refs[2 * splits + 7 :][:2], refs[2 * splits + 9 :][:5]
    keys, chances, grad_in, *held = refs[2 * splits + 14 :]
    kept, held, sems = held[3:8], held[:3], held[8]
    local, width, _ = weights[0].shape
    count = grad_in.shape[1]
    loads = [
        pltpu.make_async_copy(
            grad_all.at[
                pl.ds(pl.multiple_of(where[1 + b * chips + offset] * count, count), count), :
            ],
            grad_in.at[b],
            sems.at[b],
        )
        for b in range(2)
    ]
    pulls = [
        [
            pltpu.make_async_copy(weights[i].at[e], held[i].at[e], sems.at[2 + 3 * e + i])
            for i in range(3)
        ]
        for e in range(local)
    ]
    stores = [
        [
            pltpu.make_async_copy(
                kept[i].at[e], saved[i].at[e], sems.at[2 + 3 * local + 5 * e + i]
            )
            for i in range(5)
        ]
        for e in range(local)
    ]
    for copy in loads + sum(pulls, []):
        copy.start()
    rows = [
        jnp.concatenate([r[...] for r in row_refs[b * splits : (b + 1) * splits]], axis=0)
        for b in range(2)
    ]
    for b in range(2):
        chances[b] = router_probs(rows[b], misc[...], experts)[0].T
    for copy in loads:
        copy.wait()
    slot = lax.broadcasted_iota(jnp.int32, (cap, count), 0).astype(F32)
    lane = lax.broadcasted_iota(jnp.int32, (2 * cap, LANES), 1)
    names = [where[0] * local + e for e in range(local)]
    picks, share, mine, raw = [], [], [], []
    for b in range(2):
        keys[b] = grad_in[b, :, width:].astype(F32).T
        hits = [slot == keys[b, pl.ds(name, 1), :] for name in names]
        share.append(
            [
                jnp.sum(
                    jnp.where(hit, chances[b, pl.ds(name, 1), :], 0.0), axis=-1, keepdims=True
                )
                for hit, name in zip(hits, names)
            ]
        )
        picks.append(jnp.concatenate([hit.astype(BF16) for hit in hits], axis=0))
        mine.append(dot(picks[b], rows[b]).astype(BF16))
        raw.append(dot(picks[b], grad_in[b, :, :width]))
    both = lambda parts, e: jnp.concatenate([p[e * cap : (e + 1) * cap] for p in parts], axis=0)
    w_gate, w_up, w_down = held
    outs, backs, notes = [], [], []
    for e in range(local):
        weight = jnp.concatenate([share[b][e] for b in range(2)], axis=0)
        taken = both(mine, e)
        grad = both(raw, e) * RESID_SCALE
        grads = (grad * weight).astype(BF16)
        for copy in pulls[e]:
            copy.wait()
        gate, up = dot(taken, w_gate[e]), dot(taken, w_up[e])
        sigmoid = 1.0 / (1.0 + jnp.exp(-gate))
        silu = gate * sigmoid
        hidden = (silu * up).astype(BF16)
        out = dot(hidden, w_down[e], LAST).astype(BF16).astype(F32)
        grad_hidden = dot(grads, w_down[e])
        d_gate = (grad_hidden * up * sigmoid * (1.0 + gate * (1.0 - sigmoid))).astype(BF16)
        d_up = (grad_hidden * silu).astype(BF16)
        for i, term in enumerate((taken, grads, d_gate, d_up, hidden)):
            kept[i][e] = term
            stores[e][i].start()
        outs.append((out * weight).astype(BF16))
        backs.append((dot(d_gate, w_gate[e], LAST) + dot(d_up, w_up[e], LAST)).astype(BF16))
        note = jnp.sum(grad * out, axis=-1, keepdims=True)
        high = note.astype(BF16).astype(F32)
        notes.append(
            jnp.where(
                lane == names[e], high, jnp.where(lane == names[e] + LANES // 2, note - high, 0.0)
            ).astype(BF16)
        )
    for b in range(2):
        home = lambda parts: dot(
            picks[b],
            jnp.concatenate([p[b * cap : (b + 1) * cap] for p in parts], axis=0),
            FIRST,
        ).astype(BF16)
        mix_refs[b][...] = home(outs)
        back_refs[b][:, :width] = home(backs)
        back_refs[b][:, width:] = home(notes)
    for copy in sum(stores, []):
        copy.wait()


def expert_terms_kernel(chips, *refs):
    out = refs[-1]
    count, _, _, depth, _ = out.shape
    disp, slots, grad_gate, grad_up, hidden = (
        jnp.concatenate([r[0] for r in refs[i : 5 * chips : 5]], axis=0) for i in range(5)
    )
    pairs = ((disp, grad_gate), (disp, grad_up), (slots, hidden))
    for i, (left, right) in enumerate(pairs):
        full = dot(left, right, FIRST).astype(BF16)
        for c in range(count):
            out[c, i, 0] = full[c * depth : (c + 1) * depth]


def norm_two_back_kernel(
    experts, full, tops, _, cotangent, after, misc, gains, *refs
):
    *parts, grad_after, grad_branch, terms = refs
    width = after.shape[1]
    back = total_of([p[...] for p in parts[:full]])
    if tops:
        halves = parts[full : full + tops], parts[full + tops :]
        back = back + jnp.concatenate([total_of([p[...] for p in h]) for h in halves], axis=0)
    rows = after[...]
    scale = scale_of(rows)
    normed = rows * scale
    gain = gains[1:2, :]
    ffn_in = (normed * gain).astype(BF16)
    probs, lane = router_probs(ffn_in, misc[...], experts)
    notes = back[:, width:]
    notes = notes + pltpu.roll(notes, LANES // 2, 1)
    notes = jnp.where(lane < experts, notes, 0.0)
    logits = probs * (notes - jnp.sum(probs * notes, axis=-1, keepdims=True))
    high = logits.astype(BF16)
    low = (logits - high.astype(F32)).astype(BF16)
    grad_in = back[:, :width] + dot(high, misc[...], LAST) + dot(low, misc[...], LAST)
    grad_gain = jnp.sum(grad_in * normed, axis=0, keepdims=True)
    line = lax.broadcasted_iota(jnp.int32, (LANES, width), 0)
    terms[...] = (
        dot(ffn_in, high, FIRST)
        + dot(ffn_in, low, FIRST)
        + jnp.where(line == experts + 1, grad_gain, 0.0).T
    )
    scaled = grad_in * gain
    grad = cotangent[...].astype(F32) + scale * (
        scaled - normed * jnp.mean(scaled * normed, axis=-1, keepdims=True)
    )
    grad_after[...] = grad
    grad_branch[...] = (RESID_SCALE * grad).astype(BF16)


def pieces_of(splits, refs):
    pieces = []
    for n in splits:
        pieces.append(jnp.concatenate([r[...] for r in refs[:n]], axis=0))
        refs = refs[n:]
    return pieces, refs


def attend_back_kernel(splits, spans, *refs):
    count = len(splits)
    pieces, refs = pieces_of(splits, refs)
    pack, query, key, value, lse, cosine, sine, lin, grads, turned_of, key_sum, value_sum = refs
    kv_heads, length, _ = key.shape
    heads = query.shape[0]
    w_out = pack[:, lin.shape[1] : lin.shape[1] + heads * HEAD]
    group = heads // kv_heads
    blocks = 2 * count
    size = length // blocks
    keep = diagonal(size, group)
    for j in range(count):
        rows = dot(pieces[j], w_out).astype(BF16)
        for h in range(2):
            at = span_rows(spans, 2 * j + h, size)
            for i in range(heads):
                grads[i, at, :] = rows[h * size : (h + 1) * size, i * HEAD : (i + 1) * HEAD]

    def one_group(g, _):
        key_sum[...] = jnp.zeros_like(key_sum)
        value_sum[...] = jnp.zeros_like(value_sum)
        for i in range(blocks):
            rows = slice(i * size, (i + 1) * size)
            seen = (i + 1) * size
            q = query[pl.ds(g * group, group), rows, :].reshape(group * size, HEAD)
            grad = grads[pl.ds(g * group, group), rows, :].reshape(group * size, HEAD)
            probs = jnp.exp(scores_of(key[g, :seen, :], q, keep, size) - lse[g, i])
            grad_probs = dot(value[g, :seen, :], grad, LAST)
            delta = jnp.sum(probs * grad_probs, axis=0, keepdims=True)
            raw = (probs * (grad_probs - delta)).astype(BF16)
            value_sum[:seen, :] += dot(probs.astype(BF16), grad)
            key_sum[:seen, :] += dot(raw, q)
            grad_query = dot(key[g, :seen, :], raw, FIRST) * ATTN_SCALE
            for r in range(group):
                turned = grad_query[:, r * size : (r + 1) * size].T
                turned_of[g * group + r, rows, :] = unrope(
                    turned[:, :HALF], turned[:, HALF:], cosine[rows, :], sine[rows, :]
                ).astype(BF16)
        turned_of[heads + g] = unrope(
            key_sum[:, :HALF], key_sum[:, HALF:], cosine[...], sine[...]
        ).astype(BF16)
        turned_of[heads + kv_heads + g] = value_sum[...].astype(BF16)
        return 0

    lax.fori_loop(0, kv_heads, one_group, 0)
    for i in range(heads + 2 * kv_heads):
        lin[:, i * HEAD : (i + 1) * HEAD] = turned_of[i]


def input_terms_kernel(count, spans, lin, pack, *parts):
    weight = pack[:, : lin.shape[1]]
    size = lin.shape[0] // (2 * count)
    for j in range(count):
        own = jnp.concatenate([lin[span_rows(spans, 2 * j + h, size), :] for h in range(2)], axis=0)
        parts[j][...] = dot(own, weight, LAST).astype(parts[j].dtype)


def noted(notes):
    lane = lax.broadcasted_iota(jnp.int32, notes.shape, 1)
    high = notes.astype(BF16).astype(F32)
    return high + pltpu.roll(jnp.where(lane < LANES // 2, notes - high, 0.0), LANES // 2, 1)


def store_terms(where, out, c, full):
    if len(out.shape) == 2:
        out[c * full.shape[0] : (c + 1) * full.shape[0], :] = full
    else:
        chips, each = out.shape[1], out.shape[3]
        for f in range(2 * chips):
            offset = (f // 2 - where[1] + chips) % chips
            out[(f + where[2]) % 2, offset, c ^ where[0]] = full[f * each : (f + 1) * each]


def weight_terms_kernel(splits, experts, spans, *refs):
    count = len(splits)
    where = [spans[2 * count + i] for i in range(3)]
    pieces, refs = pieces_of(splits, refs)
    attn_in, lin, mix, pack, more, out, branch = refs
    length, width = attn_in.shape
    lin_wide = lin.shape[1]
    size = length // (2 * count)
    for j in range(count):
        for h in range(2):
            branch[span_rows(spans, 2 * j + h, size), :] = pieces[j][h * size : (h + 1) * size, :]
    step = width // count
    lane = lax.broadcasted_iota(jnp.int32, (step, LANES), 1)
    for c in range(count):
        cut = slice(c * step, (c + 1) * step)
        attn = dot(attn_in[:, cut], lin[...], FIRST)
        outs = dot(branch[:, cut], mix[...], FIRST)
        gain = pack[cut, pack.shape[1] - LANES :].astype(F32)[:, experts : experts + 1]
        weight = pack[cut, :lin_wide].astype(F32)
        grad_gain = jnp.sum(weight * attn, axis=-1, keepdims=True) / gain
        notes = noted(more[cut, :] + jnp.where(lane == experts, grad_gain, 0.0))
        store_terms(where, out, c, jnp.concatenate([attn, outs, notes], axis=1).astype(BF16))


def norm_one_back_kernel(_, x, gains, grad_after, *refs):
    parts, grad_in = refs[:-1], refs[-1]
    grad = sum(p[...].astype(F32) for p in parts) * gains[0:1, :]
    rows = x[...].astype(F32)
    scale = scale_of(rows)
    normed = rows * scale
    grad_in[...] = grad_after[...] + scale * (
        grad - normed * jnp.mean(grad * normed, axis=-1, keepdims=True)
    )


def split_kernel(count, widths, me, *refs):
    terms, outs = refs[:count], refs[count:]

    def place(own):
        for j in range(count):
            lo = 0
            for wide, out in zip(widths, outs):
                s = own ^ j
                out[:, s * wide : (s + 1) * wide] = terms[j][:, lo : lo + wide].astype(F32)
                lo += wide

    for own in range(count):
        pl.when(me[0] == own)(functools.partial(place, own))
    lo = sum(widths)
    total = total_of([t[:, lo:] for t in terms])
    outs[-1][...] = total + pltpu.roll(total, LANES // 2, 1)


def exchange(value, axis, offset):
    n = lax.axis_size(axis)
    return lax.ppermute(value, axis, [(i, i ^ offset) for i in range(n)])


def ring_pairs(n, hop):
    chips = n // 2
    return [(z * 2 + c, ((z + hop) % chips) * 2 + c) for z in range(chips) for c in range(2)]


def swap_pairs(n):
    return [(i, i ^ 1) for i in range(n)]


def ring_scatter(total, axis):
    n = lax.axis_size(axis)
    chips = n // 2
    move = lambda v, hop: lax.ppermute(v, axis, ring_pairs(n, hop))
    half = total[0].shape[0] // 2
    right = left = None
    if chips % 2 == 0:
        far = total[chips // 2]
        first, second = yield move(far[:half], 1), move(far[half:], -1)
    for s in range((chips - 1) // 2, 0, -1):
        up, down = total[s], total[chips - s]
        if right is not None:
            up, down = add(up, right), add(down, left)
        elif chips % 2 == 0:
            up = jnp.concatenate([add(up[:half], first), up[half:]], 0)
            down = jnp.concatenate([down[:half], add(down[half:], second)], 0)
        right, left = yield move(up, 1), move(down, -1)
    yield total[0], right, left


def add(*values):
    return sum(v.astype(F32) for v in values).astype(BF16)


def total_of(values):
    return sum(v.astype(F32) for v in values)


def slot_keys(route_rows, experts):
    hits = (route_rows[:, :, None] == jnp.arange(experts, dtype=jnp.int32)).any(axis=1)
    rows = jnp.arange(route_rows.shape[0], dtype=jnp.int32)
    earlier = (rows[None, :] < rows[:, None]).astype(BF16)
    ranks = jnp.dot(earlier, hits.astype(BF16), preferred_element_type=F32)
    keys = jnp.where(hits, ranks, -1.0).astype(BF16)
    return jnp.pad(keys, ((0, 0), (0, LANES - experts)), constant_values=-1)


def body(
    hidden_in, span_order, routes, attn_gain, query_weight, key_weight, value_weight, out_weight,
    ffn_gain, router_weight, gate_weight, up_weight, down_weight, cotangent
):
    ctx, fsdp = lax.axis_size("ctx"), lax.axis_size("fsdp")
    me_ctx, me_fsdp = lax.axis_index("ctx"), lax.axis_index("fsdp")
    x = hidden_in[0]
    count, width = x.shape
    length = ctx * count
    heads = query_weight.shape[1] // HEAD // ctx
    kv_heads = key_weight.shape[1] // HEAD // ctx
    experts = router_weight.shape[1]
    local, _, units = gate_weight.shape
    cap = count * routes.shape[2] * 5 // (4 * experts)
    q_wide, kv_wide = heads * HEAD, kv_heads * HEAD
    lin_wide = q_wide + 2 * kv_wide
    chips = fsdp // 2
    no_scalars = jnp.zeros((1,), jnp.int32)

    own = lambda w, wide: lax.dynamic_slice_in_dim(w, me_ctx * wide, wide, 1)
    pack = jnp.concatenate(
        [
            own(query_weight, q_wide),
            own(key_weight, kv_wide),
            own(value_weight, kv_wide),
            own(out_weight, q_wide),
            router_weight,
            attn_gain[:, None],
            ffn_gain[:, None],
            jnp.zeros((attn_gain.shape[0], LANES - experts - 2), BF16),
        ],
        axis=1,
    )
    pack = lax.all_gather(pack, "fsdp", axis=0, tiled=True)
    pieces = [x] + [exchange(x, "ctx", j) for j in range(1, ctx)]
    owners = jnp.stack([me_ctx ^ j for j in range(ctx)])
    spans = span_order.reshape(ctx, 2)[owners].reshape(-1)
    keys = slot_keys(routes[0], experts)
    grad_pack = lax.all_gather(
        jnp.concatenate([cotangent[0], keys], axis=1), "fsdp", axis=0, tiled=True
    )
    frequencies = ROPE_THETA ** (-2.0 * jnp.arange(HALF, dtype=F32) / HEAD)
    angles = jnp.arange(length, dtype=F32)[:, None] * frequencies[None, :]
    cosine, sine = jnp.cos(angles), jnp.sin(angles)

    attn_in, query, key, value, misc, gains = call(
        functools.partial(project_kernel, ctx, heads, kv_heads, experts),
        [
            shape((length, width), BF16),
            shape((heads, length, HEAD), BF16),
            shape((kv_heads, length, HEAD), BF16),
            shape((kv_heads, length, HEAD), BF16),
            shape((width, LANES), BF16),
            shape((2, width), F32),
        ],
        [spans, *pieces, pack, cosine, sine],
        flops=2 * length * width * lin_wide,
        mib=60,
    )
    part_types = [shape((count, width), F32 if j == 0 else BF16) for j in range(ctx)]
    mix, lse, *parts = call(
        functools.partial(attend_kernel, ctx),
        [
            shape((length, q_wide), BF16),
            shape((kv_heads, 2 * ctx, 1, heads // kv_heads * length // (2 * ctx)), F32),
            *part_types,
        ],
        [spans, query, key, value, pack],
        scratch=[pltpu.VMEM((heads, length, HEAD), BF16)],
        flops=8 * length * length * q_wide,
        mib=60,
    )
    parts = [parts[0]] + [exchange(parts[j], "ctx", j) for j in range(1, ctx)]
    half = count // 2
    after, upper, lower = call(
        norm_two_kernel,
        [shape((count, width), F32), *[shape((half, width), BF16)] * 2],
        [no_scalars, x, gains, *parts],
    )
    place = me_fsdp % 2
    wides = (width, width, units, units, units)
    anywhere = pl.BlockSpec(memory_space=pltpu.HBM)
    offsets = (me_fsdp // 2 + jnp.arange(chips, dtype=jnp.int32)) % chips * 2
    places = jnp.concatenate([me_fsdp[None], offsets + place, offsets + 1 - place])

    move = lambda v, hop: lax.ppermute(v, "fsdp", ring_pairs(fsdp, hop))
    swap = lambda v: lax.ppermute(v, "fsdp", swap_pairs(fsdp))

    def run_experts(offset, same, other):
        rows = [*same, *other]
        outs = pl.pallas_call(
            functools.partial(experts_kernel, experts, cap, len(rows) // 2, chips, offset),
            out_shape=[
                *[pltpu.HBM((count, width), BF16)] * 2,
                *[shape((count, width + LANES), BF16)] * 2,
                *[pltpu.HBM((local, 2 * cap, w), BF16) for w in wides],
            ],
            in_specs=[SMEM, *[VMEM] * len(rows), *[anywhere] * 4, VMEM],
            out_specs=[VMEM] * 4 + [anywhere] * 5,
            scratch_shapes=[
                pltpu.VMEM((2, LANES, count), F32),
                pltpu.VMEM((2, LANES, count), F32),
                pltpu.VMEM((2, count, width + LANES), BF16),
                *[pltpu.VMEM((local, width, units), BF16)] * 3,
                *[pltpu.VMEM((local, 2 * cap, w), BF16) for w in wides],
                pltpu.SemaphoreType.DMA((2 + 8 * local,)),
            ],
            compiler_params=params(44),
            cost_estimate=pl.CostEstimate(
                flops=32 * local * cap * width * units,
                bytes_accessed=20 * 2**20,
                transcendentals=0,
            ),
        )(
            places,
            *rows, grad_pack, gate_weight, up_weight, down_weight, misc,
        )
        return outs[0:2], outs[2:4], outs[4:]

    depth = width // ctx
    slots = fsdp * cap
    step = math.lcm(depth, LANES)
    tall = pl.BlockSpec((1, 2 * cap, step), lambda e, c: (e, 0, c))
    thin = pl.BlockSpec((1, 2 * cap, units), lambda e, c: (e, 0, 0))

    def sum_experts(saved):
        return pl.pallas_call(
            functools.partial(expert_terms_kernel, chips),
            out_shape=shape((ctx, 3, local, depth, units), BF16),
            grid=(local, width // step),
            in_specs=[tall, tall, thin, thin, thin] * chips,
            out_specs=pl.BlockSpec((step // depth, 3, 1, depth, units), lambda e, c: (c, 0, e, 0, 0)),
            compiler_params=params(60),
            cost_estimate=pl.CostEstimate(
                flops=6 * local * slots * width * units, bytes_accessed=40 * 2**20, transcendentals=0
            ),
        )(*saved)

    swaps = lambda *values: [swap(v) for v in values]
    cut_add = lambda cut, *values: add(*[v[cut] for v in values])
    top, bottom = slice(0, half), slice(half, count)
    ran = {}
    if chips == 4:
        far_top, far_bottom = move(upper, 1), move(lower, -1)
        from_left, from_right, upper, lower = lax.optimization_barrier(
            (far_top, far_bottom, upper, lower)
        )
        far_top, far_bottom = move(from_left, 1), move(from_right, -1)
        ran[0] = run_experts(0, [upper, lower], swaps(upper, lower))
        far_top, far_bottom, ran, upper, lower = lax.optimization_barrier(
            (far_top, far_bottom, ran, upper, lower)
        )
        left_rows = [from_left, move(lower, 1)]
        right_rows = [move(upper, -1), from_right]
        ran[2] = run_experts(2, [far_top, far_bottom], swaps(far_top, far_bottom))
        left_rows, right_rows, ran = lax.optimization_barrier((left_rows, right_rows, ran))
        same, other = ran[2][1]
        other = swap(other)
        sums = cut_add(top, same, other), cut_add(bottom, same, other)
        left_rows, right_rows, sums = lax.optimization_barrier((left_rows, right_rows, sums))
        far_top, far_bottom = move(sums[0], 1), move(sums[1], -1)
        ran[3] = run_experts(3, left_rows, swaps(*left_rows))
        far_top, far_bottom, ran = lax.optimization_barrier((far_top, far_bottom, ran))
        same, other = ran[3][1]
        other = swap(other)
        sums = cut_add(top, same, other), add(same[bottom], other[bottom], far_bottom)
        right_rows, sums = lax.optimization_barrier((right_rows, sums))
        down_top, down_bottom = move(sums[0], -1), move(sums[1], -1)
        ran[1] = run_experts(1, right_rows, swaps(*right_rows))
        down_top, down_bottom, ran = lax.optimization_barrier((down_top, down_bottom, ran))
        same, other = ran[1][1]
        other = swap(other)
        saved = [v for r in range(chips) for v in ran[r][2]]
        expert_terms = sum_experts(saved)
        same, other, expert_terms = lax.optimization_barrier((same, other, expert_terms))
        sums = add(same[top], other[top], far_top), cut_add(bottom, same, other)
        backs = [
            [ran[0][1][0], swap(ran[0][1][1])],
            [move(sums[0], 1), down_top],
            [move(sums[1], 1), down_bottom],
        ]
    else:
        rows_all = lax.all_gather(jnp.concatenate([upper, lower], axis=0), "fsdp", axis=0, tiled=True)
        back = jnp.zeros((fsdp * count, width + LANES), BF16)
        mix_all = jnp.zeros((fsdp * count, width), BF16)
        for r in range(chips):
            chip = (me_fsdp // 2 + r) % chips * 2
            at = [(chip + place) * count, (chip + 1 - place) * count]
            same, other = (lax.dynamic_slice_in_dim(rows_all, v, count, 0) for v in at)
            ran[r] = run_experts(r, [same], [other])
            for b in range(2):
                mix_all = lax.dynamic_update_slice_in_dim(mix_all, ran[r][0][b], at[b], 0)
                back = lax.dynamic_update_slice_in_dim(back, ran[r][1][b], at[b], 0)
        backs = [[lax.psum_scatter(back, "fsdp", scatter_dimension=0, tiled=True)], [], []]
        expert_terms = sum_experts([v for r in range(chips) for v in ran[r][2]])

    expert_sums = lax.psum_scatter(
        expert_terms.reshape(-1, units), "ctx", scatter_dimension=0, tiled=True
    ).reshape(3, local, depth, units)
    if chips == 4:
        mixes = {r: add(ran[r][0][0], swap(ran[r][0][1])) for r in range(chips)}
        mixes, backs = lax.optimization_barrier((mixes, backs))
        mix_steps = ring_scatter(mixes, "fsdp")
        moving = mix_steps.send(next(mix_steps))
    else:
        moving = [lax.psum_scatter(mix_all, "fsdp", scatter_dimension=0, tiled=True)]
    grad_after, grad_branch, more = call(
        functools.partial(norm_two_back_kernel, experts, len(backs[0]), len(backs[1])),
        [shape((count, width), F32), shape((count, width), BF16), shape((width, LANES), F32)],
        [no_scalars, cotangent[0], after, misc, gains, *backs[0], *backs[1], *backs[2]],
    )
    if ctx == 4:
        beside = [exchange(grad_branch, "ctx", j) for j in (1, 2)]
        branches = [[grad_branch], [beside[0]], [beside[1]]]
        branches.append(
            [exchange(beside[0][:half], "ctx", 2), exchange(beside[1][half:], "ctx", 1)]
        )
    else:
        branches = [[grad_branch]] + [[exchange(grad_branch, "ctx", j)] for j in range(1, ctx)]
    splits = [len(b) for b in branches]
    branches = sum(branches, [])
    branches, moving = lax.optimization_barrier((branches, moving))
    each = width // (ctx * fsdp)
    direct = each % 16 == 0 and chips == 4
    term_shape = lambda wide: shape(
        (2, chips, ctx, each, wide) if direct else (width, wide), BF16
    )

    [lin] = call(
        functools.partial(attend_back_kernel, splits),
        [shape((length, lin_wide), BF16)],
        [spans, *branches, pack, query, key, value, lse, cosine, sine],
        scratch=[
            pltpu.VMEM((heads, length, HEAD), BF16),
            pltpu.VMEM((heads + 2 * kv_heads, length, HEAD), BF16),
            pltpu.VMEM((length, HEAD), F32),
            pltpu.VMEM((length, HEAD), F32),
        ],
        flops=20 * length * length * q_wide,
    )
    [terms] = call(
        functools.partial(weight_terms_kernel, splits, experts),
        [term_shape(lin_wide + q_wide + LANES)],
        [
            jnp.concatenate([spans, jnp.stack([me_ctx, me_fsdp // 2, place])]),
            *branches, attn_in, lin, mix, pack, more,
        ],
        scratch=[pltpu.VMEM((length, width), BF16)],
        flops=2 * length * width * (lin_wide + q_wide),
    )
    in_parts = call(
        functools.partial(input_terms_kernel, ctx),
        part_types,
        [spans, lin, pack],
        flops=2 * length * width * lin_wide,
    )
    if direct:
        other = swap(terms[1])
        other, in_parts = lax.optimization_barrier((other, in_parts))
        totals = {r: add(terms[0, r], other[r]) for r in range(chips)}
        totals, in_parts = lax.optimization_barrier((totals, in_parts))
        steps = ring_scatter(totals, "fsdp")
        arriving = steps.send(steps.send(next(steps)))
    else:
        terms = terms.reshape(ctx, fsdp, each, -1).swapaxes(0, 1)
        terms = lax.psum_scatter(terms, "fsdp", scatter_dimension=0, tiled=True)[0]
        terms = [
            lax.dynamic_index_in_dim(terms, me_ctx ^ j, 0, keepdims=False) for j in range(ctx)
        ]
    in_parts = [in_parts[0]] + [exchange(in_parts[j], "ctx", j) for j in range(1, ctx)]
    if chips == 4:
        moving = mix_steps.send(moving)
    hidden_out = (after + RESID_SCALE * total_of(moving)).astype(BF16)[None]
    grad_gate, grad_up, grad_down = (expert_sums[i].astype(F32) for i in range(3))
    grad_gate, grad_up, grad_down, in_parts = lax.optimization_barrier(
        (grad_gate, grad_up, grad_down, in_parts)
    )
    [grad_in] = call(
        norm_one_back_kernel,
        [shape((count, width), F32)],
        [no_scalars, x, gains, grad_after, *in_parts],
    )
    if direct:
        arriving, grad_in = lax.optimization_barrier((arriving, grad_in))
        terms = [add(*[v[j] for v in arriving]) for j in range(ctx)]
    terms = [terms[0]] + [exchange(terms[j], "ctx", j) for j in range(1, ctx)]
    widths = (q_wide, kv_wide, kv_wide, q_wide)
    grad_query, grad_key, grad_value, grad_out, notes = call(
        functools.partial(split_kernel, ctx, widths),
        [*[shape((each, ctx * w), F32) for w in widths], shape((each, LANES), F32)],
        [me_ctx[None], *terms],
    )
    return (
        hidden_out,
        grad_in[None],
        notes[:, experts],
        grad_query,
        grad_key,
        grad_value,
        grad_out,
        notes[:, experts + 1],
        notes[:, :experts],
        grad_gate,
        grad_up,
        grad_down,
    )


def solution(mesh):
    rows, both = P("fsdp", "ctx", None), ("ctx", "fsdp")
    split = P("fsdp", None)
    return jax.shard_map(
        body,
        mesh=mesh,
        in_specs=(
            rows, P(), rows, P("fsdp"), split, split, split, split, P("fsdp"), split,
            P("fsdp", None, None), P("fsdp", None, None), P("fsdp", None, None), rows,
        ),
        out_specs=(
            rows, rows, P(both), P(both, None), P(both, None), P(both, None), P(both, None),
            P(both), P(both, None), rows, rows, rows,
        ),
        check_vma=False,
    )
```

```python
import functools
import math

import jax
import jax.numpy as jnp
from jax import lax
from jax.experimental import pallas as pl
from jax.experimental.pallas import tpu as pltpu
from jax.sharding import PartitionSpec as P

HEAD = 64
HALF = HEAD // 2
NORM_EPS = 1e-06
ATTN_SCALE = 0.015625
RESID_SCALE = 0.22
ROPE_THETA = 10000.0
MASKED_SCORE = -1e30
LANES = 128
LAST = (((1,), (1,)), ((), ()))
FIRST = (((0,), (0,)), ((), ()))
F32 = jnp.float32
BF16 = jnp.bfloat16
VMEM = pl.BlockSpec(memory_space=pltpu.VMEM)
SMEM = pl.BlockSpec(memory_space=pltpu.SMEM)


def params(mib=60, **kw):
    return pltpu.CompilerParams(vmem_limit_bytes=mib * 2**20, **kw)


def call(kernel, outs, ins, scratch=(), flops=0, mib=24):
    size = lambda v: v.size * v.dtype.itemsize
    return pl.pallas_call(
        kernel,
        out_shape=outs,
        in_specs=[SMEM] + [VMEM] * (len(ins) - 1),
        out_specs=[VMEM] * len(outs),
        scratch_shapes=list(scratch),
        compiler_params=params(mib),
        cost_estimate=pl.CostEstimate(
            flops=flops, bytes_accessed=sum(map(size, list(ins) + list(outs))), transcendentals=0
        ),
    )(*ins)


def shape(dims, dtype):
    return jax.ShapeDtypeStruct(tuple(dims), dtype)


def dot(a, b, dims=(((1,), (0,)), ((), ()))):
    return lax.dot_general(a, b, dims, preferred_element_type=F32)


def scale_of(x):
    return lax.rsqrt(jnp.mean(x * x, axis=-1, keepdims=True) + NORM_EPS)


def span_rows(spans, index, size):
    return pl.ds(pl.multiple_of(spans[index] * size, size), size)


def rope(front, back, cosine, sine):
    return jnp.concatenate([front * cosine - back * sine, back * cosine + front * sine], axis=-1)


def unrope(front, back, cosine, sine):
    return jnp.concatenate([front * cosine + back * sine, back * cosine - front * sine], axis=-1)


def project_kernel(count, heads, kv_heads, experts, spans, *refs):
    pieces = refs[:count]
    pack, cosine, sine, attn_in, query, key, value, router, gains = refs[count:]
    lin_wide = (heads + 2 * kv_heads) * HEAD
    router[...] = pack[:, lin_wide + heads * HEAD :]
    turned = router[...].astype(F32).T
    gains[...] = turned[experts : experts + 2, :]
    gain = turned[experts : experts + 1, :]
    size = pieces[0].shape[0] // 2
    for j in range(count):
        x = pieces[j][...].astype(F32)
        rows_in = (x * scale_of(x) * gain).astype(BF16)
        lin = dot(rows_in, pack[:, :lin_wide])
        for h in range(2):
            at = span_rows(spans, 2 * j + h, size)
            cut = slice(h * size, (h + 1) * size)
            attn_in[at, :] = rows_in[cut]
            cos, sin = cosine[at, :], sine[at, :]
            for i in range(heads + kv_heads):
                lo = i * HEAD
                turned = rope(lin[cut, lo : lo + HALF], lin[cut, lo + HALF : lo + HEAD], cos, sin)
                if i < heads:
                    query[i, at, :] = (turned * ATTN_SCALE).astype(BF16)
                else:
                    key[i - heads, at, :] = turned.astype(BF16)
            for i in range(kv_heads):
                lo = (heads + kv_heads + i) * HEAD
                value[i, at, :] = lin[cut, lo : lo + HEAD].astype(BF16)


def diagonal(size, group):
    keys = lax.broadcasted_iota(jnp.int32, (size, group * size), 0)
    queries = lax.broadcasted_iota(jnp.int32, (size, group * size), 1) % size
    return keys <= queries


def scores_of(key_rows, query_rows, keep, size):
    raw = dot(key_rows, query_rows, LAST)
    seen = raw.shape[0] - size
    last = jnp.where(keep, raw[seen:], MASKED_SCORE)
    return last if seen == 0 else jnp.concatenate([raw[:seen], last], axis=0)


def attend_kernel(count, spans, query, key, value, pack, mix, lse, *refs):
    parts, rows_of = refs[:-1], refs[-1]
    kv_heads, length, _ = key.shape
    heads = query.shape[0]
    lo = (heads + 2 * kv_heads) * HEAD
    w_out = pack[:, lo : lo + mix.shape[1]]
    group = heads // kv_heads
    blocks = 2 * count
    size = length // blocks
    keep = diagonal(size, group)

    def one_group(g, _):
        for i in range(blocks):
            rows = slice(i * size, (i + 1) * size)
            seen = (i + 1) * size
            q = query[pl.ds(g * group, group), rows, :].reshape(group * size, HEAD)
            scores = scores_of(key[g, :seen, :], q, keep, size)
            top = jnp.max(scores, axis=0, keepdims=True)
            grown = jnp.exp(scores - top)
            total = jnp.sum(grown, axis=0, keepdims=True)
            mixed = dot(value[g, :seen, :], grown.astype(BF16), FIRST) / total
            lse[g, i, :, :] = top + jnp.log(total)
            for r in range(group):
                turned = mixed[:, r * size : (r + 1) * size].T
                rows_of[g * group + r, rows, :] = turned.astype(BF16)
        return 0

    lax.fori_loop(0, kv_heads, one_group, 0)
    for i in range(heads):
        mix[:, i * HEAD : (i + 1) * HEAD] = rows_of[i]
    for j in range(count):
        own = jnp.concatenate([mix[span_rows(spans, 2 * j + h, size), :] for h in range(2)], axis=0)
        parts[j][...] = dot(own, w_out, LAST).astype(parts[j].dtype)


def norm_two_kernel(_, x, gains, *refs):
    parts, (after, upper, lower) = refs[:-3], refs[-3:]
    branch = sum(p[...].astype(F32) for p in parts)
    rows = x[...].astype(F32) + RESID_SCALE * branch
    after[...] = rows
    ffn_in = (rows * scale_of(rows) * gains[1:2, :]).astype(BF16)
    half = upper.shape[0]
    upper[...], lower[...] = ffn_in[:half], ffn_in[half:]


def router_probs(rows, router, experts):
    logits = dot(rows, router)
    lane = lax.broadcasted_iota(jnp.int32, logits.shape, 1)
    logits = jnp.where(lane < experts, logits, MASKED_SCORE)
    grown = jnp.exp(logits - jnp.max(logits, axis=-1, keepdims=True))
    return grown / jnp.sum(grown, axis=-1, keepdims=True), lane


def experts_kernel(experts, cap, splits, chips, offset, where, *refs):
    row_refs = refs[: 2 * splits]
    grad_all, *weights, misc = refs[2 * splits : 2 * splits + 5]
    mix_refs, back_refs, saved = refs[2 * splits + 5 :][:2], refs[2 * splits + 7 :][:2], refs[2 * splits + 9 :][:5]
    keys, chances, grad_in, *held = refs[2 * splits + 14 :]
    kept, held, sems = held[3:8], held[:3], held[8]
    local, width, _ = weights[0].shape
    count = grad_in.shape[1]
    loads = [
        pltpu.make_async_copy(
            grad_all.at[
                pl.ds(pl.multiple_of(where[1 + b * chips + offset] * count, count), count), :
            ],
            grad_in.at[b],
            sems.at[b],
        )
        for b in range(2)
    ]
    pulls = [
        [
            pltpu.make_async_copy(weights[i].at[e], held[i].at[e], sems.at[2 + 3 * e + i])
            for i in range(3)
        ]
        for e in range(local)
    ]
    stores = [
        [
            pltpu.make_async_copy(
                kept[i].at[e], saved[i].at[e], sems.at[2 + 3 * local + 5 * e + i]
            )
            for i in range(5)
        ]
        for e in range(local)
    ]
    for copy in loads + sum(pulls, []):
        copy.start()
    rows = [
        jnp.concatenate([r[...] for r in row_refs[b * splits : (b + 1) * splits]], axis=0)
        for b in range(2)
    ]
    for b in range(2):
        chances[b] = router_probs(rows[b], misc[...], experts)[0].T
    for copy in loads:
        copy.wait()
    slot = lax.broadcasted_iota(jnp.int32, (cap, count), 0).astype(F32)
    lane = lax.broadcasted_iota(jnp.int32, (2 * cap, LANES), 1)
    names = [where[0] * local + e for e in range(local)]
    picks, share, mine, raw = [], [], [], []
    for b in range(2):
        keys[b] = grad_in[b, :, width:].astype(F32).T
        hits = [slot == keys[b, pl.ds(name, 1), :] for name in names]
        share.append(
            [
                jnp.sum(
                    jnp.where(hit, chances[b, pl.ds(name, 1), :], 0.0), axis=-1, keepdims=True
                )
                for hit, name in zip(hits, names)
            ]
        )
        picks.append(jnp.concatenate([hit.astype(BF16) for hit in hits], axis=0))
        mine.append(dot(picks[b], rows[b]).astype(BF16))
        raw.append(dot(picks[b], grad_in[b, :, :width]))
    both = lambda parts, e: jnp.concatenate([p[e * cap : (e + 1) * cap] for p in parts], axis=0)
    w_gate, w_up, w_down = held
    outs, backs, notes = [], [], []
    for e in range(local):
        weight = jnp.concatenate([share[b][e] for b in range(2)], axis=0)
        taken = both(mine, e)
        grad = both(raw, e) * RESID_SCALE
        grads = (grad * weight).astype(BF16)
        for copy in pulls[e]:
            copy.wait()
        gate, up = dot(taken, w_gate[e]), dot(taken, w_up[e])
        sigmoid = 1.0 / (1.0 + jnp.exp(-gate))
        silu = gate * sigmoid
        hidden = (silu * up).astype(BF16)
        out = dot(hidden, w_down[e], LAST).astype(BF16).astype(F32)
        grad_hidden = dot(grads, w_down[e])
        d_gate = (grad_hidden * up * sigmoid * (1.0 + gate * (1.0 - sigmoid))).astype(BF16)
        d_up = (grad_hidden * silu).astype(BF16)
        for i, term in enumerate((taken, grads, d_gate, d_up, hidden)):
            kept[i][e] = term
            stores[e][i].start()
        outs.append((out * weight).astype(BF16))
        backs.append((dot(d_gate, w_gate[e], LAST) + dot(d_up, w_up[e], LAST)).astype(BF16))
        note = jnp.sum(grad * out, axis=-1, keepdims=True)
        high = note.astype(BF16).astype(F32)
        notes.append(
            jnp.where(
                lane == names[e], high, jnp.where(lane == names[e] + LANES // 2, note - high, 0.0)
            ).astype(BF16)
        )
    for b in range(2):
        home = lambda parts: dot(
            picks[b],
            jnp.concatenate([p[b * cap : (b + 1) * cap] for p in parts], axis=0),
            FIRST,
        ).astype(BF16)
        mix_refs[b][...] = home(outs)
        back_refs[b][:, :width] = home(backs)
        back_refs[b][:, width:] = home(notes)
    for copy in sum(stores, []):
        copy.wait()


def expert_terms_kernel(chips, *refs):
    out, joined = refs[-2:]
    count, _, _, depth, _ = out.shape
    rows = joined.shape[1] // chips

    @pl.when(pl.program_id(1) == 0)
    def _():
        for r in range(chips):
            for i in range(3):
                joined[i, r * rows : (r + 1) * rows, :] = refs[5 * r + 2 + i][0]

    disp, slots = (
        jnp.concatenate([r[0] for r in refs[i : 5 * chips : 5]], axis=0) for i in range(2)
    )
    for i, left in enumerate((disp, disp, slots)):
        full = dot(left, joined[i], FIRST).astype(BF16)
        for c in range(count):
            out[c, i, 0] = full[c * depth : (c + 1) * depth]


def norm_two_back_kernel(
    experts, full, tops, _, cotangent, after, misc, gains, *refs
):
    *parts, grad_after, grad_branch, terms = refs
    width = after.shape[1]
    back = total_of([p[...] for p in parts[:full]])
    if tops:
        halves = parts[full : full + tops], parts[full + tops :]
        back = back + jnp.concatenate([total_of([p[...] for p in h]) for h in halves], axis=0)
    rows = after[...]
    scale = scale_of(rows)
    normed = rows * scale
    gain = gains[1:2, :]
    ffn_in = (normed * gain).astype(BF16)
    probs, lane = router_probs(ffn_in, misc[...], experts)
    notes = back[:, width:]
    notes = notes + pltpu.roll(notes, LANES // 2, 1)
    notes = jnp.where(lane < experts, notes, 0.0)
    logits = probs * (notes - jnp.sum(probs * notes, axis=-1, keepdims=True))
    high = logits.astype(BF16)
    low = (logits - high.astype(F32)).astype(BF16)
    grad_in = back[:, :width] + dot(high, misc[...], LAST) + dot(low, misc[...], LAST)
    grad_gain = jnp.sum(grad_in * normed, axis=0, keepdims=True)
    line = lax.broadcasted_iota(jnp.int32, (LANES, width), 0)
    terms[...] = (
        dot(ffn_in, high, FIRST)
        + dot(ffn_in, low, FIRST)
        + jnp.where(line == experts + 1, grad_gain, 0.0).T
    )
    scaled = grad_in * gain
    grad = cotangent[...].astype(F32) + scale * (
        scaled - normed * jnp.mean(scaled * normed, axis=-1, keepdims=True)
    )
    grad_after[...] = grad
    grad_branch[...] = (RESID_SCALE * grad).astype(BF16)


def pieces_of(splits, refs):
    pieces = []
    for n in splits:
        pieces.append(jnp.concatenate([r[...] for r in refs[:n]], axis=0))
        refs = refs[n:]
    return pieces, refs


def attend_back_kernel(splits, spans, *refs):
    count = len(splits)
    pieces, refs = pieces_of(splits, refs)
    pack, query, key, value, lse, cosine, sine, lin, grads, turned_of, key_sum, value_sum = refs
    kv_heads, length, _ = key.shape
    heads = query.shape[0]
    w_out = pack[:, lin.shape[1] : lin.shape[1] + heads * HEAD]
    group = heads // kv_heads
    blocks = 2 * count
    size = length // blocks
    keep = diagonal(size, group)
    for j in range(count):
        rows = dot(pieces[j], w_out).astype(BF16)
        for h in range(2):
            at = span_rows(spans, 2 * j + h, size)
            for i in range(heads):
                grads[i, at, :] = rows[h * size : (h + 1) * size, i * HEAD : (i + 1) * HEAD]

    def one_group(g, _):
        key_sum[...] = jnp.zeros_like(key_sum)
        value_sum[...] = jnp.zeros_like(value_sum)
        for i in range(blocks):
            rows = slice(i * size, (i + 1) * size)
            seen = (i + 1) * size
            q = query[pl.ds(g * group, group), rows, :].reshape(group * size, HEAD)
            grad = grads[pl.ds(g * group, group), rows, :].reshape(group * size, HEAD)
            probs = jnp.exp(scores_of(key[g, :seen, :], q, keep, size) - lse[g, i])
            grad_probs = dot(value[g, :seen, :], grad, LAST)
            delta = jnp.sum(probs * grad_probs, axis=0, keepdims=True)
            raw = (probs * (grad_probs - delta)).astype(BF16)
            value_sum[:seen, :] += dot(probs.astype(BF16), grad)
            key_sum[:seen, :] += dot(raw, q)
            grad_query = dot(key[g, :seen, :], raw, FIRST) * ATTN_SCALE
            for r in range(group):
                turned = grad_query[:, r * size : (r + 1) * size].T
                turned_of[g * group + r, rows, :] = unrope(
                    turned[:, :HALF], turned[:, HALF:], cosine[rows, :], sine[rows, :]
                ).astype(BF16)
        turned_of[heads + g] = unrope(
            key_sum[:, :HALF], key_sum[:, HALF:], cosine[...], sine[...]
        ).astype(BF16)
        turned_of[heads + kv_heads + g] = value_sum[...].astype(BF16)
        return 0

    lax.fori_loop(0, kv_heads, one_group, 0)
    for i in range(heads + 2 * kv_heads):
        lin[:, i * HEAD : (i + 1) * HEAD] = turned_of[i]


def input_terms_kernel(count, spans, lin, pack, *parts):
    weight = pack[:, : lin.shape[1]]
    size = lin.shape[0] // (2 * count)
    for j in range(count):
        own = jnp.concatenate([lin[span_rows(spans, 2 * j + h, size), :] for h in range(2)], axis=0)
        parts[j][...] = dot(own, weight, LAST).astype(parts[j].dtype)


def noted(notes):
    lane = lax.broadcasted_iota(jnp.int32, notes.shape, 1)
    high = notes.astype(BF16).astype(F32)
    return high + pltpu.roll(jnp.where(lane < LANES // 2, notes - high, 0.0), LANES // 2, 1)


def store_terms(where, out, c, full):
    if len(out.shape) == 2:
        out[c * full.shape[0] : (c + 1) * full.shape[0], :] = full
    else:
        chips, each = out.shape[1], out.shape[3]
        for f in range(2 * chips):
            offset = (f // 2 - where[1] + chips) % chips
            out[(f + where[2]) % 2, offset, c ^ where[0]] = full[f * each : (f + 1) * each]


def weight_terms_kernel(splits, experts, spans, *refs):
    count = len(splits)
    where = [spans[2 * count + i] for i in range(3)]
    pieces, refs = pieces_of(splits, refs)
    attn_in, lin, mix, pack, more, out, branch = refs
    length, width = attn_in.shape
    lin_wide = lin.shape[1]
    size = length // (2 * count)
    for j in range(count):
        for h in range(2):
            branch[span_rows(spans, 2 * j + h, size), :] = pieces[j][h * size : (h + 1) * size, :]
    step = width // count
    lane = lax.broadcasted_iota(jnp.int32, (step, LANES), 1)
    for c in range(count):
        cut = slice(c * step, (c + 1) * step)
        attn = dot(attn_in[:, cut], lin[...], FIRST)
        outs = dot(branch[:, cut], mix[...], FIRST)
        gain = pack[cut, pack.shape[1] - LANES :].astype(F32)[:, experts : experts + 1]
        weight = pack[cut, :lin_wide].astype(F32)
        grad_gain = jnp.sum(weight * attn, axis=-1, keepdims=True) / gain
        notes = noted(more[cut, :] + jnp.where(lane == experts, grad_gain, 0.0))
        store_terms(where, out, c, jnp.concatenate([attn, outs, notes], axis=1).astype(BF16))


def norm_one_back_kernel(_, x, gains, grad_after, *refs):
    parts, grad_in = refs[:-1], refs[-1]
    grad = sum(p[...].astype(F32) for p in parts) * gains[0:1, :]
    rows = x[...].astype(F32)
    scale = scale_of(rows)
    normed = rows * scale
    grad_in[...] = grad_after[...] + scale * (
        grad - normed * jnp.mean(grad * normed, axis=-1, keepdims=True)
    )


def split_kernel(count, widths, me, *refs):
    terms, outs = refs[:count], refs[count:]

    def place(own):
        for j in range(count):
            lo = 0
            for wide, out in zip(widths, outs):
                s = own ^ j
                out[:, s * wide : (s + 1) * wide] = terms[j][:, lo : lo + wide].astype(F32)
                lo += wide

    for own in range(count):
        pl.when(me[0] == own)(functools.partial(place, own))
    lo = sum(widths)
    total = total_of([t[:, lo:] for t in terms])
    outs[-1][...] = total + pltpu.roll(total, LANES // 2, 1)


def exchange(value, axis, offset):
    n = lax.axis_size(axis)
    return lax.ppermute(value, axis, [(i, i ^ offset) for i in range(n)])


def ring_pairs(n, hop):
    chips = n // 2
    return [(z * 2 + c, ((z + hop) % chips) * 2 + c) for z in range(chips) for c in range(2)]


def swap_pairs(n):
    return [(i, i ^ 1) for i in range(n)]


def ring_scatter(total, axis):
    n = lax.axis_size(axis)
    chips = n // 2
    move = lambda v, hop: lax.ppermute(v, axis, ring_pairs(n, hop))
    half = total[0].shape[0] // 2
    right = left = None
    if chips % 2 == 0:
        far = total[chips // 2]
        first, second = yield move(far[:half], 1), move(far[half:], -1)
    for s in range((chips - 1) // 2, 0, -1):
        up, down = total[s], total[chips - s]
        if right is not None:
            up, down = add(up, right), add(down, left)
        elif chips % 2 == 0:
            up = jnp.concatenate([add(up[:half], first), up[half:]], 0)
            down = jnp.concatenate([down[:half], add(down[half:], second)], 0)
        right, left = yield move(up, 1), move(down, -1)
    yield total[0], right, left


def add(*values):
    return sum(v.astype(F32) for v in values).astype(BF16)


def total_of(values):
    return sum(v.astype(F32) for v in values)


def slot_keys(route_rows, experts):
    hits = (route_rows[:, :, None] == jnp.arange(experts, dtype=jnp.int32)).any(axis=1)
    rows = jnp.arange(route_rows.shape[0], dtype=jnp.int32)
    earlier = (rows[None, :] < rows[:, None]).astype(BF16)
    ranks = jnp.dot(earlier, hits.astype(BF16), preferred_element_type=F32)
    keys = jnp.where(hits, ranks, -1.0).astype(BF16)
    return jnp.pad(keys, ((0, 0), (0, LANES - experts)), constant_values=-1)


def body(
    hidden_in, span_order, routes, attn_gain, query_weight, key_weight, value_weight, out_weight,
    ffn_gain, router_weight, gate_weight, up_weight, down_weight, cotangent
):
    ctx, fsdp = lax.axis_size("ctx"), lax.axis_size("fsdp")
    me_ctx, me_fsdp = lax.axis_index("ctx"), lax.axis_index("fsdp")
    x = hidden_in[0]
    count, width = x.shape
    length = ctx * count
    heads = query_weight.shape[1] // HEAD // ctx
    kv_heads = key_weight.shape[1] // HEAD // ctx
    experts = router_weight.shape[1]
    local, _, units = gate_weight.shape
    cap = count * routes.shape[2] * 5 // (4 * experts)
    q_wide, kv_wide = heads * HEAD, kv_heads * HEAD
    lin_wide = q_wide + 2 * kv_wide
    chips = fsdp // 2
    no_scalars = jnp.zeros((1,), jnp.int32)

    own = lambda w, wide: lax.dynamic_slice_in_dim(w, me_ctx * wide, wide, 1)
    pack = jnp.concatenate(
        [
            own(query_weight, q_wide),
            own(key_weight, kv_wide),
            own(value_weight, kv_wide),
            own(out_weight, q_wide),
            router_weight,
            attn_gain[:, None],
            ffn_gain[:, None],
            jnp.zeros((attn_gain.shape[0], LANES - experts - 2), BF16),
        ],
        axis=1,
    )
    pack = lax.all_gather(pack, "fsdp", axis=0, tiled=True)
    pieces = [x] + [exchange(x, "ctx", j) for j in range(1, ctx)]
    owners = jnp.stack([me_ctx ^ j for j in range(ctx)])
    spans = span_order.reshape(ctx, 2)[owners].reshape(-1)
    keys = slot_keys(routes[0], experts)
    grad_pack = lax.all_gather(
        jnp.concatenate([cotangent[0], keys], axis=1), "fsdp", axis=0, tiled=True
    )
    frequencies = ROPE_THETA ** (-2.0 * jnp.arange(HALF, dtype=F32) / HEAD)
    angles = jnp.arange(length, dtype=F32)[:, None] * frequencies[None, :]
    cosine, sine = jnp.cos(angles), jnp.sin(angles)

    attn_in, query, key, value, misc, gains = call(
        functools.partial(project_kernel, ctx, heads, kv_heads, experts),
        [
            shape((length, width), BF16),
            shape((heads, length, HEAD), BF16),
            shape((kv_heads, length, HEAD), BF16),
            shape((kv_heads, length, HEAD), BF16),
            shape((width, LANES), BF16),
            shape((2, width), F32),
        ],
        [spans, *pieces, pack, cosine, sine],
        flops=2 * length * width * lin_wide,
        mib=60,
    )
    part_types = [shape((count, width), F32 if j == 0 else BF16) for j in range(ctx)]
    mix, lse, *parts = call(
        functools.partial(attend_kernel, ctx),
        [
            shape((length, q_wide), BF16),
            shape((kv_heads, 2 * ctx, 1, heads // kv_heads * length // (2 * ctx)), F32),
            *part_types,
        ],
        [spans, query, key, value, pack],
        scratch=[pltpu.VMEM((heads, length, HEAD), BF16)],
        flops=8 * length * length * q_wide,
        mib=60,
    )
    parts = [parts[0]] + [exchange(parts[j], "ctx", j) for j in range(1, ctx)]
    half = count // 2
    after, upper, lower = call(
        norm_two_kernel,
        [shape((count, width), F32), *[shape((half, width), BF16)] * 2],
        [no_scalars, x, gains, *parts],
    )
    place = me_fsdp % 2
    wides = (width, width, units, units, units)
    anywhere = pl.BlockSpec(memory_space=pltpu.HBM)
    offsets = (me_fsdp // 2 + jnp.arange(chips, dtype=jnp.int32)) % chips * 2
    places = jnp.concatenate([me_fsdp[None], offsets + place, offsets + 1 - place])

    move = lambda v, hop: lax.ppermute(v, "fsdp", ring_pairs(fsdp, hop))
    swap = lambda v: lax.ppermute(v, "fsdp", swap_pairs(fsdp))

    def run_experts(offset, same, other):
        rows = [*same, *other]
        outs = pl.pallas_call(
            functools.partial(experts_kernel, experts, cap, len(rows) // 2, chips, offset),
            out_shape=[
                *[pltpu.HBM((count, width), BF16)] * 2,
                *[shape((count, width + LANES), BF16)] * 2,
                *[pltpu.HBM((local, 2 * cap, w), BF16) for w in wides],
            ],
            in_specs=[SMEM, *[VMEM] * len(rows), *[anywhere] * 4, VMEM],
            out_specs=[VMEM] * 4 + [anywhere] * 5,
            scratch_shapes=[
                pltpu.VMEM((2, LANES, count), F32),
                pltpu.VMEM((2, LANES, count), F32),
                pltpu.VMEM((2, count, width + LANES), BF16),
                *[pltpu.VMEM((local, width, units), BF16)] * 3,
                *[pltpu.VMEM((local, 2 * cap, w), BF16) for w in wides],
                pltpu.SemaphoreType.DMA((2 + 8 * local,)),
            ],
            compiler_params=params(44),
            cost_estimate=pl.CostEstimate(
                flops=32 * local * cap * width * units,
                bytes_accessed=20 * 2**20,
                transcendentals=0,
            ),
        )(
            places,
            *rows, grad_pack, gate_weight, up_weight, down_weight, misc,
        )
        return outs[0:2], outs[2:4], outs[4:]

    depth = width // ctx
    slots = fsdp * cap
    step = math.lcm(depth, LANES)
    tall = pl.BlockSpec((1, 2 * cap, step), lambda e, c: (e, 0, c))
    thin = pl.BlockSpec((1, 2 * cap, units), lambda e, c: (e, 0, 0))

    def sum_experts(saved):
        return pl.pallas_call(
            functools.partial(expert_terms_kernel, chips),
            out_shape=shape((ctx, 3, local, depth, units), BF16),
            grid=(local, width // step),
            in_specs=[tall, tall, thin, thin, thin] * chips,
            out_specs=pl.BlockSpec((step // depth, 3, 1, depth, units), lambda e, c: (c, 0, e, 0, 0)),
            scratch_shapes=[pltpu.VMEM((3, slots, units), BF16)],
            compiler_params=params(60),
            cost_estimate=pl.CostEstimate(
                flops=6 * local * slots * width * units, bytes_accessed=40 * 2**20, transcendentals=0
            ),
        )(*saved)

    swaps = lambda *values: [swap(v) for v in values]
    cut_add = lambda cut, *values: add(*[v[cut] for v in values])
    top, bottom = slice(0, half), slice(half, count)
    ran = {}
    if chips == 4:
        far_top, far_bottom = move(upper, 1), move(lower, -1)
        from_left, from_right, upper, lower = lax.optimization_barrier(
            (far_top, far_bottom, upper, lower)
        )
        far_top, far_bottom = move(from_left, 1), move(from_right, -1)
        ran[0] = run_experts(0, [upper, lower], swaps(upper, lower))
        far_top, far_bottom, ran, upper, lower = lax.optimization_barrier(
            (far_top, far_bottom, ran, upper, lower)
        )
        left_rows = [from_left, move(lower, 1)]
        right_rows = [move(upper, -1), from_right]
        ran[2] = run_experts(2, [far_top, far_bottom], swaps(far_top, far_bottom))
        left_rows, right_rows, ran = lax.optimization_barrier((left_rows, right_rows, ran))
        same, other = ran[2][1]
        other = swap(other)
        sums = cut_add(top, same, other), cut_add(bottom, same, other)
        left_rows, right_rows, sums = lax.optimization_barrier((left_rows, right_rows, sums))
        far_top, far_bottom = move(sums[0], 1), move(sums[1], -1)
        ran[3] = run_experts(3, left_rows, swaps(*left_rows))
        far_top, far_bottom, ran = lax.optimization_barrier((far_top, far_bottom, ran))
        same, other = ran[3][1]
        other = swap(other)
        sums = cut_add(top, same, other), add(same[bottom], other[bottom], far_bottom)
        right_rows, sums = lax.optimization_barrier((right_rows, sums))
        down_top, down_bottom = move(sums[0], -1), move(sums[1], -1)
        ran[1] = run_experts(1, right_rows, swaps(*right_rows))
        down_top, down_bottom, ran = lax.optimization_barrier((down_top, down_bottom, ran))
        same, other = ran[1][1]
        other = swap(other)
        saved = [v for r in range(chips) for v in ran[r][2]]
        expert_terms = sum_experts(saved)
        same, other, expert_terms = lax.optimization_barrier((same, other, expert_terms))
        sums = add(same[top], other[top], far_top), cut_add(bottom, same, other)
        backs = [
            [ran[0][1][0], swap(ran[0][1][1])],
            [move(sums[0], 1), down_top],
            [move(sums[1], 1), down_bottom],
        ]
    else:
        rows_all = lax.all_gather(jnp.concatenate([upper, lower], axis=0), "fsdp", axis=0, tiled=True)
        back = jnp.zeros((fsdp * count, width + LANES), BF16)
        mix_all = jnp.zeros((fsdp * count, width), BF16)
        for r in range(chips):
            chip = (me_fsdp // 2 + r) % chips * 2
            at = [(chip + place) * count, (chip + 1 - place) * count]
            same, other = (lax.dynamic_slice_in_dim(rows_all, v, count, 0) for v in at)
            ran[r] = run_experts(r, [same], [other])
            for b in range(2):
                mix_all = lax.dynamic_update_slice_in_dim(mix_all, ran[r][0][b], at[b], 0)
                back = lax.dynamic_update_slice_in_dim(back, ran[r][1][b], at[b], 0)
        backs = [[lax.psum_scatter(back, "fsdp", scatter_dimension=0, tiled=True)], [], []]
        expert_terms = sum_experts([v for r in range(chips) for v in ran[r][2]])

    expert_sums = lax.psum_scatter(
        expert_terms.reshape(-1, units), "ctx", scatter_dimension=0, tiled=True
    ).reshape(3, local, depth, units)
    if chips == 4:
        mixes = {r: add(ran[r][0][0], swap(ran[r][0][1])) for r in range(chips)}
        mixes, backs = lax.optimization_barrier((mixes, backs))
        mix_steps = ring_scatter(mixes, "fsdp")
        moving = mix_steps.send(next(mix_steps))
    else:
        moving = [lax.psum_scatter(mix_all, "fsdp", scatter_dimension=0, tiled=True)]
    grad_after, grad_branch, more = call(
        functools.partial(norm_two_back_kernel, experts, len(backs[0]), len(backs[1])),
        [shape((count, width), F32), shape((count, width), BF16), shape((width, LANES), F32)],
        [no_scalars, cotangent[0], after, misc, gains, *backs[0], *backs[1], *backs[2]],
    )
    if ctx == 4:
        beside = [exchange(grad_branch, "ctx", j) for j in (1, 2)]
        branches = [[grad_branch], [beside[0]], [beside[1]]]
        branches.append(
            [exchange(beside[0][:half], "ctx", 2), exchange(beside[1][half:], "ctx", 1)]
        )
    else:
        branches = [[grad_branch]] + [[exchange(grad_branch, "ctx", j)] for j in range(1, ctx)]
    splits = [len(b) for b in branches]
    branches = sum(branches, [])
    branches, moving = lax.optimization_barrier((branches, moving))
    each = width // (ctx * fsdp)
    direct = each % 16 == 0 and chips == 4
    term_shape = lambda wide: shape(
        (2, chips, ctx, each, wide) if direct else (width, wide), BF16
    )

    [lin] = call(
        functools.partial(attend_back_kernel, splits),
        [shape((length, lin_wide), BF16)],
        [spans, *branches, pack, query, key, value, lse, cosine, sine],
        scratch=[
            pltpu.VMEM((heads, length, HEAD), BF16),
            pltpu.VMEM((heads + 2 * kv_heads, length, HEAD), BF16),
            pltpu.VMEM((length, HEAD), F32),
            pltpu.VMEM((length, HEAD), F32),
        ],
        flops=20 * length * length * q_wide,
    )
    [terms] = call(
        functools.partial(weight_terms_kernel, splits, experts),
        [term_shape(lin_wide + q_wide + LANES)],
        [
            jnp.concatenate([spans, jnp.stack([me_ctx, me_fsdp // 2, place])]),
            *branches, attn_in, lin, mix, pack, more,
        ],
        scratch=[pltpu.VMEM((length, width), BF16)],
        flops=2 * length * width * (lin_wide + q_wide),
    )
    in_parts = call(
        functools.partial(input_terms_kernel, ctx),
        part_types,
        [spans, lin, pack],
        flops=2 * length * width * lin_wide,
    )
    if direct:
        other = swap(terms[1])
        other, in_parts = lax.optimization_barrier((other, in_parts))
        totals = {r: add(terms[0, r], other[r]) for r in range(chips)}
        totals, in_parts = lax.optimization_barrier((totals, in_parts))
        steps = ring_scatter(totals, "fsdp")
        arriving = steps.send(steps.send(next(steps)))
    else:
        terms = terms.reshape(ctx, fsdp, each, -1).swapaxes(0, 1)
        terms = lax.psum_scatter(terms, "fsdp", scatter_dimension=0, tiled=True)[0]
        terms = [
            lax.dynamic_index_in_dim(terms, me_ctx ^ j, 0, keepdims=False) for j in range(ctx)
        ]
    in_parts = [in_parts[0]] + [exchange(in_parts[j], "ctx", j) for j in range(1, ctx)]
    if chips == 4:
        moving = mix_steps.send(moving)
    hidden_out = (after + RESID_SCALE * total_of(moving)).astype(BF16)[None]
    grad_gate, grad_up, grad_down = (expert_sums[i].astype(F32) for i in range(3))
    grad_gate, grad_up, grad_down, in_parts = lax.optimization_barrier(
        (grad_gate, grad_up, grad_down, in_parts)
    )
    [grad_in] = call(
        norm_one_back_kernel,
        [shape((count, width), F32)],
        [no_scalars, x, gains, grad_after, *in_parts],
    )
    if direct:
        arriving, grad_in = lax.optimization_barrier((arriving, grad_in))
        terms = [add(*[v[j] for v in arriving]) for j in range(ctx)]
    terms = [terms[0]] + [exchange(terms[j], "ctx", j) for j in range(1, ctx)]
    widths = (q_wide, kv_wide, kv_wide, q_wide)
    grad_query, grad_key, grad_value, grad_out, notes = call(
        functools.partial(split_kernel, ctx, widths),
        [*[shape((each, ctx * w), F32) for w in widths], shape((each, LANES), F32)],
        [me_ctx[None], *terms],
    )
    return (
        hidden_out,
        grad_in[None],
        notes[:, experts],
        grad_query,
        grad_key,
        grad_value,
        grad_out,
        notes[:, experts + 1],
        notes[:, :experts],
        grad_gate,
        grad_up,
        grad_down,
    )


def solution(mesh):
    rows, both = P("fsdp", "ctx", None), ("ctx", "fsdp")
    split = P("fsdp", None)
    return jax.shard_map(
        body,
        mesh=mesh,
        in_specs=(
            rows, P(), rows, P("fsdp"), split, split, split, split, P("fsdp"), split,
            P("fsdp", None, None), P("fsdp", None, None), P("fsdp", None, None), rows,
        ),
        out_specs=(
            rows, rows, P(both), P(both, None), P(both, None), P(both, None), P(both, None),
            P(both), P(both, None), rows, rows, rows,
        ),
        check_vma=False,
    )
```
